256 devices in a mesh: blk: 32 (over y, x, core), mpo: 8 (over z).
Axes of the slice: x: 4, y: 4, z: 8, core: 2. Of those that a mesh axis runs over, the one named last changes fastest.
Arguments:
- wavefunction: bfloat16 [8192, 8192], P('blk'), may hold values from -6 to 6
- left_env: bfloat16 [16, 8192, 256], P('mpo', 'blk'), may hold values from -0.375 to 0.375
- right_env: bfloat16 [16, 8192, 256], P('mpo', 'blk'), may hold values from -0.09375 to 0.09375
- left_sizes: int32 [32], replicated, may hold values from 64 to 256, as said below
- right_sizes: int32 [32], replicated, may hold values from 64 to 256, as said below
Outputs:
- applied: bfloat16 [32, 256, 8192], P(None, 'mpo', 'blk')
The draws below stay inside these ranges and needn't reach their ends.
Inputs may be any that keep to these rules, and one draw needn't show every extreme that they name: `left_sizes`: one sector has exactly 256 and one exactly 64. `right_sizes`: one sector has exactly 256 and one exactly 64.
All inputs are finite; a program needn't handle non-finite values.
Results may differ from the reference program's by a relative error of at most 0.0049.
Values may be sent and summed in bfloat16 or wider, within the bound.
No kernel may reach another device: no remote copies, remote signals or barrier semaphores. Data moves between devices by JAX's collectives and lax.ppermute only.
A program may use at most 192 MiB of HBM per device.

```python
import jax
import jax.numpy as jnp
from jax import lax

LMAX = 256
RMAX = 256
W = 16
SECTORS = 32


def sector_dims(key, largest):
    key_dims, key_top, key_low = jax.random.split(key, 3)
    dims = jax.random.randint(key_dims, (SECTORS,), largest // 4, largest + 1)
    largest_at = jax.random.randint(key_top, (), 0, SECTORS)
    smallest_at = (largest_at + 1 + jax.random.randint(key_low, (), 0, SECTORS - 1)) % SECTORS
    dims = dims.at[largest_at].set(largest)
    dims = dims.at[smallest_at].set(largest // 4)
    return dims.astype(jnp.int32)


def draw_left_sizes(key, part):
    key = jax.random.fold_in(key, 11)
    return sector_dims(key, LMAX)


def draw_right_sizes(key, part):
    key = jax.random.fold_in(key, 23)
    return sector_dims(key, RMAX)


def block_scale(key, shape, pieces, low, top_value):
    factor_of, own = 1.0, jax.random.fold_in(key, 6)
    for axis_at, parts in pieces:
        steps = jnp.exp(jax.random.uniform(jax.random.fold_in(own, axis_at), (parts,), jnp.float32, low / len(pieces), top_value / len(pieces)))
        factor_of = factor_of * jnp.repeat(steps, shape[axis_at] // parts).reshape([-1 if axis == axis_at else 1 for axis in range(len(shape))])
    return factor_of


def gaussian(key, shape, scale, reach, shards=(), held_as=jnp.bfloat16):
    drawn = scale * jax.random.normal(key, shape, jnp.float32)
    if shards:
        drawn = drawn * block_scale(key, shape, shards, -0.22, 0.18)
    return jnp.clip(drawn, -reach, reach).astype(held_as)


def setup_inputs(seed: int = 0) -> dict:
    streams_of = jax.random.split(jax.random.key(seed), 6)
    return {
        "wavefunction": gaussian(streams_of[0], (SECTORS * LMAX, SECTORS * RMAX), 1.0, 6.0, ((0, 32),)),
        "left_env": gaussian(streams_of[1], (W, SECTORS * LMAX, LMAX), LMAX ** -0.5, 0.375, ((0, 8), (1, 32))),
        "right_env": gaussian(streams_of[2], (W, SECTORS * RMAX, RMAX), (RMAX * W) ** -0.5, 0.09375, ((0, 8), (1, 32))),
        "left_sizes": draw_left_sizes(jax.random.fold_in(streams_of[5], 71), 0),
        "right_sizes": draw_right_sizes(jax.random.fold_in(streams_of[5], 71), 0),
    }


def reference(wavefunction, left_env, right_env, left_sizes, right_sizes):
    row_mask = (jnp.arange(LMAX, dtype=jnp.int32)[None, :] < left_sizes[:, None]).astype(jnp.float32)
    col_mask = (jnp.arange(RMAX, dtype=jnp.int32)[None, :] < right_sizes[:, None]).astype(jnp.float32)
    full_mask = row_mask[:, :, None, None] * col_mask[None, None, :, :]
    blocks = wavefunction.reshape(SECTORS, LMAX, SECTORS, RMAX).astype(jnp.float32)
    masked = (blocks * full_mask).astype(jnp.bfloat16).astype(jnp.float32)
    left_blocks = left_env.reshape(W, SECTORS, LMAX, LMAX)
    right_blocks = right_env.reshape(W, SECTORS, RMAX, RMAX)

    def apply_index(running, pair):
        left_block, right_block = pair
        contracted = jnp.einsum("aij,ajbr->aibr", left_block.astype(jnp.float32), masked,
                                precision=lax.Precision.HIGHEST).astype(jnp.bfloat16)
        projected = jnp.einsum("aibr,brc->aibc", contracted.astype(jnp.float32), right_block.astype(jnp.float32),
                               precision=lax.Precision.HIGHEST)
        return running + projected, None

    start = jnp.zeros((SECTORS, LMAX, SECTORS, RMAX), jnp.float32)
    summed, unused = lax.scan(apply_index, start, (left_blocks, right_blocks))
    summed = summed * full_mask
    return summed.reshape(SECTORS, LMAX, SECTORS * RMAX).astype(jnp.bfloat16)
```

```python
import jax
import jax.numpy as jnp
from jax import lax
from jax.sharding import PartitionSpec as P


def ring_gather(block, axis, n):
    up = [(i, (i + 1) % n) for i in range(n)]
    down = [(i, (i + n - 1) % n) for i in range(n)]
    pieces = {0: block}
    from_below = from_above = block
    for hop in range(1, n // 2 + 1):
        from_below = lax.ppermute(from_below, axis, up)
        pieces[-hop] = from_below
        if 2 * hop < n:
            from_above = lax.ppermute(from_above, axis, down)
            pieces[hop] = from_above
    hops = sorted(pieces)
    stacked = jnp.stack([pieces[hop] for hop in hops])
    owners = jnp.arange(n, dtype=jnp.int32)
    places = jnp.remainder(owners - lax.axis_index(axis) - hops[0], n)
    return jnp.take(stacked, places, axis=0)


def local(wavefunction, left_env, right_env, left_sizes, right_sizes):
    sector = lax.axis_index("blk")
    rank = lax.axis_index("mpo")
    ranks = lax.axis_size("mpo")
    own_w, left_dim, _ = left_env.shape
    right_dim = right_env.shape[2]
    sectors = wavefunction.shape[1] // right_dim
    rows = left_dim // ranks
    own_left = left_sizes[sector]
    own_right = right_sizes[sector]

    split = left_env.reshape(own_w, ranks, rows, left_dim).transpose(1, 0, 2, 3)
    mine = lax.all_to_all(split, "mpo", 0, 0)
    lefts = lax.all_gather(mine, "blk")

    row_own = jnp.arange(left_dim, dtype=jnp.int32) < own_left
    masked = jnp.where(row_own[:, None], wavefunction, jnp.zeros_like(wavefunction))
    by_right = masked.reshape(left_dim, sectors, right_dim).transpose(1, 0, 2)
    psi = lax.all_to_all(by_right, "blk", 0, 0)
    col_own = jnp.arange(right_dim, dtype=jnp.int32) < own_right
    psi = jnp.where(col_own, psi, jnp.zeros_like(psi))

    rights = ring_gather(right_env, "mpo", ranks)

    contracted = jnp.einsum(
        "apwij,ajr->apwir", lefts, psi, preferred_element_type=jnp.float32
    ).astype(jnp.bfloat16)
    summed = jnp.einsum(
        "apwir,pwrc->aic", contracted, rights, preferred_element_type=jnp.float32
    )
    row_ids = rank * rows + jnp.arange(rows, dtype=jnp.int32)
    keep = (row_ids[None, :] < left_sizes[:, None])[:, :, None] & col_own
    return jnp.where(keep, summed, 0.0).astype(jnp.bfloat16)


def solution(mesh):
    placed = (P("blk", None), P("mpo", "blk", None), P("mpo", "blk", None), P(), P())
    return jax.shard_map(
        local, mesh=mesh, in_specs=placed, out_specs=P(None, "mpo", "blk"), check_vma=False
    )
```

```python
import jax
import jax.numpy as jnp
from jax import lax
from jax.experimental import pallas as pl
from jax.experimental.pallas import tpu as pltpu
from jax.sharding import PartitionSpec as P

MIB = 1024 * 1024


def ring_gather(block, axis, n):
    up = [(i, (i + 1) % n) for i in range(n)]
    down = [(i, (i + n - 1) % n) for i in range(n)]
    pieces = {0: block}
    from_below = from_above = block
    for hop in range(1, n // 2 + 1):
        from_below = lax.ppermute(from_below, axis, up)
        pieces[-hop] = from_below
        if 2 * hop < n:
            from_above = lax.ppermute(from_above, axis, down)
            pieces[hop] = from_above
    hops = sorted(pieces)
    stacked = jnp.stack([pieces[hop] for hop in hops])
    owners = jnp.arange(n, dtype=jnp.int32)
    places = jnp.remainder(owners - lax.axis_index(axis) - hops[0], n)
    return jnp.take(stacked, places, axis=0)


def split_kernel(scalars, psi_ref, keep_ref, send_ref):
    step = pl.program_id(0)
    core, own_left = scalars[0], scalars[1]
    left_dim, both = psi_ref.shape
    right_dim = both // 2
    row = lax.broadcasted_iota(jnp.int32, (left_dim, right_dim), 0)
    col = lax.broadcasted_iota(jnp.int32, (left_dim, right_dim), 1)

    def masked(at):
        size = scalars[2 + 2 * step + at]
        block = psi_ref[:, at * right_dim : (at + 1) * right_dim]
        inside = jnp.logical_and(row < own_left, col < size)
        return jnp.where(inside, block.astype(jnp.float32), 0.0).astype(block.dtype)

    first, second = masked(0), masked(1)

    @pl.when(core == 0)
    def _():
        keep_ref[0], send_ref[0] = first, second

    @pl.when(core != 0)
    def _():
        keep_ref[0], send_ref[0] = second, first


def split_psi(wavefunction, scalars, sectors):
    left_dim, columns = wavefunction.shape
    right_dim = columns // sectors
    block = pl.BlockSpec((1, left_dim, right_dim), lambda i, s: (i, 0, 0))
    shape = jax.ShapeDtypeStruct((sectors // 2, left_dim, right_dim), wavefunction.dtype)
    return pl.pallas_call(
        split_kernel,
        out_shape=(shape, shape),
        grid_spec=pltpu.PrefetchScalarGridSpec(
            num_scalar_prefetch=1,
            grid=(sectors // 2,),
            in_specs=[pl.BlockSpec((left_dim, 2 * right_dim), lambda i, s: (0, i))],
            out_specs=(block, block),
        ),
        compiler_params=pltpu.CompilerParams(vmem_limit_bytes=32 * MIB),
    )(scalars, wavefunction)


def apply_kernel(scalars, left_ref, psi_ref, right_ref, keep_ref, send_ref, middle):
    step = pl.program_id(0)
    parity, first_row, own_right = scalars[0], scalars[1], scalars[2]
    chips, halves, pairs, rows, left_dim = left_ref.shape
    right_dim = psi_ref.shape[2]
    indices = halves * pairs
    for a in range(chips):
        block = left_ref[a].reshape(indices * rows, left_dim)
        out = jnp.dot(block, psi_ref[a], preferred_element_type=jnp.float32)
        middle[:, a] = out.astype(middle.dtype).reshape(indices, rows, right_dim)
    total = jnp.zeros((chips * rows, right_dim), jnp.float32)
    for half in range(halves):
        for pair in range(pairs):
            block = middle[half * pairs + pair].reshape(chips * rows, right_dim)
            total += jnp.dot(block, right_ref[pair, half], preferred_element_type=jnp.float32)
    row = first_row + lax.broadcasted_iota(jnp.int32, (rows, right_dim), 0)
    col = lax.broadcasted_iota(jnp.int32, (rows, right_dim), 1)
    for a in range(chips):
        size = scalars[3 + step * chips + a]
        inside = jnp.logical_and(row < size, col < own_right)
        block = jnp.where(inside, total[a * rows : (a + 1) * rows], 0.0)
        low, high = block[: rows // 2], block[rows // 2 :]
        keep_ref[a] = jnp.where(parity == 0, low, high).astype(keep_ref.dtype)
        send_ref[a] = jnp.where(parity == 0, high, low).astype(send_ref.dtype)


def apply(scalars, lefts, psi, rights, steps):
    chips, halves, pairs, rows, left_dim = lefts.shape
    right_dim = psi.shape[2]
    some = chips // steps
    out = pl.BlockSpec((some, rows // 2, right_dim), lambda i, s: (i, 0, 0))
    shape = jax.ShapeDtypeStruct((chips, rows // 2, right_dim), psi.dtype)
    return pl.pallas_call(
        apply_kernel,
        out_shape=(shape, shape),
        grid_spec=pltpu.PrefetchScalarGridSpec(
            num_scalar_prefetch=1,
            grid=(steps,),
            in_specs=[
                pl.BlockSpec((some, halves, pairs, rows, left_dim), lambda i, s: (i, 0, 0, 0, 0)),
                pl.BlockSpec((some, left_dim, right_dim), lambda i, s: (i, 0, 0)),
                pl.BlockSpec(rights.shape, lambda i, s: (0, 0, 0, 0)),
            ],
            out_specs=(out, out),
            scratch_shapes=[pltpu.VMEM((halves * pairs, some, rows, right_dim), psi.dtype)],
        ),
        compiler_params=pltpu.CompilerParams(vmem_limit_bytes=48 * MIB),
    )(scalars, lefts, psi, rights)


def local(wavefunction, left_env, right_env, left_sizes, right_sizes):
    sector = lax.axis_index("blk")
    rank = lax.axis_index("mpo")
    sectors, ranks = lax.axis_size("blk"), lax.axis_size("mpo")
    core, parity = sector % 2, rank % 2
    _, left_dim, _ = left_env.shape
    right_dim = right_env.shape[2]
    chips = sectors // 2
    rows = 2 * left_dim // ranks
    own_left = left_sizes[sector]
    own_right = right_sizes[sector]

    swap = [(i, i ^ 1) for i in range(sectors)]
    own_w = lax.dynamic_index_in_dim(left_env, core, 0, keepdims=False)
    other_w = lax.dynamic_index_in_dim(left_env, 1 - core, 0, keepdims=False)
    got = lax.ppermute(other_w, "blk", swap)
    both = jnp.where(core == 0, jnp.stack([own_w, got]), jnp.stack([got, own_w]))
    pieces = both.reshape(2, ranks // 2, rows, left_dim).transpose(1, 0, 2, 3)
    mine = lax.all_to_all(pieces.reshape(ranks, rows, left_dim), "mpo", 0, 0)
    lefts = lax.all_gather(mine, "blk").reshape(chips, 2, ranks, rows, left_dim)

    scalars = jnp.concatenate([jnp.stack([core, own_left]), right_sizes]).astype(jnp.int32)
    keep, send = split_psi(wavefunction, scalars, sectors)
    give = [
        ((2 * chip + z % 2) * ranks + z, (2 * chip + 1 - z % 2) * ranks + z)
        for chip in range(chips)
        for z in range(ranks)
    ]
    given = lax.ppermute(send, ("blk", "mpo"), give)
    columns = jnp.where(core == parity, keep, given)
    groups = [[2 * chip + c for chip in range(chips)] for c in range(2)]
    psi = lax.all_to_all(columns, "blk", 0, 0, axis_index_groups=groups)

    rights = ring_gather(right_env, "mpo", ranks)

    sizes = lax.dynamic_index_in_dim(left_sizes.reshape(chips, 2), parity, 1, keepdims=False)
    first_row = (rank // 2) * rows
    scalars = jnp.concatenate([jnp.stack([parity, first_row, own_right]), sizes])
    kept, sent = apply(scalars.astype(jnp.int32), lefts, psi, rights, 4)

    came = lax.ppermute(sent, "mpo", [(z, z ^ 1) for z in range(ranks)])
    even = jnp.where(parity == 0, kept, came)
    odd = jnp.where(parity == 0, came, kept)
    return jnp.stack([even, odd], axis=1).reshape(sectors, rows // 2, right_dim)


def solution(mesh):
    placed = (P("blk", None), P("mpo", "blk", None), P("mpo", "blk", None), P(), P())
    return jax.shard_map(
        local, mesh=mesh, in_specs=placed, out_specs=P(None, "mpo", "blk"), check_vma=False
    )
```

```python
import functools

import jax
import jax.numpy as jnp
from jax import lax
from jax.experimental import pallas as pl
from jax.experimental.pallas import tpu as pltpu
from jax.sharding import PartitionSpec as P

MIB = 1024 * 1024
SIDE = 4
OFFSETS = (0, SIDE - 1, 1, 2)


def place(y, x, core):
    return ((y % SIDE) * SIDE + x % SIDE) * 2 + core


def stack_kernel(places, *refs):
    inputs, out, sems = refs[: len(places)], refs[-2], refs[-1]
    copies = []
    for i, (ref, (at, lo, hi)) in enumerate(zip(inputs, places)):
        copies.append(pltpu.make_async_copy(ref, out.at[at, lo:hi], sems.at[i]))
    for copy in copies:
        copy.start()
    for copy in copies:
        copy.wait()


def stack(pieces, places, shape):
    return pl.pallas_call(
        functools.partial(stack_kernel, places),
        out_shape=jax.ShapeDtypeStruct(shape, pieces[0].dtype),
        in_specs=[pl.BlockSpec(memory_space=pl.ANY)] * len(pieces),
        out_specs=pl.BlockSpec(memory_space=pl.ANY),
        scratch_shapes=[pltpu.SemaphoreType.DMA((len(pieces),))],
        compiler_params=pltpu.CompilerParams(vmem_limit_bytes=MIB),
    )(*pieces)


def rows_kernel(scalars, psi_ref, out_ref):
    first, own_left = scalars[0], scalars[1]
    sectors, rows, right_dim = out_ref.shape
    row = first + lax.broadcasted_iota(jnp.int32, (rows, right_dim), 0)
    col = lax.broadcasted_iota(jnp.int32, (rows, right_dim), 1)
    for at in range(sectors):
        g, y = at // SIDE, at % SIDE
        b = place(y, g % SIDE, g // SIDE)
        block = psi_ref[:, b * right_dim : (b + 1) * right_dim].astype(jnp.float32)
        inside = jnp.logical_and(row < own_left, col < scalars[2 + b])
        out_ref[at] = jnp.where(inside, block, 0.0).astype(out_ref.dtype)


def split_rows(wavefunction, scalars, sectors, ranks):
    left_dim, columns = wavefunction.shape
    rows, right_dim = left_dim // ranks, columns // sectors
    return pl.pallas_call(
        rows_kernel,
        out_shape=jax.ShapeDtypeStruct((sectors, rows, right_dim), wavefunction.dtype),
        grid_spec=pltpu.PrefetchScalarGridSpec(
            num_scalar_prefetch=1,
            grid=(1,),
            in_specs=[pl.BlockSpec((rows, columns), lambda i, s: (s[0] // rows, 0))],
            out_specs=pl.BlockSpec((sectors, rows, right_dim), lambda i, s: (0, 0, 0)),
        ),
        compiler_params=pltpu.CompilerParams(vmem_limit_bytes=60 * MIB),
    )(scalars, wavefunction)


def add_blocks(scalars, pieces, refs, psi_ref, right_ref, total):
    core, x0, y0, rank = scalars[0], scalars[1], scalars[2], scalars[3]
    ranks, parts, rows, right_dim = psi_ref.shape
    for ref, (sibling, far, first) in zip(refs, pieces):
        tree = 1 - core if sibling else core
        for k in range(ref.shape[0]):
            near = OFFSETS[first + k]
            y = jnp.where(tree == 0, y0 + far, y0 + near) & (SIDE - 1)
            x = jnp.where(tree == 0, x0 + near, x0 + far) & (SIDE - 1)
            at = (2 * x + tree - rank) & (ranks - 1)
            psi = psi_ref[:, pl.ds(y, 1)].reshape(ranks * rows, right_dim)
            _, left_dim, inner = ref.shape[1:]
            block = ref[k].reshape(2 * left_dim, inner)
            both = jnp.dot(block, psi, preferred_element_type=jnp.float32).astype(psi.dtype)
            term = jnp.dot(both[:left_dim], right_ref[at, 0], preferred_element_type=jnp.float32)
            term += jnp.dot(both[left_dim:], right_ref[at, 1], preferred_element_type=jnp.float32)
            total[y] += term


def first_kernel(pieces, scalars, *refs):
    blocks, (psi_ref, right_ref, total) = refs[: len(pieces)], refs[len(pieces) :]
    total[...] = jnp.zeros_like(total)
    add_blocks(scalars, pieces, blocks, psi_ref, right_ref, total)


def last_kernel(pieces, scalars, *refs):
    blocks, (psi_ref, right_ref, total_in, out_ref, total) = refs[: len(pieces)], refs[len(pieces) :]
    total[...] = total_in[...]
    add_blocks(scalars, pieces, blocks, psi_ref, right_ref, total)
    ranks, parts, rows, right_dim = out_ref.shape
    row = lax.broadcasted_iota(jnp.int32, (ranks * rows, right_dim), 0)
    col = lax.broadcasted_iota(jnp.int32, (ranks * rows, right_dim), 1)
    for y in range(parts):
        inside = jnp.logical_and(row < scalars[5 + y], col < scalars[4])
        block = jnp.where(inside, total[y], 0.0).astype(out_ref.dtype)
        out_ref[:, y] = block.reshape(ranks, rows, right_dim)


def call(kernel, pieces, scalars, arrays, shape, scratch):
    smem = pl.BlockSpec(memory_space=pltpu.SMEM)
    vmem = pl.BlockSpec(memory_space=pltpu.VMEM)
    return pl.pallas_call(
        functools.partial(kernel, pieces),
        out_shape=shape,
        in_specs=[smem] + [vmem] * len(arrays),
        out_specs=vmem,
        scratch_shapes=scratch,
        compiler_params=pltpu.CompilerParams(vmem_limit_bytes=28 * MIB),
    )(scalars, *arrays)


def local(wavefunction, left_env, right_env, left_sizes, right_sizes):
    sector = lax.axis_index("blk")
    rank = lax.axis_index("mpo")
    sectors, ranks = lax.axis_size("blk"), lax.axis_size("mpo")
    left_dim, right_dim = left_env.shape[2], right_env.shape[2]
    rows = left_dim // ranks
    core, x0, y0 = sector % 2, sector // 2 % SIDE, sector // (2 * SIDE)
    spots = [(y, x, c) for y in range(SIDE) for x in range(SIDE) for c in range(2)]

    def axis_step(second, by):
        pairs = []
        for y, x, c in spots:
            along_x = (c == 0) != second
            to = place(y, x + by, c) if along_x else place(y + by, x, c)
            pairs.append((place(y, x, c), to))
        return pairs

    turn = [
        (place(y, x, c) * ranks + z, place(y, z // 2, z % 2) * ranks + x + SIDE * c)
        for y, x, c in spots
        for z in range(ranks)
    ]
    own = lax.ppermute(left_env, ("blk", "mpo"), turn)

    scalars = jnp.concatenate([jnp.stack([rank * rows, left_sizes[sector]]), right_sizes])
    mine = split_rows(wavefunction, scalars.astype(jnp.int32), sectors, ranks)
    order = [place(y, g % SIDE, g // SIDE) for g in range(ranks) for y in range(SIDE)]
    spread = lax.all_to_all(mine, "blk", 0, 0, axis_index_groups=[order])
    spread = spread.reshape(ranks, SIDE, rows, right_dim)
    own, spread = lax.optimization_barrier((own, spread))

    below = lax.ppermute(own, "blk", axis_step(False, 1))
    above = lax.ppermute(own, "blk", axis_step(False, -1))
    below2 = lax.ppermute(below[:1], "blk", axis_step(False, 1))
    above2 = lax.ppermute(above[1:], "blk", axis_step(False, -1))
    line = stack(
        (own, below, above, below2, above2),
        ((0, 0, 2), (1, 0, 2), (2, 0, 2), (3, 0, 1), (3, 1, 2)),
        (SIDE, *left_env.shape),
    )
    line, spread = lax.optimization_barrier((line, spread))
    line_below = lax.ppermute(line, "blk", axis_step(True, 1))
    line_above = lax.ppermute(line, "blk", axis_step(True, -1))
    far_below = lax.ppermute(line_below[: SIDE // 2], "blk", axis_step(True, 1))
    far_above = lax.ppermute(line_above[SIDE // 2 :], "blk", axis_step(True, -1))
    psi = lax.all_to_all(spread, "mpo", 0, 0)

    swap = [(i, i ^ 1) for i in range(sectors)]
    near = [line, line_below, line_above]
    near += [lax.ppermute(block, "blk", swap) for block in near]
    distant = [far_below, far_above]
    distant += [lax.ppermute(block, "blk", swap) for block in distant]

    up = [(z, (z + 1) % ranks) for z in range(ranks)]
    down = [(z, (z - 1) % ranks) for z in range(ranks)]
    ring = {0: right_env}
    for hop in range(1, ranks // 2 + 1):
        ring[ranks - hop] = lax.ppermute(ring[(ranks + 1 - hop) % ranks], "mpo", up)
        if 2 * hop < ranks:
            ring[hop] = lax.ppermute(ring[hop - 1], "mpo", down)
    rights = stack(
        [ring[i] for i in range(ranks)],
        [(i, 0, 2) for i in range(ranks)],
        (ranks, *right_env.shape),
    )

    group = jnp.stack([left_sizes[place(y, 0, 0) + rank % SIDE * 2 + rank // SIDE] for y in range(SIDE)])
    scalars = jnp.concatenate([jnp.stack([core, x0, y0, rank, right_sizes[sector]]), group])
    scalars = scalars.astype(jnp.int32)
    total = jax.ShapeDtypeStruct((SIDE, left_dim, right_dim), jnp.float32)
    pieces = tuple((s, d, 0) for s in (False, True) for d in (0, SIDE - 1, 1))
    begun = call(first_kernel, pieces, scalars, (*near, psi, rights), total, [])
    pieces = tuple((s, 2, k) for s in (False, True) for k in (0, SIDE // 2))
    done = call(
        last_kernel,
        pieces,
        scalars,
        (*distant, psi, rights, begun),
        jax.ShapeDtypeStruct((ranks, SIDE, rows, right_dim), wavefunction.dtype),
        [pltpu.VMEM(total.shape, total.dtype)],
    )

    out = lax.all_to_all(done, "mpo", 0, 0).reshape(2, SIDE, SIDE, rows, right_dim)
    return out.transpose(2, 1, 0, 3, 4).reshape(sectors, rows, right_dim)


def solution(mesh):
    placed = (P("blk", None), P("mpo", "blk", None), P("mpo", "blk", None), P(), P())
    return jax.shard_map(
        local, mesh=mesh, in_specs=placed, out_specs=P(None, "mpo", "blk"), check_vma=False
    )
```

```python
import functools

import jax
import jax.numpy as jnp
from jax import lax
from jax.experimental import pallas as pl
from jax.experimental.pallas import tpu as pltpu
from jax.sharding import PartitionSpec as P

MIB = 1024 * 1024
VMEM_LIMIT = 60
SIDE = 4
OFFSETS = (0, SIDE - 1, 1, 2)


def place(y, x, core):
    return ((y % SIDE) * SIDE + x % SIDE) * 2 + core


def stack_kernel(places, *refs):
    inputs, out, sems = refs[: len(places)], refs[-2], refs[-1]
    copies = []
    for i, (ref, (at, lo, hi)) in enumerate(zip(inputs, places)):
        copies.append(pltpu.make_async_copy(ref, out.at[at, lo:hi], sems.at[i]))
    for copy in copies:
        copy.start()
    for copy in copies:
        copy.wait()


def stack(pieces, places, shape):
    return pl.pallas_call(
        functools.partial(stack_kernel, places),
        out_shape=jax.ShapeDtypeStruct(shape, pieces[0].dtype),
        in_specs=[pl.BlockSpec(memory_space=pl.ANY)] * len(pieces),
        out_specs=pl.BlockSpec(memory_space=pl.ANY),
        scratch_shapes=[pltpu.SemaphoreType.DMA((len(pieces),))],
        compiler_params=pltpu.CompilerParams(vmem_limit_bytes=MIB),
    )(*pieces)


def coordinates():
    sector, rank = lax.axis_index("blk"), lax.axis_index("mpo")
    return sector, rank, sector % 2, sector // 2 % SIDE, sector // (2 * SIDE)


def rows_kernel(left_sizes, right_sizes, psi_ref, out_ref, held, sem):
    sector, rank, _, _, _ = coordinates()
    sectors, rows, right_dim = out_ref.shape
    first = pl.multiple_of(rank * rows, rows)
    copy = pltpu.make_async_copy(psi_ref.at[pl.ds(first, rows)], held, sem)
    copy.start()
    copy.wait()
    row = first + lax.broadcasted_iota(jnp.int32, (rows, right_dim), 0)
    col = lax.broadcasted_iota(jnp.int32, (rows, right_dim), 1)
    own_left = left_sizes[sector]
    for at in range(sectors):
        g, y = at // SIDE, at % SIDE
        b = place(y, g % SIDE, g // SIDE)
        block = held[:, b * right_dim : (b + 1) * right_dim].astype(jnp.float32)
        inside = jnp.logical_and(row < own_left, col < right_sizes[b])
        out_ref[at] = jnp.where(inside, block, 0.0).astype(out_ref.dtype)


SMEM = pl.BlockSpec(memory_space=pltpu.SMEM)
VMEM = pl.BlockSpec(memory_space=pltpu.VMEM)


def split_rows(wavefunction, left_sizes, right_sizes, ranks):
    left_dim, columns = wavefunction.shape
    sectors = left_sizes.shape[0]
    rows, right_dim = left_dim // ranks, columns // sectors
    return pl.pallas_call(
        rows_kernel,
        out_shape=jax.ShapeDtypeStruct((sectors, rows, right_dim), wavefunction.dtype),
        in_specs=[SMEM, SMEM, pl.BlockSpec(memory_space=pl.ANY)],
        out_specs=VMEM,
        scratch_shapes=[pltpu.VMEM((rows, columns), wavefunction.dtype), pltpu.SemaphoreType.DMA],
        compiler_params=pltpu.CompilerParams(vmem_limit_bytes=60 * MIB),
    )(left_sizes, right_sizes, wavefunction)


def fetch(refs, held, sems, first):
    copies = [pltpu.make_async_copy(r, h, sems.at[first + i]) for i, (r, h) in enumerate(zip(refs, held))]
    for copy in copies:
        copy.start()
    return copies


def add_blocks(pieces, refs, total_in, total, held, psi_held, right_held, sems):
    _, rank, core, x0, y0 = coordinates()
    ranks, parts, rows, right_dim = psi_held.shape
    blocks, psi_ref, rights = refs[: len(pieces)], refs[len(pieces)], refs[len(pieces) + 1 :]
    needed = fetch((psi_ref, *rights), (psi_held, *(right_held.at[i] for i in range(ranks))), sems, 0)
    if total_in is not None:
        needed += fetch((total_in,), (total,), sems, len(needed))
    coming = fetch(blocks, [held.at[i] for i in range(len(pieces))], sems, len(needed))
    if total_in is None:
        total[...] = jnp.zeros_like(total)
    for copy in needed:
        copy.wait()
    for i, (sibling, far, first) in enumerate(pieces):
        tree = 1 - core if sibling else core
        coming[i].wait()
        _, count, _, left_dim, inner = held.shape
        for k in range(count):
            near = OFFSETS[first + k]
            y = jnp.where(tree == 0, y0 + far, y0 + near) & (SIDE - 1)
            x = jnp.where(tree == 0, x0 + near, x0 + far) & (SIDE - 1)
            at = (2 * x + tree - rank) & (ranks - 1)
            psi = psi_held[:, pl.ds(y, 1)].reshape(ranks * rows, right_dim)
            block = held[i, k].reshape(2 * left_dim, inner)
            both = jnp.dot(block, psi, preferred_element_type=jnp.float32).astype(psi.dtype)
            term = jnp.dot(both[:left_dim], right_held[at, 0], preferred_element_type=jnp.float32)
            term += jnp.dot(both[left_dim:], right_held[at, 1], preferred_element_type=jnp.float32)
            total[y] += term


def first_kernel(pieces, *refs):
    refs, (total, held, psi_held, right_held, sems) = refs[:-5], refs[-5:]
    add_blocks(pieces, refs, None, total, held, psi_held, right_held, sems)


def last_kernel(pieces, left_sizes, right_sizes, total_in, *refs):
    refs, (out_ref, total, held, psi_held, right_held, sems) = refs[:-6], refs[-6:]
    add_blocks(pieces, refs, total_in, total, held, psi_held, right_held, sems)
    sector, rank, _, _, _ = coordinates()
    own_right = right_sizes[sector]
    ranks, parts, rows, right_dim = out_ref.shape
    row = lax.broadcasted_iota(jnp.int32, (ranks * rows, right_dim), 0)
    col = lax.broadcasted_iota(jnp.int32, (ranks * rows, right_dim), 1)
    for y in range(parts):
        own_left = left_sizes[2 * SIDE * y + rank % SIDE * 2 + rank // SIDE]
        inside = jnp.logical_and(row < own_left, col < own_right)
        block = jnp.where(inside, total[y], 0.0).astype(out_ref.dtype)
        out_ref[:, y] = block.reshape(ranks, rows, right_dim)


def call(kernel, pieces, ready, blocks, psi, rights, shape, scratch):
    dtype = psi.dtype
    scratch = scratch + [
        pltpu.VMEM((len(pieces), *blocks[0].shape), dtype),
        pltpu.VMEM(psi.shape, dtype),
        pltpu.VMEM((len(rights), *rights[0].shape), dtype),
        pltpu.SemaphoreType.DMA((len(pieces) + len(rights) + 2,)),
    ]
    anywhere = pl.BlockSpec(memory_space=pl.ANY)
    others = (*blocks, psi, *rights)
    return pl.pallas_call(
        functools.partial(kernel, pieces),
        out_shape=shape,
        in_specs=[SMEM, SMEM, anywhere][: len(ready)] + [anywhere] * len(others),
        out_specs=VMEM,
        scratch_shapes=scratch,
        compiler_params=pltpu.CompilerParams(vmem_limit_bytes=VMEM_LIMIT * MIB),
    )(*ready, *others)


def together(*values):
    return lax.optimization_barrier(values)


def local(wavefunction, left_env, right_env, left_sizes, right_sizes):
    sectors, ranks = lax.axis_size("blk"), lax.axis_size("mpo")
    left_dim, right_dim = left_env.shape[2], right_env.shape[2]
    rows = left_dim // ranks
    spots = [(y, x, c) for y in range(SIDE) for x in range(SIDE) for c in range(2)]

    def step(second, by):
        pairs = []
        for y, x, c in spots:
            along_x = (c == 0) != second
            to = place(y, x + by, c) if along_x else place(y + by, x, c)
            pairs.append((place(y, x, c), to))
        return pairs

    def near_step(block, by):
        return lax.ppermute(block, "blk", step(False, by))

    def far_step(block, by):
        return lax.ppermute(block, "blk", step(True, by))

    def swap(block):
        return lax.ppermute(block, "blk", [(i, i ^ 1) for i in range(sectors)])

    def up(block):
        return lax.ppermute(block, "mpo", [(z, (z + 1) % ranks) for z in range(ranks)])

    def down(block):
        return lax.ppermute(block, "mpo", [(z, (z - 1) % ranks) for z in range(ranks)])

    turn = [
        (place(y, x, c) * ranks + z, place(y, z // 2, z % 2) * ranks + x + SIDE * c)
        for y, x, c in spots
        for z in range(ranks)
    ]
    own = lax.ppermute(left_env, ("blk", "mpo"), turn)
    up1, down1 = up(right_env), down(right_env)
    mine = split_rows(wavefunction, left_sizes, right_sizes, ranks)
    order = [place(y, g % SIDE, g // SIDE) for g in range(ranks) for y in range(SIDE)]
    own, up1, down1, mine = together(own, up1, down1, mine)
    spread = lax.all_to_all(mine, "blk", 0, 0, axis_index_groups=[order])
    spread = spread.reshape(ranks, SIDE, rows, right_dim)

    below, above = near_step(own, 1), near_step(own, -1)
    up2, down2 = up(up1), down(down1)
    below, above, up2, down2 = together(below, above, up2, down2)

    two = near_step(below, 1)
    line_a = stack((own, below), ((0, 0, 2), (1, 0, 2)), (2, *left_env.shape))
    a_below, a_above = far_step(line_a, 1), far_step(line_a, -1)
    up3, down3 = up(up2), down(down2)
    two, up3, down3 = together(two, up3, down3)

    line_b = stack((above, two), ((0, 0, 2), (1, 0, 2)), (2, *left_env.shape))
    b_below, b_above = far_step(line_b, 1), far_step(line_b, -1)
    up4 = up(up3)
    line_b, a_below, a_above, spread = together(line_b, a_below, a_above, spread)
    a_two = far_step(a_below, 1)
    psi = lax.all_to_all(spread, "mpo", 0, 0)
    b_two = far_step(b_above, -1)

    rights = (right_env, down1, down2, down3, up4, up3, up2, up1)
    early = (line_a, line_b, a_below, a_above, b_below, b_above)
    early += tuple(swap(block) for block in early)
    late = (a_two, b_two)
    late += tuple(swap(block) for block in late)
    total = jax.ShapeDtypeStruct((SIDE, left_dim, right_dim), jnp.float32)
    places = ((0, 0), (0, 2), (SIDE - 1, 0), (1, 0), (SIDE - 1, 2), (1, 2))
    pieces = tuple((s, *p) for s in (False, True) for p in places)
    begun = call(first_kernel, pieces, (), early, psi, rights, total, [])
    pieces = tuple((s, 2, k) for s in (False, True) for k in (0, 2))
    done = call(
        last_kernel,
        pieces,
        (left_sizes, right_sizes, begun),
        late,
        psi,
        rights,
        jax.ShapeDtypeStruct((ranks, SIDE, rows, right_dim), wavefunction.dtype),
        [pltpu.VMEM(total.shape, total.dtype)],
    )

    out = lax.all_to_all(done, "mpo", 0, 0).reshape(2, SIDE, SIDE, rows, right_dim)
    return out.transpose(2, 1, 0, 3, 4).reshape(sectors, rows, right_dim)


def solution(mesh):
    placed = (P("blk", None), P("mpo", "blk", None), P("mpo", "blk", None), P(), P())
    return jax.shard_map(
        local, mesh=mesh, in_specs=placed, out_specs=P(None, "mpo", "blk"), check_vma=False
    )
```

```python
import functools

import jax
import jax.numpy as jnp
from jax import lax
from jax.experimental import pallas as pl
from jax.experimental.pallas import tpu as pltpu
from jax.sharding import PartitionSpec as P

MIB = 1024 * 1024
SIDE = 4
OFFSETS = (0, SIDE - 1, 1, 2)


def place(y, x, core):
    return ((y % SIDE) * SIDE + x % SIDE) * 2 + core


def stack_kernel(places, *refs):
    inputs, out, sems = refs[: len(places)], refs[-2], refs[-1]
    copies = []
    for i, (ref, (at, lo, hi)) in enumerate(zip(inputs, places)):
        copies.append(pltpu.make_async_copy(ref, out.at[at, lo:hi], sems.at[i]))
    for copy in copies:
        copy.start()
    for copy in copies:
        copy.wait()


def stack(pieces, places, shape):
    return pl.pallas_call(
        functools.partial(stack_kernel, places),
        out_shape=jax.ShapeDtypeStruct(shape, pieces[0].dtype),
        in_specs=[pl.BlockSpec(memory_space=pl.ANY)] * len(pieces),
        out_specs=pl.BlockSpec(memory_space=pl.ANY),
        scratch_shapes=[pltpu.SemaphoreType.DMA((len(pieces),))],
        compiler_params=pltpu.CompilerParams(vmem_limit_bytes=MIB),
    )(*pieces)


def coordinates():
    sector, rank = lax.axis_index("blk"), lax.axis_index("mpo")
    return sector, rank, sector % 2, sector // 2 % SIDE, sector // (2 * SIDE)


def columns_kernel(left_sizes, right_sizes, psi_ref, *refs):
    outs, (held, sems) = refs[:SIDE], refs[SIDE:]
    sector, rank, _, _, y0 = coordinates()
    _, left_dim, right_dim = outs[0].shape
    at = [2 * SIDE * ((y0 + ahead) & (SIDE - 1)) + rank for ahead in range(SIDE)]
    copies = []
    for ahead in range(SIDE):
        first = pl.multiple_of(at[ahead] * right_dim, right_dim)
        source = psi_ref.at[:, pl.ds(first, right_dim)]
        copies.append(pltpu.make_async_copy(source, held.at[ahead], sems.at[ahead]))
    for copy in copies:
        copy.start()
    row = lax.broadcasted_iota(jnp.int32, (left_dim, right_dim), 0)
    col = lax.broadcasted_iota(jnp.int32, (left_dim, right_dim), 1)
    own_left = left_sizes[sector]
    for ahead in range(SIDE):
        copies[ahead].wait()
        block = held[ahead].astype(jnp.float32)
        inside = jnp.logical_and(row < own_left, col < right_sizes[at[ahead]])
        outs[ahead][0] = jnp.where(inside, block, 0.0).astype(outs[ahead].dtype)


SMEM = pl.BlockSpec(memory_space=pltpu.SMEM)
VMEM = pl.BlockSpec(memory_space=pltpu.VMEM)


def pick_columns(wavefunction, left_sizes, right_sizes):
    left_dim, columns = wavefunction.shape
    shape = (1, left_dim, columns // right_sizes.shape[0])
    return pl.pallas_call(
        columns_kernel,
        out_shape=[jax.ShapeDtypeStruct(shape, wavefunction.dtype)] * SIDE,
        in_specs=[SMEM, SMEM, pl.BlockSpec(memory_space=pl.ANY)],
        out_specs=[VMEM] * SIDE,
        scratch_shapes=[
            pltpu.VMEM((SIDE, *shape[1:]), wavefunction.dtype),
            pltpu.SemaphoreType.DMA((SIDE,)),
        ],
        compiler_params=pltpu.CompilerParams(vmem_limit_bytes=60 * MIB),
    )(left_sizes, right_sizes, wavefunction)


def fetch(refs, held, sems, first):
    copies = [pltpu.make_async_copy(r, h, sems.at[first + i]) for i, (r, h) in enumerate(zip(refs, held))]
    for copy in copies:
        copy.start()
    return copies


def apply_kernel(pieces, left_sizes, right_sizes, *refs):
    refs, (out_ref, total, held, psi_held, right_held, sems) = refs[:-6], refs[-6:]
    sector, rank, core, x0, y0 = coordinates()
    ranks, parts, rows, right_dim = out_ref.shape
    blocks, others = refs[: len(pieces)], refs[len(pieces) :]
    places = [psi_held.at[pl.ds(i, 1)] for i in range(parts)] + [right_held.at[i] for i in range(ranks)]
    needed = fetch(others, places, sems, 0)
    coming = fetch(blocks, [held.at[i] for i in range(len(pieces))], sems, len(needed))
    total[...] = jnp.zeros_like(total)
    for copy in needed:
        copy.wait()
    _, count, _, left_dim, inner = held.shape
    for i, (sibling, far, first) in enumerate(pieces):
        tree = 1 - core if sibling else core
        coming[i].wait()
        for k in range(count):
            near = OFFSETS[first + k]
            y = jnp.where(tree == 0, y0 + far, y0 + near) & (SIDE - 1)
            x = jnp.where(tree == 0, x0 + near, x0 + far) & (SIDE - 1)
            at = (2 * x + tree - rank) & (ranks - 1)
            block = held[i, k].reshape(2 * left_dim, inner)
            both = jnp.dot(block, psi_held[(y0 - y) & (SIDE - 1)], preferred_element_type=jnp.float32).astype(out_ref.dtype)
            term = jnp.dot(both[:left_dim], right_held[at, 0], preferred_element_type=jnp.float32)
            term += jnp.dot(both[left_dim:], right_held[at, 1], preferred_element_type=jnp.float32)
            total[y] += term
    own_right = right_sizes[sector]
    row = lax.broadcasted_iota(jnp.int32, (left_dim, right_dim), 0)
    col = lax.broadcasted_iota(jnp.int32, (left_dim, right_dim), 1)
    for y in range(parts):
        own_left = left_sizes[2 * SIDE * y + rank % SIDE * 2 + rank // SIDE]
        inside = jnp.logical_and(row < own_left, col < own_right)
        block = jnp.where(inside, total[y], 0.0).astype(out_ref.dtype)
        out_ref[:, y] = block.reshape(ranks, rows, right_dim)


def apply(pieces, blocks, psi, rights, left_sizes, right_sizes):
    dtype, ranks, parts = psi[0].dtype, len(rights), len(psi)
    _, left_dim, right_dim = psi[0].shape
    anywhere = pl.BlockSpec(memory_space=pl.ANY)
    others = (*blocks, *psi, *rights)
    return pl.pallas_call(
        functools.partial(apply_kernel, pieces),
        out_shape=jax.ShapeDtypeStruct((ranks, parts, left_dim // ranks, right_dim), dtype),
        in_specs=[SMEM, SMEM] + [anywhere] * len(others),
        out_specs=VMEM,
        scratch_shapes=[
            pltpu.VMEM((parts, left_dim, right_dim), jnp.float32),
            pltpu.VMEM((len(pieces), *blocks[0].shape), dtype),
            pltpu.VMEM((parts, left_dim, right_dim), dtype),
            pltpu.VMEM((ranks, *rights[0].shape), dtype),
            pltpu.SemaphoreType.DMA((len(others),)),
        ],
        compiler_params=pltpu.CompilerParams(vmem_limit_bytes=60 * MIB),
    )(left_sizes, right_sizes, *others)


def together(*values):
    return lax.optimization_barrier(values)


def local(wavefunction, left_env, right_env, left_sizes, right_sizes):
    sectors, ranks = lax.axis_size("blk"), lax.axis_size("mpo")
    rows, right_dim = left_env.shape[1] // ranks, right_env.shape[2]
    spots = [(y, x, c) for y in range(SIDE) for x in range(SIDE) for c in range(2)]

    def step(second, by):
        pairs = []
        for y, x, c in spots:
            along_x = (c == 0) != second
            to = place(y, x + by, c) if along_x else place(y + by, x, c)
            pairs.append((place(y, x, c), to))
        return pairs

    def near_step(block, by):
        return lax.ppermute(block, "blk", step(False, by))

    def far_step(block, by):
        return lax.ppermute(block, "blk", step(True, by))

    def swap(block):
        return lax.ppermute(block, "blk", [(i, i ^ 1) for i in range(sectors)])

    def up(block):
        return lax.ppermute(block, "mpo", [(z, (z + 1) % ranks) for z in range(ranks)])

    def down(block):
        return lax.ppermute(block, "mpo", [(z, (z - 1) % ranks) for z in range(ranks)])

    turn = [
        (place(y, x, c) * ranks + z, place(y, z // 2, z % 2) * ranks + x + SIDE * c)
        for y, x, c in spots
        for z in range(ranks)
    ]
    own = lax.ppermute(left_env, ("blk", "mpo"), turn)
    up1, down1 = up(right_env), down(right_env)
    mine = pick_columns(wavefunction, left_sizes, right_sizes)
    own, *mine = together(own, *mine)

    def turned(block):
        return lax.ppermute(block, ("blk", "mpo"), turn)

    def rows_on(block, by):
        pairs = [(place(y, x, c), place(y + by, x, c)) for y, x, c in spots]
        return lax.ppermute(block, "blk", pairs)

    below, above = near_step(own, 1), near_step(own, -1)
    psi1 = turned(mine[1])
    below, above, up1, down1, psi1 = together(below, above, up1, down1, psi1)

    two = near_step(below, 1)
    line_a = stack((own, below), ((0, 0, 2), (1, 0, 2)), (2, *left_env.shape))
    a_below, a_above = far_step(line_a, 1), far_step(line_a, -1)
    up2, down2 = up(up1), down(down1)
    psi3 = turned(mine[3])
    two, up2, down2, psi3 = together(two, up2, down2, psi3)

    line_b = stack((above, two), ((0, 0, 2), (1, 0, 2)), (2, *left_env.shape))
    b_below, b_above = far_step(line_b, 1), far_step(line_b, -1)
    up3, down3 = up(up2), down(down2)
    psi1, psi2 = rows_on(psi1, 1), turned(mine[2])
    a_below, a_above, up3, psi2 = together(a_below, a_above, up3, psi2)

    a_two = far_step(a_below, 1)
    up4 = up(up3)
    psi3, psi2, psi0 = rows_on(psi3, 3), rows_on(psi2, 2), turned(mine[0])
    b_two = far_step(b_above, -1)
    psi = (psi0, psi1, psi2, psi3)

    rights = (right_env, down1, down2, down3, up4, up3, up2, up1)
    blocks = (line_a, line_b, a_below, a_above, b_below, b_above, a_two, b_two)
    blocks += tuple(swap(block) for block in blocks)
    places = ((0, 0), (0, 2), (SIDE - 1, 0), (1, 0), (SIDE - 1, 2), (1, 2), (2, 0), (2, 2))
    pieces = tuple((s, *p) for s in (False, True) for p in places)
    done = apply(pieces, blocks, psi, rights, left_sizes, right_sizes)

    out = lax.all_to_all(done, "mpo", 0, 0).reshape(2, SIDE, SIDE, rows, right_dim)
    return out.transpose(2, 1, 0, 3, 4).reshape(sectors, rows, right_dim)


def solution(mesh):
    placed = (P("blk", None), P("mpo", "blk", None), P("mpo", "blk", None), P(), P())
    return jax.shard_map(
        local, mesh=mesh, in_specs=placed, out_specs=P(None, "mpo", "blk"), check_vma=False
    )
```

```python
import functools

import jax
import jax.numpy as jnp
from jax import lax
from jax.experimental import pallas as pl
from jax.experimental.pallas import tpu as pltpu
from jax.sharding import PartitionSpec as P

MIB = 1024 * 1024
SIDE = 4
OFFSETS = (0, SIDE - 1, 1, 2)
ANYWHERE = pl.BlockSpec(memory_space=pl.ANY)
SMEM = pl.BlockSpec(memory_space=pltpu.SMEM)
VMEM = pl.BlockSpec(memory_space=pltpu.VMEM)


def place(y, x, core):
    return ((y % SIDE) * SIDE + x % SIDE) * 2 + core


def stack_kernel(*refs):
    inputs, out, sems = refs[:-2], refs[-2], refs[-1]
    copies = [pltpu.make_async_copy(ref, out.at[i], sems.at[i]) for i, ref in enumerate(inputs)]
    for copy in copies:
        copy.start()
    for copy in copies:
        copy.wait()


def stack(*pieces):
    return pl.pallas_call(
        stack_kernel,
        out_shape=jax.ShapeDtypeStruct((len(pieces), *pieces[0].shape), pieces[0].dtype),
        in_specs=[ANYWHERE] * len(pieces),
        out_specs=ANYWHERE,
        scratch_shapes=[pltpu.SemaphoreType.DMA((len(pieces),))],
        compiler_params=pltpu.CompilerParams(vmem_limit_bytes=MIB),
    )(*pieces)


def split_kernel(psi_ref, out_ref, sems):
    sectors, _, right_dim = out_ref.shape
    copies = []
    for b in range(sectors):
        source = psi_ref.at[:, pl.ds(b * right_dim, right_dim)]
        copies.append(pltpu.make_async_copy(source, out_ref.at[b], sems.at[b]))
    for copy in copies:
        copy.start()
    for copy in copies:
        copy.wait()


def split(wavefunction, sectors):
    left_dim, columns = wavefunction.shape
    return pl.pallas_call(
        split_kernel,
        out_shape=jax.ShapeDtypeStruct((sectors, left_dim, columns // sectors), wavefunction.dtype),
        in_specs=[ANYWHERE],
        out_specs=ANYWHERE,
        scratch_shapes=[pltpu.SemaphoreType.DMA((sectors,))],
        compiler_params=pltpu.CompilerParams(vmem_limit_bytes=60 * MIB),
    )(wavefunction)


def fetch(refs, held, sems, first):
    copies = [pltpu.make_async_copy(r, h, sems.at[first + i]) for i, (r, h) in enumerate(zip(refs, held))]
    for copy in copies:
        copy.start()
    return copies


def apply_kernel(groups, carried, left_sizes, right_sizes, *refs):
    refs, (out_ref, held, psi_held, right_held, middle, result, sems, out_sems) = refs[:-8], refs[-8:]
    refs = refs[1:] if carried else refs
    sector, rank = lax.axis_index("blk"), lax.axis_index("mpo")
    core, x0, y0 = sector % 2, sector // 2 % SIDE, sector // (2 * SIDE)
    sectors, rows, right_dim = out_ref.shape
    pieces = [piece for group in groups for piece in group]
    blocks, psi_ref, rights = refs[: len(pieces)], refs[len(pieces)], refs[len(pieces) + 1 :]
    ranks = len(rights)
    coming = fetch(blocks[: len(groups[0])], [held.at[i] for i in range(len(groups[0]))], sems, 0)
    psi_copy = pltpu.make_async_copy(psi_ref, psi_held, sems.at[len(pieces)])
    psi_copy.start()
    right_copies = fetch(rights, [right_held.at[i] for i in range(ranks)], sems, len(pieces) + 1)
    for i in range(len(groups[0]), len(pieces)):
        coming += fetch(blocks[i : i + 1], [held.at[i]], sems, i)
    own_right = right_sizes[sector]
    left_dim = psi_held.shape[1]
    psi_row = lax.broadcasted_iota(jnp.int32, (left_dim, right_dim), 0)
    psi_col = lax.broadcasted_iota(jnp.int32, (left_dim, right_dim), 1)
    row = rank * rows + lax.broadcasted_iota(jnp.int32, (rows, right_dim), 0)
    col = lax.broadcasted_iota(jnp.int32, (rows, right_dim), 1)
    psi_copy.wait()
    at, going = 0, []
    for number, group in enumerate(groups):
        places = []
        for sibling, far, first in group:
            coming[at].wait()
            tree = 1 - core if sibling else core
            for k in range(held.shape[1]):
                near = OFFSETS[first + k]
                y = jnp.where(tree == 0, y0 + far, y0 + near) & (SIDE - 1)
                x = jnp.where(tree == 0, x0 + near, x0 + far) & (SIDE - 1)
                a = (y * SIDE + x) * 2 + tree
                inside = jnp.logical_and(psi_row < left_sizes[a], psi_col < own_right)
                psi = jnp.where(inside, psi_held[a].astype(jnp.float32), 0.0).astype(middle.dtype)
                block = held[at, k].reshape(2 * ranks * rows, left_dim)
                both = jnp.dot(block, psi, preferred_element_type=jnp.float32).astype(middle.dtype)
                middle[:, len(places)] = both.reshape(2 * ranks, rows, right_dim)
                places.append(a)
            at += 1
        if number == 0:
            for copy in right_copies:
                copy.wait()
        count = len(places)
        total = jnp.zeros((count * rows, right_dim), jnp.float32)
        for w in range(2 * ranks):
            right = right_held[(w // 2 - rank) & (ranks - 1), w % 2]
            block = middle[w, :count].reshape(count * rows, right_dim)
            total += jnp.dot(block, right, preferred_element_type=jnp.float32)
        for i, a in enumerate(places):
            inside = jnp.logical_and(row < left_sizes[a], col < own_right)
            part = jnp.where(inside, total[i * rows : (i + 1) * rows], 0.0)
            slot = number * count + i
            result[slot] = part.astype(result.dtype)
            going.append(pltpu.make_async_copy(result.at[slot], out_ref.at[a], out_sems.at[slot]))
            going[-1].start()
    for copy in going:
        copy.wait()


def apply(groups, blocks, psi, rights, left_sizes, right_sizes, carried):
    dtype, ranks = psi.dtype, len(rights)
    sectors, left_dim, right_dim = psi.shape
    rows = left_dim // ranks
    pieces, some = len(blocks), blocks[0].shape[0]
    count = some * len(groups[0])
    before = () if carried is None else (carried,)
    others = (*before, *blocks, psi, *rights)
    return pl.pallas_call(
        functools.partial(apply_kernel, groups, carried is not None),
        out_shape=jax.ShapeDtypeStruct((sectors, rows, right_dim), dtype),
        in_specs=[SMEM, SMEM] + [ANYWHERE] * len(others),
        out_specs=ANYWHERE,
        scratch_shapes=[
            pltpu.VMEM((pieces, *blocks[0].shape), dtype),
            pltpu.VMEM(psi.shape, dtype),
            pltpu.VMEM((ranks, *rights[0].shape), dtype),
            pltpu.VMEM((2 * ranks, count, rows, right_dim), dtype),
            pltpu.VMEM((count * len(groups), rows, right_dim), dtype),
            pltpu.SemaphoreType.DMA((pieces + ranks + 1,)),
            pltpu.SemaphoreType.DMA((count * len(groups),)),
        ],
        input_output_aliases={} if carried is None else {2: 0},
        compiler_params=pltpu.CompilerParams(vmem_limit_bytes=60 * MIB),
    )(left_sizes, right_sizes, *others)


def together(*values):
    return lax.optimization_barrier(values)


def local(wavefunction, left_env, right_env, left_sizes, right_sizes):
    sectors, ranks = lax.axis_size("blk"), lax.axis_size("mpo")
    own_w, left_dim, _ = left_env.shape
    rows = left_dim // ranks
    spots = [(y, x, c) for y in range(SIDE) for x in range(SIDE) for c in range(2)]

    def step(second, by):
        pairs = []
        for y, x, c in spots:
            along_x = (c == 0) != second
            to = place(y, x + by, c) if along_x else place(y + by, x, c)
            pairs.append((place(y, x, c), to))
        return pairs

    def near_step(block, by):
        return lax.ppermute(block, "blk", step(False, by))

    def far_step(block, by):
        return lax.ppermute(block, "blk", step(True, by))

    def swap(block):
        return lax.ppermute(block, "blk", [(i, i ^ 1) for i in range(sectors)])

    def up(block):
        return lax.ppermute(block, "mpo", [(z, (z + 1) % ranks) for z in range(ranks)])

    def down(block):
        return lax.ppermute(block, "mpo", [(z, (z - 1) % ranks) for z in range(ranks)])

    by_right = split(wavefunction, sectors)
    left_env, by_right = together(left_env, by_right)
    psi = lax.all_to_all(by_right, "blk", 0, 0)

    pieces = left_env.reshape(own_w, ranks, rows, left_dim).transpose(1, 0, 2, 3)
    own = lax.all_to_all(pieces, "mpo", 0, 0)
    below, above = near_step(own, 1), near_step(own, -1)
    up1, down1 = up(right_env), down(right_env)
    below, above, up1, down1 = together(below, above, up1, down1)

    two = near_step(below, 1)
    up2, down2 = up(up1), down(down1)
    two, up2, down2 = together(two, up2, down2)

    line = stack(own, below, above, two)
    line_below, line_above = far_step(line, 1), far_step(line, -1)
    line_other = swap(line)
    up3, down3 = up(up2), down(down2)
    line_below, line_above, up3, down3 = together(line_below, line_above, up3, down3)

    half = SIDE // 2
    far_below = far_step(line_below[:half], 1)
    far_above = far_step(line_above[half:], -1)
    below_other, above_other = swap(line_below), swap(line_above)
    up4 = up(up3)
    far_below_other, far_above_other = swap(far_below), swap(far_above)

    rights = (right_env, down1, down2, down3, up4, up3, up2, up1)
    groups = tuple(((False, far, 0), (True, far, 0)) for far in (0, SIDE - 1, 1))
    blocks = (line, line_other, line_below, below_other, line_above, above_other)
    begun = apply(groups, blocks, psi, rights, left_sizes, right_sizes, None)
    groups = (tuple((s, 2, first) for s in (False, True) for first in (0, half)),)
    blocks = (far_below, far_above, far_below_other, far_above_other)
    return apply(groups, blocks, psi, rights, left_sizes, right_sizes, begun)


def solution(mesh):
    placed = (P("blk", None), P("mpo", "blk", None), P("mpo", "blk", None), P(), P())
    return jax.shard_map(
        local, mesh=mesh, in_specs=placed, out_specs=P(None, "mpo", "blk"), check_vma=False
    )
```

```python
import functools

import jax
import jax.numpy as jnp
from jax import lax
from jax.experimental import pallas as pl
from jax.experimental.pallas import tpu as pltpu
from jax.sharding import PartitionSpec as P

MIB = 1024 * 1024
SIDE = 4
OFFSETS = (0, SIDE - 1, 1, 2)
ANYWHERE = pl.BlockSpec(memory_space=pl.ANY)
SMEM = pl.BlockSpec(memory_space=pltpu.SMEM)
VMEM = pl.BlockSpec(memory_space=pltpu.VMEM)


def place(y, x, core):
    return ((y % SIDE) * SIDE + x % SIDE) * 2 + core


def stack_kernel(*refs):
    inputs, out, sems = refs[:-2], refs[-2], refs[-1]
    copies = [pltpu.make_async_copy(ref, out.at[i], sems.at[i]) for i, ref in enumerate(inputs)]
    for copy in copies:
        copy.start()
    for copy in copies:
        copy.wait()


def stack(*pieces):
    return pl.pallas_call(
        stack_kernel,
        out_shape=jax.ShapeDtypeStruct((len(pieces), *pieces[0].shape), pieces[0].dtype),
        in_specs=[ANYWHERE] * len(pieces),
        out_specs=ANYWHERE,
        scratch_shapes=[pltpu.SemaphoreType.DMA((len(pieces),))],
        compiler_params=pltpu.CompilerParams(vmem_limit_bytes=MIB),
    )(*pieces)


def coordinates():
    sector, rank = lax.axis_index("blk"), lax.axis_index("mpo")
    return sector, rank, sector % 2, sector // 2 % SIDE, sector // (2 * SIDE)


def right_sector(rank, core, which):
    y = ((rank // SIDE + core) & 1) + 2 * which
    return (y * SIDE + rank % SIDE) * 2 + core


def cut_kernel(left_sizes, right_sizes, psi_ref, keep_ref, give_ref, held, sems):
    sector, rank, core, _, _ = coordinates()
    _, left_dim, right_dim = keep_ref.shape
    wanted = [right_sector(rank, c, i) for c in (core, 1 - core) for i in range(2)]
    copies = []
    for i, b in enumerate(wanted):
        first = pl.multiple_of(b * right_dim, right_dim)
        copies.append(pltpu.make_async_copy(psi_ref.at[:, pl.ds(first, right_dim)], held.at[i], sems.at[i]))
    for copy in copies:
        copy.start()
    row = lax.broadcasted_iota(jnp.int32, (left_dim, right_dim), 0)
    col = lax.broadcasted_iota(jnp.int32, (left_dim, right_dim), 1)
    own_left = left_sizes[sector]
    for i, b in enumerate(wanted):
        copies[i].wait()
        inside = jnp.logical_and(row < own_left, col < right_sizes[b])
        block = jnp.where(inside, held[i].astype(jnp.float32), 0.0).astype(held.dtype)
        (keep_ref if i < 2 else give_ref)[i % 2] = block


def cut(wavefunction, left_sizes, right_sizes):
    left_dim, columns = wavefunction.shape
    block = (left_dim, columns // right_sizes.shape[0])
    shape = jax.ShapeDtypeStruct((2, *block), wavefunction.dtype)
    return pl.pallas_call(
        cut_kernel,
        out_shape=(shape, shape),
        in_specs=[SMEM, SMEM, ANYWHERE],
        out_specs=(VMEM, VMEM),
        scratch_shapes=[pltpu.VMEM((4, *block), wavefunction.dtype), pltpu.SemaphoreType.DMA((4,))],
        compiler_params=pltpu.CompilerParams(vmem_limit_bytes=60 * MIB),
    )(left_sizes, right_sizes, wavefunction)


def contract_kernel(left_ref, other_ref, psi_ref, other_psi_ref, out_ref):
    for w in range(2):
        for a, (left, psi) in enumerate(((left_ref, psi_ref), (other_ref, other_psi_ref))):
            for b in range(2):
                product = jnp.dot(left[0, w], psi[b], preferred_element_type=jnp.float32)
                out_ref[0, b, w, a] = product.astype(out_ref.dtype)


def contract(lefts, others, psi, other_psi):
    ranks, _, left_dim, _ = lefts.shape
    right_dim = psi.shape[2]
    left = pl.BlockSpec((1, *lefts.shape[1:]), lambda i: (i, 0, 0, 0))
    whole = pl.BlockSpec(psi.shape, lambda i: (0, 0, 0))
    block = (2, 2, 2, left_dim, right_dim)
    return pl.pallas_call(
        contract_kernel,
        out_shape=jax.ShapeDtypeStruct((ranks, *block), psi.dtype),
        grid=(ranks,),
        in_specs=[left, left, whole, whole],
        out_specs=pl.BlockSpec((1, *block), lambda i: (i, 0, 0, 0, 0, 0)),
        compiler_params=pltpu.CompilerParams(vmem_limit_bytes=60 * MIB),
    )(lefts, others, psi, other_psi)


def add_shards(pieces, refs, products, total, held, factors, sems, more):
    _, rank, core, x0, y0 = coordinates()
    ranks, _, _, _, left_dim, right_dim = products.shape
    shards, at = [], 0
    copies = []
    for ref, (far, first) in zip(refs, pieces):
        for k in range(ref.shape[0]):
            near = OFFSETS[first + k]
            y = jnp.where(core == 0, y0 + far, y0 + near) & (SIDE - 1)
            x = jnp.where(core == 0, x0 + near, x0 + far) & (SIDE - 1)
            which, pair = y // 2, x + SIDE * (y & 1)
            source = products.at[(pair - rank) & (ranks - 1), which]
            copies.append(pltpu.make_async_copy(source, factors.at[at], sems.at[2 * at]))
            copies.append(pltpu.make_async_copy(ref.at[k], held.at[at], sems.at[2 * at + 1]))
            shards.append(which)
            at += 1
    for copy in copies + more:
        copy.start()
    if not more:
        total[...] = jnp.zeros_like(total)
    for copy in more:
        copy.wait()
    for i, which in enumerate(shards):
        copies[2 * i].wait()
        copies[2 * i + 1].wait()
        term = None
        for w in range(2):
            product = factors[i, w].reshape(2 * left_dim, right_dim)
            part = jnp.dot(product, held[i, w], preferred_element_type=jnp.float32)
            term = part if term is None else term + part
        total[which] += term


def early_kernel(pieces, *refs):
    shards, (products, total, held, factors, sems) = refs[:-5], refs[-5:]
    add_shards(pieces, shards, products, total, held, factors, sems, [])


def late_kernel(pieces, left_sizes, right_sizes, *refs):
    shards, (products, before, out_ref, total, held, factors, sems) = refs[:-7], refs[-7:]
    more = [pltpu.make_async_copy(before, total, sems.at[sems.shape[0] - 1])]
    add_shards(pieces, shards, products, total, held, factors, sems, more)
    sector, rank, core, _, _ = coordinates()
    ranks, _, _, rows, right_dim = out_ref.shape
    left_dim = ranks * rows
    row = lax.broadcasted_iota(jnp.int32, (left_dim, right_dim), 0)
    col = lax.broadcasted_iota(jnp.int32, (left_dim, right_dim), 1)
    for b in range(2):
        own_right = right_sizes[right_sector(rank, core, b)]
        for a, spot in enumerate((core, 1 - core)):
            inside = jnp.logical_and(row < left_sizes[sector - core + spot], col < own_right)
            block = jnp.where(inside, total[b, a * left_dim : (a + 1) * left_dim], 0.0)
            block = block.astype(out_ref.dtype).reshape(ranks, 1, rows, right_dim)
            out_ref[:, b, pl.ds(spot, 1)] = block


def add(kernel, pieces, sizes, shards, products, before, shape, scratch):
    count = sum(shard.shape[0] for shard in shards)
    others = (*shards, products, *before)
    return pl.pallas_call(
        functools.partial(kernel, pieces),
        out_shape=shape,
        in_specs=[SMEM] * len(sizes) + [ANYWHERE] * len(others),
        out_specs=VMEM,
        scratch_shapes=scratch
        + [
            pltpu.VMEM((count, *shards[0].shape[1:]), products.dtype),
            pltpu.VMEM((count, *products.shape[2:]), products.dtype),
            pltpu.SemaphoreType.DMA((2 * count + 1,)),
        ],
        compiler_params=pltpu.CompilerParams(vmem_limit_bytes=60 * MIB),
    )(*sizes, *others)


def order_kernel(in_ref, out_ref, sems):
    _, _, core, _, _ = coordinates()
    copies = []
    for i in range(SIDE * SIDE):
        half, x, which = i // (2 * SIDE), i // 2 % SIDE, i % 2
        chip = (2 * which + (half + core) % 2) * SIDE + x
        copies.append(pltpu.make_async_copy(in_ref.at[i], out_ref.at[chip], sems.at[i]))
    for copy in copies:
        copy.start()
    for copy in copies:
        copy.wait()


def order(blocks):
    return pl.pallas_call(
        order_kernel,
        out_shape=jax.ShapeDtypeStruct(blocks.shape, blocks.dtype),
        in_specs=[VMEM],
        out_specs=ANYWHERE,
        scratch_shapes=[pltpu.SemaphoreType.DMA((blocks.shape[0],))],
        compiler_params=pltpu.CompilerParams(vmem_limit_bytes=8 * MIB),
    )(blocks)


def together(*values):
    return lax.optimization_barrier(values)


def local(wavefunction, left_env, right_env, left_sizes, right_sizes):
    sectors, ranks = lax.axis_size("blk"), lax.axis_size("mpo")
    left_dim, right_dim = left_env.shape[2], right_env.shape[2]
    rows = left_dim // ranks
    spots = [(y, x, c) for y in range(SIDE) for x in range(SIDE) for c in range(2)]

    def step(second, by):
        pairs = []
        for y, x, c in spots:
            along_x = (c == 0) != second
            to = place(y, x + by, c) if along_x else place(y + by, x, c)
            pairs.append((place(y, x, c), to))
        return pairs

    def near_step(block, by):
        return lax.ppermute(block, "blk", step(False, by))

    def far_step(block, by):
        return lax.ppermute(block, "blk", step(True, by))

    def swap(block):
        return lax.ppermute(block, "blk", [(i, i ^ 1) for i in range(sectors)])

    def up(block):
        return lax.ppermute(block, "mpo", [(z, (z + 1) % ranks) for z in range(ranks)])

    def down(block):
        return lax.ppermute(block, "mpo", [(z, (z - 1) % ranks) for z in range(ranks)])

    turn = [
        (
            place(y, x, c) * ranks + z,
            place(2 * (y // 2) + z // SIDE, z % SIDE, c) * ranks + x + SIDE * ((y + c) % 2),
        )
        for y, x, c in spots
        for z in range(ranks)
    ]
    own = lax.ppermute(right_env, ("blk", "mpo"), turn)
    up1, down1 = up(left_env), down(left_env)
    keep, give = cut(wavefunction, left_sizes, right_sizes)
    own, up1, down1, keep, give = together(own, up1, down1, keep, give)

    below, above = near_step(own, 1), near_step(own, -1)
    up2, down2 = up(up1), down(down1)
    got = swap(give)
    below, above, up2, down2 = together(below, above, up2, down2)
    two = near_step(below, 1)
    up3, down3 = up(up2), down(down2)
    two, up3, down3, got = together(two, up3, down3, got)
    line = stack(own, below, above, two)
    line, up3, down3 = together(line, up3, down3)
    line_below, line_above = far_step(line, 1), far_step(line, -1)
    up4 = up(up3)
    lefts = stack(left_env, down1, down2, down3, up4, up3, up2, up1)
    others = swap(lefts)
    line_below, line_above, others = together(line_below, line_above, others)
    half = SIDE // 2
    far_below = far_step(line_below[:half], 1)
    far_above = far_step(line_above[half:], -1)

    products = contract(lefts, others, keep, got)
    total = jax.ShapeDtypeStruct((2, 2 * left_dim, right_dim), jnp.float32)
    pieces = ((0, 0), (SIDE - 1, 0), (1, 0))
    shards = (line, line_below, line_above)
    begun = add(early_kernel, pieces, (), shards, products, (), total, [])
    done = add(
        late_kernel,
        ((2, 0), (2, half)),
        (left_sizes, right_sizes),
        (far_below, far_above),
        products,
        (begun,),
        jax.ShapeDtypeStruct((ranks, 2, 2, rows, right_dim), wavefunction.dtype),
        [pltpu.VMEM(total.shape, total.dtype)],
    )

    by_plane = lax.all_to_all(done, "mpo", 0, 0)
    chips = SIDE * SIDE
    by_plane = by_plane.reshape(chips, 2, rows, right_dim)
    groups = [
        [place(2 * i + (g // SIDE + c) % 2, g % SIDE, c) for g in range(ranks) for i in range(2)]
        for c in range(2)
    ]
    out = order(lax.all_to_all(by_plane, "blk", 0, 0, axis_index_groups=groups))
    return out.reshape(sectors, rows, right_dim)


def solution(mesh):
    placed = (P("blk", None), P("mpo", "blk", None), P("mpo", "blk", None), P(), P())
    return jax.shard_map(
        local, mesh=mesh, in_specs=placed, out_specs=P(None, "mpo", "blk"), check_vma=False
    )
```

```python
import functools

import jax
import jax.numpy as jnp
from jax import lax
from jax.experimental import pallas as pl
from jax.experimental.pallas import tpu as pltpu
from jax.sharding import PartitionSpec as P

MIB = 1024 * 1024
SIDE = 4
OFFSETS = (0, SIDE - 1, 1, 2)
ANYWHERE = pl.BlockSpec(memory_space=pl.ANY)
SMEM = pl.BlockSpec(memory_space=pltpu.SMEM)
VMEM = pl.BlockSpec(memory_space=pltpu.VMEM)


def place(y, x, core):
    return ((y % SIDE) * SIDE + x % SIDE) * 2 + core


def stack_kernel(*refs):
    inputs, out, sems = refs[:-2], refs[-2], refs[-1]
    copies = [pltpu.make_async_copy(ref, out.at[i], sems.at[i]) for i, ref in enumerate(inputs)]
    for copy in copies:
        copy.start()
    for copy in copies:
        copy.wait()


def stack(*pieces):
    return pl.pallas_call(
        stack_kernel,
        out_shape=jax.ShapeDtypeStruct((len(pieces), *pieces[0].shape), pieces[0].dtype),
        in_specs=[ANYWHERE] * len(pieces),
        out_specs=ANYWHERE,
        scratch_shapes=[pltpu.SemaphoreType.DMA((len(pieces),))],
        compiler_params=pltpu.CompilerParams(vmem_limit_bytes=MIB),
    )(*pieces)


def coordinates():
    sector, rank = lax.axis_index("blk"), lax.axis_index("mpo")
    return sector, rank, sector % 2, sector // 2 % SIDE, sector // (2 * SIDE)


def right_sector(rank, core, which):
    y = ((rank // SIDE + core) & 1) + 2 * which
    return (y * SIDE + rank % SIDE) * 2 + core


def cut_kernel(left_sizes, right_sizes, psi_ref, keep_ref, give_ref, held, sems):
    sector, rank, core, _, _ = coordinates()
    _, left_dim, right_dim = keep_ref.shape
    wanted = [right_sector(rank, c, i) for c in (core, 1 - core) for i in range(2)]
    copies = []
    for i, b in enumerate(wanted):
        first = pl.multiple_of(b * right_dim, right_dim)
        copies.append(pltpu.make_async_copy(psi_ref.at[:, pl.ds(first, right_dim)], held.at[i], sems.at[i]))
    for copy in copies:
        copy.start()
    row = lax.broadcasted_iota(jnp.int32, (left_dim, right_dim), 0)
    col = lax.broadcasted_iota(jnp.int32, (left_dim, right_dim), 1)
    own_left = left_sizes[sector]
    for i, b in enumerate(wanted):
        copies[i].wait()
        inside = jnp.logical_and(row < own_left, col < right_sizes[b])
        block = jnp.where(inside, held[i].astype(jnp.float32), 0.0).astype(held.dtype)
        (keep_ref if i < 2 else give_ref)[i % 2] = block


def cut(wavefunction, left_sizes, right_sizes):
    left_dim, columns = wavefunction.shape
    block = (left_dim, columns // right_sizes.shape[0])
    shape = jax.ShapeDtypeStruct((2, *block), wavefunction.dtype)
    return pl.pallas_call(
        cut_kernel,
        out_shape=(shape, shape),
        in_specs=[SMEM, SMEM, ANYWHERE],
        out_specs=(VMEM, VMEM),
        scratch_shapes=[pltpu.VMEM((4, *block), wavefunction.dtype), pltpu.SemaphoreType.DMA((4,))],
        compiler_params=pltpu.CompilerParams(vmem_limit_bytes=60 * MIB),
    )(left_sizes, right_sizes, wavefunction)


def contract_kernel(left_ref, other_ref, psi_ref, other_psi_ref, out_ref):
    _, pair, left_dim, inner = left_ref.shape
    right_dim = psi_ref.shape[2]
    for a, (left, psi) in enumerate(((left_ref, psi_ref), (other_ref, other_psi_ref))):
        block = left[0].reshape(pair * left_dim, inner)
        for b in range(2):
            product = jnp.dot(block, psi[b], preferred_element_type=jnp.float32).astype(out_ref.dtype)
            for w in range(pair):
                columns = slice(w * right_dim, (w + 1) * right_dim)
                out_ref[0, b, a * left_dim : (a + 1) * left_dim, columns] = product[
                    w * left_dim : (w + 1) * left_dim
                ]


def contract(lefts, others, psi, other_psi):
    ranks, pair, left_dim, _ = lefts.shape
    right_dim = psi.shape[2]
    left = pl.BlockSpec((1, *lefts.shape[1:]), lambda i: (i, 0, 0, 0))
    whole = pl.BlockSpec(psi.shape, lambda i: (0, 0, 0))
    block = (2, 2 * left_dim, pair * right_dim)
    return pl.pallas_call(
        contract_kernel,
        out_shape=jax.ShapeDtypeStruct((ranks, *block), psi.dtype),
        grid=(ranks,),
        in_specs=[left, left, whole, whole],
        out_specs=pl.BlockSpec((1, *block), lambda i: (i, 0, 0, 0)),
        compiler_params=pltpu.CompilerParams(vmem_limit_bytes=60 * MIB),
    )(lefts, others, psi, other_psi)


def add_kernel(pieces, left_sizes, right_sizes, *refs):
    shards, (products, out_ref, total, held, factors, sems) = refs[:-6], refs[-6:]
    sector, rank, core, x0, y0 = coordinates()
    ranks, _, _, rows, right_dim = out_ref.shape
    left_dim = ranks * rows
    sectors_of, copies = [], []
    for ref, (far, first) in zip(shards, pieces):
        for k in range(ref.shape[0]):
            at = len(sectors_of)
            near = OFFSETS[first + k]
            y = jnp.where(core == 0, y0 + far, y0 + near) & (SIDE - 1)
            x = jnp.where(core == 0, x0 + near, x0 + far) & (SIDE - 1)
            which, pair = y // 2, x + SIDE * (y & 1)
            source = products.at[(pair - rank) & (ranks - 1), which]
            copies.append(pltpu.make_async_copy(source, factors.at[at], sems.at[2 * at]))
            copies.append(pltpu.make_async_copy(ref.at[k], held.at[at], sems.at[2 * at + 1]))
            sectors_of.append(which)
    for copy in copies:
        copy.start()
    total[...] = jnp.zeros_like(total)
    for i, which in enumerate(sectors_of):
        copies[2 * i].wait()
        copies[2 * i + 1].wait()
        shard = held[i].reshape(factors.shape[2], right_dim)
        total[which] += jnp.dot(factors[i], shard, preferred_element_type=jnp.float32)
    row = lax.broadcasted_iota(jnp.int32, (left_dim, right_dim), 0)
    col = lax.broadcasted_iota(jnp.int32, (left_dim, right_dim), 1)
    for b in range(2):
        own_right = right_sizes[right_sector(rank, core, b)]
        for a, spot in enumerate((core, 1 - core)):
            inside = jnp.logical_and(row < left_sizes[sector - core + spot], col < own_right)
            block = jnp.where(inside, total[b, a * left_dim : (a + 1) * left_dim], 0.0)
            block = block.astype(out_ref.dtype).reshape(ranks, 1, rows, right_dim)
            out_ref[:, b, pl.ds(spot, 1)] = block


def add(pieces, shards, products, left_sizes, right_sizes):
    count = sum(shard.shape[0] for shard in shards)
    dtype, ranks = products.dtype, products.shape[0]
    _, pair, right_inner, right_dim = shards[0].shape
    left_dim = products.shape[2] // 2
    return pl.pallas_call(
        functools.partial(add_kernel, pieces),
        out_shape=jax.ShapeDtypeStruct((ranks, 2, 2, left_dim // ranks, right_dim), dtype),
        in_specs=[SMEM, SMEM] + [ANYWHERE] * (len(shards) + 1),
        out_specs=VMEM,
        scratch_shapes=[
            pltpu.VMEM((2, 2 * left_dim, right_dim), jnp.float32),
            pltpu.VMEM((count, pair, right_inner, right_dim), dtype),
            pltpu.VMEM((count, *products.shape[2:]), dtype),
            pltpu.SemaphoreType.DMA((2 * count,)),
        ],
        compiler_params=pltpu.CompilerParams(vmem_limit_bytes=60 * MIB),
    )(left_sizes, right_sizes, *shards, products)


def order_kernel(in_ref, out_ref, sems):
    _, _, core, _, _ = coordinates()
    copies = []
    for i in range(SIDE * SIDE):
        half, x, which = i // (2 * SIDE), i // 2 % SIDE, i % 2
        chip = (2 * which + (half + core) % 2) * SIDE + x
        copies.append(pltpu.make_async_copy(in_ref.at[i], out_ref.at[chip], sems.at[i]))
    for copy in copies:
        copy.start()
    for copy in copies:
        copy.wait()


def order(blocks):
    return pl.pallas_call(
        order_kernel,
        out_shape=jax.ShapeDtypeStruct(blocks.shape, blocks.dtype),
        in_specs=[VMEM],
        out_specs=ANYWHERE,
        scratch_shapes=[pltpu.SemaphoreType.DMA((blocks.shape[0],))],
        compiler_params=pltpu.CompilerParams(vmem_limit_bytes=8 * MIB),
    )(blocks)


def together(*values):
    return lax.optimization_barrier(values)


def local(wavefunction, left_env, right_env, left_sizes, right_sizes):
    sectors, ranks = lax.axis_size("blk"), lax.axis_size("mpo")
    rows, right_dim = left_env.shape[1] // ranks, right_env.shape[2]
    spots = [(y, x, c) for y in range(SIDE) for x in range(SIDE) for c in range(2)]

    def step(second, by):
        pairs = []
        for y, x, c in spots:
            along_x = (c == 0) != second
            to = place(y, x + by, c) if along_x else place(y + by, x, c)
            pairs.append((place(y, x, c), to))
        return pairs

    def near_step(block, by):
        return lax.ppermute(block, "blk", step(False, by))

    def far_step(block, by):
        return lax.ppermute(block, "blk", step(True, by))

    def swap(block):
        return lax.ppermute(block, "blk", [(i, i ^ 1) for i in range(sectors)])

    def up(block):
        return lax.ppermute(block, "mpo", [(z, (z + 1) % ranks) for z in range(ranks)])

    def down(block):
        return lax.ppermute(block, "mpo", [(z, (z - 1) % ranks) for z in range(ranks)])

    turn = [
        (
            place(y, x, c) * ranks + z,
            place(2 * (y // 2) + z // SIDE, z % SIDE, c) * ranks + x + SIDE * ((y + c) % 2),
        )
        for y, x, c in spots
        for z in range(ranks)
    ]
    own = lax.ppermute(right_env, ("blk", "mpo"), turn)
    up1, down1 = up(left_env), down(left_env)
    keep, give = cut(wavefunction, left_sizes, right_sizes)
    own, keep, give = together(own, keep, give)

    below, above = near_step(own, 1), near_step(own, -1)
    got = swap(give)
    below, above, up1, down1 = together(below, above, up1, down1)
    two = near_step(below, 1)
    line_a = stack(own, below)
    a_below, a_above = far_step(line_a, 1), far_step(line_a, -1)
    up2, down2 = up(up1), down(down1)
    two, up2, down2, got = together(two, up2, down2, got)
    line_b = stack(above, two)
    line_b, a_below, a_above, up2, down2 = together(line_b, a_below, a_above, up2, down2)
    b_below, b_above = far_step(line_b, 1), far_step(line_b, -1)
    up3, down3 = up(up2), down(down2)
    a_two = far_step(a_below, 1)
    up4 = up(up3)
    b_below, b_above, up4 = together(b_below, b_above, up4)
    b_two = far_step(b_above, -1)
    lefts = stack(left_env, down1, down2, down3, up4, up3, up2, up1)
    others = swap(lefts)

    products = contract(lefts, others, keep, got)
    pieces = ((0, 0), (SIDE - 1, 0), (1, 0), (0, 2), (2, 0), (SIDE - 1, 2), (1, 2), (2, 2))
    shards = (line_a, a_below, a_above, line_b, a_two, b_below, b_above, b_two)
    done = add(pieces, shards, products, left_sizes, right_sizes)

    by_plane = lax.all_to_all(done, "mpo", 0, 0)
    chips = SIDE * SIDE
    by_plane = by_plane.reshape(chips, 2, rows, right_dim)
    groups = [
        [place(2 * i + (g // SIDE + c) % 2, g % SIDE, c) for g in range(ranks) for i in range(2)]
        for c in range(2)
    ]
    out = order(lax.all_to_all(by_plane, "blk", 0, 0, axis_index_groups=groups))
    return out.reshape(sectors, rows, right_dim)


def solution(mesh):
    placed = (P("blk", None), P("mpo", "blk", None), P("mpo", "blk", None), P(), P())
    return jax.shard_map(
        local, mesh=mesh, in_specs=placed, out_specs=P(None, "mpo", "blk"), check_vma=False
    )
```

```python
import functools

import jax
import jax.numpy as jnp
from jax import lax
from jax.experimental import pallas as pl
from jax.experimental.pallas import tpu as pltpu
from jax.sharding import PartitionSpec as P

MIB = 1024 * 1024
SIDE = 4
OFFSETS = (0, SIDE - 1, 1, 2)
ANYWHERE = pl.BlockSpec(memory_space=pl.ANY)
SMEM = pl.BlockSpec(memory_space=pltpu.SMEM)
VMEM = pl.BlockSpec(memory_space=pltpu.VMEM)


def place(y, x, core):
    return ((y % SIDE) * SIDE + x % SIDE) * 2 + core


def stack_kernel(*refs):
    inputs, out, sems = refs[:-2], refs[-2], refs[-1]
    copies = [pltpu.make_async_copy(ref, out.at[i], sems.at[i]) for i, ref in enumerate(inputs)]
    for copy in copies:
        copy.start()
    for copy in copies:
        copy.wait()


def stack(*pieces):
    return pl.pallas_call(
        stack_kernel,
        out_shape=jax.ShapeDtypeStruct((len(pieces), *pieces[0].shape), pieces[0].dtype),
        in_specs=[ANYWHERE] * len(pieces),
        out_specs=ANYWHERE,
        scratch_shapes=[pltpu.SemaphoreType.DMA((len(pieces),))],
        compiler_params=pltpu.CompilerParams(vmem_limit_bytes=MIB),
    )(*pieces)


def coordinates():
    sector, rank = lax.axis_index("blk"), lax.axis_index("mpo")
    return sector, rank, sector % 2, sector // 2 % SIDE, sector // (2 * SIDE)


def right_sector(rank, core, which):
    y = ((rank // SIDE + core) & 1) + 2 * which
    return (y * SIDE + rank % SIDE) * 2 + core


def cut_kernel(left_sizes, right_sizes, psi_ref, keep_ref, give_ref, held, sems):
    sector, rank, core, _, _ = coordinates()
    _, left_dim, right_dim = keep_ref.shape
    wanted = [right_sector(rank, c, i) for c in (core, 1 - core) for i in range(2)]
    copies = []
    for i, b in enumerate(wanted):
        first = pl.multiple_of(b * right_dim, right_dim)
        copies.append(pltpu.make_async_copy(psi_ref.at[:, pl.ds(first, right_dim)], held.at[i], sems.at[i]))
    for copy in copies:
        copy.start()
    row = lax.broadcasted_iota(jnp.int32, (left_dim, right_dim), 0)
    col = lax.broadcasted_iota(jnp.int32, (left_dim, right_dim), 1)
    own_left = left_sizes[sector]
    for i, b in enumerate(wanted):
        copies[i].wait()
        inside = jnp.logical_and(row < own_left, col < right_sizes[b])
        block = jnp.where(inside, held[i].astype(jnp.float32), 0.0).astype(held.dtype)
        (keep_ref if i < 2 else give_ref)[i % 2] = block


def cut(wavefunction, left_sizes, right_sizes):
    left_dim, columns = wavefunction.shape
    block = (left_dim, columns // right_sizes.shape[0])
    shape = jax.ShapeDtypeStruct((2, *block), wavefunction.dtype)
    return pl.pallas_call(
        cut_kernel,
        out_shape=(shape, shape),
        in_specs=[SMEM, SMEM, ANYWHERE],
        out_specs=(VMEM, VMEM),
        scratch_shapes=[pltpu.VMEM((4, *block), wavefunction.dtype), pltpu.SemaphoreType.DMA((4,))],
        compiler_params=pltpu.CompilerParams(vmem_limit_bytes=60 * MIB),
    )(left_sizes, right_sizes, wavefunction)


def apply_kernel(pieces, left_sizes, right_sizes, *refs):
    ins, (out_ref, total, held, left_held, psi_held, middle, sems) = refs[:-7], refs[-7:]
    shards, lefts, psis = ins[: len(pieces)], ins[len(pieces) : -2], ins[-2:]
    sector, rank, core, x0, y0 = coordinates()
    ranks, _, _, rows, right_dim = out_ref.shape
    left_dim = ranks * rows
    first = [pltpu.make_async_copy(psis[a], psi_held.at[a], sems.at[a]) for a in range(2)]
    first += [pltpu.make_async_copy(lefts[a], left_held.at[a], sems.at[2 + a]) for a in range(2)]
    coming = [pltpu.make_async_copy(r, held.at[i], sems.at[4 + i]) for i, r in enumerate(shards)]
    for copy in first + coming:
        copy.start()
    total[...] = jnp.zeros_like(total)
    for copy in first:
        copy.wait()
    for i, (far, start) in enumerate(pieces):
        coming[i].wait()
        for k in range(held.shape[1]):
            near = OFFSETS[start + k]
            y = jnp.where(core == 0, y0 + far, y0 + near) & (SIDE - 1)
            x = jnp.where(core == 0, x0 + near, x0 + far) & (SIDE - 1)
            which, pair = y // 2, (x + SIDE * (y & 1) - rank) & (ranks - 1)
            for a in range(2):
                block = left_held[a, pair].reshape(2 * left_dim, left_dim)
                product = jnp.dot(block, psi_held[a, which], preferred_element_type=jnp.float32)
                product = product.astype(middle.dtype)
                for w in range(2):
                    middle[k % 2, a * left_dim : (a + 1) * left_dim, w * right_dim : (w + 1) * right_dim] = (
                        product[w * left_dim : (w + 1) * left_dim]
                    )
            shard = held[i, k].reshape(2 * right_dim, right_dim)
            total[which] += jnp.dot(middle[k % 2], shard, preferred_element_type=jnp.float32)
    row = lax.broadcasted_iota(jnp.int32, (left_dim, right_dim), 0)
    col = lax.broadcasted_iota(jnp.int32, (left_dim, right_dim), 1)
    for b in range(2):
        own_right = right_sizes[right_sector(rank, core, b)]
        for a, spot in enumerate((core, 1 - core)):
            inside = jnp.logical_and(row < left_sizes[sector - core + spot], col < own_right)
            block = jnp.where(inside, total[b, a * left_dim : (a + 1) * left_dim], 0.0)
            block = block.astype(out_ref.dtype).reshape(ranks, 1, rows, right_dim)
            out_ref[:, b, pl.ds(spot, 1)] = block


def apply(pieces, shards, lefts, psis, left_sizes, right_sizes):
    dtype = psis[0].dtype
    ranks, pair, left_dim, _ = lefts[0].shape
    right_dim = psis[0].shape[2]
    others = (*shards, *lefts, *psis)
    return pl.pallas_call(
        functools.partial(apply_kernel, pieces),
        out_shape=jax.ShapeDtypeStruct((ranks, 2, 2, left_dim // ranks, right_dim), dtype),
        in_specs=[SMEM, SMEM] + [ANYWHERE] * len(others),
        out_specs=VMEM,
        scratch_shapes=[
            pltpu.VMEM((2, 2 * left_dim, right_dim), jnp.float32),
            pltpu.VMEM((len(shards), *shards[0].shape), dtype),
            pltpu.VMEM((2, *lefts[0].shape), dtype),
            pltpu.VMEM((2, *psis[0].shape), dtype),
            pltpu.VMEM((2, 2 * left_dim, pair * right_dim), dtype),
            pltpu.SemaphoreType.DMA((len(shards) + 4,)),
        ],
        compiler_params=pltpu.CompilerParams(vmem_limit_bytes=60 * MIB),
    )(left_sizes, right_sizes, *others)


def order_kernel(in_ref, out_ref, sems):
    _, _, core, _, _ = coordinates()
    copies = []
    for i in range(SIDE * SIDE):
        half, x, which = i // (2 * SIDE), i // 2 % SIDE, i % 2
        chip = (2 * which + (half + core) % 2) * SIDE + x
        copies.append(pltpu.make_async_copy(in_ref.at[i], out_ref.at[chip], sems.at[i]))
    for copy in copies:
        copy.start()
    for copy in copies:
        copy.wait()


def order(blocks):
    return pl.pallas_call(
        order_kernel,
        out_shape=jax.ShapeDtypeStruct(blocks.shape, blocks.dtype),
        in_specs=[VMEM],
        out_specs=ANYWHERE,
        scratch_shapes=[pltpu.SemaphoreType.DMA((blocks.shape[0],))],
        compiler_params=pltpu.CompilerParams(vmem_limit_bytes=8 * MIB),
    )(blocks)


def together(*values):
    return lax.optimization_barrier(values)


def local(wavefunction, left_env, right_env, left_sizes, right_sizes):
    sectors, ranks = lax.axis_size("blk"), lax.axis_size("mpo")
    rows, right_dim = left_env.shape[1] // ranks, right_env.shape[2]
    spots = [(y, x, c) for y in range(SIDE) for x in range(SIDE) for c in range(2)]

    def step(second, by):
        pairs = []
        for y, x, c in spots:
            along_x = (c == 0) != second
            to = place(y, x + by, c) if along_x else place(y + by, x, c)
            pairs.append((place(y, x, c), to))
        return pairs

    def near_step(block, by):
        return lax.ppermute(block, "blk", step(False, by))

    def far_step(block, by):
        return lax.ppermute(block, "blk", step(True, by))

    def swap(block):
        return lax.ppermute(block, "blk", [(i, i ^ 1) for i in range(sectors)])

    def up(block):
        return lax.ppermute(block, "mpo", [(z, (z + 1) % ranks) for z in range(ranks)])

    def down(block):
        return lax.ppermute(block, "mpo", [(z, (z - 1) % ranks) for z in range(ranks)])

    turn = [
        (
            place(y, x, c) * ranks + z,
            place(2 * (y // 2) + z // SIDE, z % SIDE, c) * ranks + x + SIDE * ((y + c) % 2),
        )
        for y, x, c in spots
        for z in range(ranks)
    ]
    own = lax.ppermute(right_env, ("blk", "mpo"), turn)
    up1, down1 = up(left_env), down(left_env)
    keep, give = cut(wavefunction, left_sizes, right_sizes)
    own, keep, give = together(own, keep, give)

    below, above, two = near_step(own, 1), near_step(own, -1), near_step(own, 2)
    got = swap(give)
    below, above, up1, down1 = together(below, above, up1, down1)
    line_a = stack(own, below)
    a_below, a_above = far_step(line_a, 1), far_step(line_a, -1)
    up2, down2 = up(up1), down(down1)
    two, got, line_a = together(two, got, line_a)
    line_b = stack(above, two)
    b_below, b_above = far_step(line_b, 1), far_step(line_b, -1)
    a_below, a_above, up2, down2 = together(a_below, a_above, up2, down2)
    a_two = far_step(a_below, 1)
    up3, down3 = up(up2), down(down2)
    b_below, b_above, a_two, up3, down3 = together(b_below, b_above, a_two, up3, down3)
    b_two = far_step(b_above, -1)
    up4 = up(up3)
    lefts = stack(left_env, down1, down2, down3, up4, up3, up2, up1)
    others = swap(lefts)

    pieces = ((0, 0), (SIDE - 1, 0), (1, 0), (0, 2), (SIDE - 1, 2), (1, 2), (2, 0), (2, 2))
    shards = (line_a, a_below, a_above, line_b, b_below, b_above, a_two, b_two)
    done = apply(pieces, shards, (lefts, others), (keep, got), left_sizes, right_sizes)

    by_plane = lax.all_to_all(done, "mpo", 0, 0)
    chips = SIDE * SIDE
    by_plane = by_plane.reshape(chips, 2, rows, right_dim)
    groups = [
        [place(2 * i + (g // SIDE + c) % 2, g % SIDE, c) for g in range(ranks) for i in range(2)]
        for c in range(2)
    ]
    out = order(lax.all_to_all(by_plane, "blk", 0, 0, axis_index_groups=groups))
    return out.reshape(sectors, rows, right_dim)


def solution(mesh):
    placed = (P("blk", None), P("mpo", "blk", None), P("mpo", "blk", None), P(), P())
    return jax.shard_map(
        local, mesh=mesh, in_specs=placed, out_specs=P(None, "mpo", "blk"), check_vma=False
    )
```

```python
import functools

import jax
import jax.numpy as jnp
from jax import lax
from jax.experimental import pallas as pl
from jax.experimental.pallas import tpu as pltpu
from jax.sharding import PartitionSpec as P

MIB = 1024 * 1024
SIDE = 4
OFFSETS = (0, SIDE - 1, 1, 2)
ANYWHERE = pl.BlockSpec(memory_space=pl.ANY)
SMEM = pl.BlockSpec(memory_space=pltpu.SMEM)
VMEM = pl.BlockSpec(memory_space=pltpu.VMEM)


def place(y, x, core):
    return ((y % SIDE) * SIDE + x % SIDE) * 2 + core


def stack_kernel(*refs):
    inputs, out, sems = refs[:-2], refs[-2], refs[-1]
    copies = [pltpu.make_async_copy(ref, out.at[i], sems.at[i]) for i, ref in enumerate(inputs)]
    for copy in copies:
        copy.start()
    for copy in copies:
        copy.wait()


def stack(*pieces):
    return pl.pallas_call(
        stack_kernel,
        out_shape=jax.ShapeDtypeStruct((len(pieces), *pieces[0].shape), pieces[0].dtype),
        in_specs=[ANYWHERE] * len(pieces),
        out_specs=ANYWHERE,
        scratch_shapes=[pltpu.SemaphoreType.DMA((len(pieces),))],
        compiler_params=pltpu.CompilerParams(vmem_limit_bytes=MIB),
    )(*pieces)


def coordinates():
    sector, rank = lax.axis_index("blk"), lax.axis_index("mpo")
    return sector, rank, sector % 2, sector // 2 % SIDE, sector // (2 * SIDE)


def right_sector(rank, core, which):
    y = ((rank // SIDE + core) & 1) + 2 * which
    return (y * SIDE + rank % SIDE) * 2 + core


def cut_kernel(left_sizes, right_sizes, psi_ref, keep_ref, give_ref, held, sems):
    sector, rank, core, _, _ = coordinates()
    _, left_dim, right_dim = keep_ref.shape
    wanted = [right_sector(rank, c, i) for c in (core, 1 - core) for i in range(2)]
    copies = []
    for i, b in enumerate(wanted):
        first = pl.multiple_of(b * right_dim, right_dim)
        copies.append(pltpu.make_async_copy(psi_ref.at[:, pl.ds(first, right_dim)], held.at[i], sems.at[i]))
    for copy in copies:
        copy.start()
    row = lax.broadcasted_iota(jnp.int32, (left_dim, right_dim), 0)
    col = lax.broadcasted_iota(jnp.int32, (left_dim, right_dim), 1)
    own_left = left_sizes[sector]
    for i, b in enumerate(wanted):
        copies[i].wait()
        inside = jnp.logical_and(row < own_left, col < right_sizes[b])
        block = jnp.where(inside, held[i].astype(jnp.float32), 0.0).astype(held.dtype)
        (keep_ref if i < 2 else give_ref)[i % 2] = block


def cut(wavefunction, left_sizes, right_sizes):
    left_dim, columns = wavefunction.shape
    block = (left_dim, columns // right_sizes.shape[0])
    shape = jax.ShapeDtypeStruct((2, *block), wavefunction.dtype)
    return pl.pallas_call(
        cut_kernel,
        out_shape=(shape, shape),
        in_specs=[SMEM, SMEM, ANYWHERE],
        out_specs=(VMEM, VMEM),
        scratch_shapes=[pltpu.VMEM((4, *block), wavefunction.dtype), pltpu.SemaphoreType.DMA((4,))],
        compiler_params=pltpu.CompilerParams(vmem_limit_bytes=60 * MIB),
    )(left_sizes, right_sizes, wavefunction)


def apply_kernel(pieces, left_sizes, right_sizes, *refs):
    ins, (out_ref, total, held, left_held, psi_held, middle, sems) = refs[:-7], refs[-7:]
    shards, (own, other, psi) = ins[: len(pieces)], ins[len(pieces) :]
    sector, rank, core, x0, y0 = coordinates()
    ranks, _, _, rows, right_dim = out_ref.shape
    left_dim = ranks * rows
    first = [
        pltpu.make_async_copy(source, place_in, sems.at[i])
        for i, (source, place_in) in enumerate(
            (
                (psi, psi_held.at[0]),
                (other.at[ranks], psi_held.at[1]),
                (own.at[pl.ds(0, ranks)], left_held.at[0]),
                (other.at[pl.ds(0, ranks)], left_held.at[1]),
            )
        )
    ]
    coming = [pltpu.make_async_copy(r, held.at[i], sems.at[4 + i]) for i, r in enumerate(shards)]
    for copy in first + coming:
        copy.start()
    total[...] = jnp.zeros_like(total)
    for copy in first:
        copy.wait()
    for i, (far, start) in enumerate(pieces):
        coming[i].wait()
        for k in range(held.shape[1]):
            near = OFFSETS[start + k]
            y = jnp.where(core == 0, y0 + far, y0 + near) & (SIDE - 1)
            x = jnp.where(core == 0, x0 + near, x0 + far) & (SIDE - 1)
            which, pair = y // 2, (x + SIDE * (y & 1) - rank) & (ranks - 1)
            for a in range(2):
                block = left_held[a, pair].reshape(2 * left_dim, left_dim)
                product = jnp.dot(block, psi_held[a, which], preferred_element_type=jnp.float32)
                product = product.astype(middle.dtype)
                for w in range(2):
                    middle[k % 2, a * left_dim : (a + 1) * left_dim, w * right_dim : (w + 1) * right_dim] = (
                        product[w * left_dim : (w + 1) * left_dim]
                    )
            shard = held[i, k].reshape(2 * right_dim, right_dim)
            total[which] += jnp.dot(middle[k % 2], shard, preferred_element_type=jnp.float32)
    row = lax.broadcasted_iota(jnp.int32, (left_dim, right_dim), 0)
    col = lax.broadcasted_iota(jnp.int32, (left_dim, right_dim), 1)
    for b in range(2):
        own_right = right_sizes[right_sector(rank, core, b)]
        for a, spot in enumerate((core, 1 - core)):
            inside = jnp.logical_and(row < left_sizes[sector - core + spot], col < own_right)
            block = jnp.where(inside, total[b, a * left_dim : (a + 1) * left_dim], 0.0)
            block = block.astype(out_ref.dtype).reshape(ranks, 1, rows, right_dim)
            out_ref[:, b, pl.ds(spot, 1)] = block


def apply(pieces, shards, own, other, psi, left_sizes, right_sizes):
    dtype = psi.dtype
    slots, pair, left_dim, _ = own.shape
    ranks, right_dim = slots - 1, psi.shape[2]
    others = (*shards, own, other, psi)
    return pl.pallas_call(
        functools.partial(apply_kernel, pieces),
        out_shape=jax.ShapeDtypeStruct((ranks, 2, 2, left_dim // ranks, right_dim), dtype),
        in_specs=[SMEM, SMEM] + [ANYWHERE] * len(others),
        out_specs=VMEM,
        scratch_shapes=[
            pltpu.VMEM((2, 2 * left_dim, right_dim), jnp.float32),
            pltpu.VMEM((len(shards), *shards[0].shape), dtype),
            pltpu.VMEM((2, ranks, *own.shape[1:]), dtype),
            pltpu.VMEM((2, *psi.shape), dtype),
            pltpu.VMEM((2, 2 * left_dim, pair * right_dim), dtype),
            pltpu.SemaphoreType.DMA((len(shards) + 4,)),
        ],
        compiler_params=pltpu.CompilerParams(vmem_limit_bytes=60 * MIB),
    )(left_sizes, right_sizes, *others)


def order_kernel(in_ref, out_ref, sems):
    _, _, core, _, _ = coordinates()
    copies = []
    for i in range(SIDE * SIDE):
        half, x, which = i // (2 * SIDE), i // 2 % SIDE, i % 2
        chip = (2 * which + (half + core) % 2) * SIDE + x
        copies.append(pltpu.make_async_copy(in_ref.at[i], out_ref.at[chip], sems.at[i]))
    for copy in copies:
        copy.start()
    for copy in copies:
        copy.wait()


def order(blocks):
    return pl.pallas_call(
        order_kernel,
        out_shape=jax.ShapeDtypeStruct(blocks.shape, blocks.dtype),
        in_specs=[VMEM],
        out_specs=ANYWHERE,
        scratch_shapes=[pltpu.SemaphoreType.DMA((blocks.shape[0],))],
        compiler_params=pltpu.CompilerParams(vmem_limit_bytes=8 * MIB),
    )(blocks)


def together(*values):
    return lax.optimization_barrier(values)


def local(wavefunction, left_env, right_env, left_sizes, right_sizes):
    sectors, ranks = lax.axis_size("blk"), lax.axis_size("mpo")
    rows, right_dim = left_env.shape[1] // ranks, right_env.shape[2]
    spots = [(y, x, c) for y in range(SIDE) for x in range(SIDE) for c in range(2)]

    def step(second, by):
        pairs = []
        for y, x, c in spots:
            along_x = (c == 0) != second
            to = place(y, x + by, c) if along_x else place(y + by, x, c)
            pairs.append((place(y, x, c), to))
        return pairs

    def near_step(block, by):
        return lax.ppermute(block, "blk", step(False, by))

    def far_step(block, by):
        return lax.ppermute(block, "blk", step(True, by))

    def swap(block):
        return lax.ppermute(block, "blk", [(i, i ^ 1) for i in range(sectors)])

    def up(block):
        return lax.ppermute(block, "mpo", [(z, (z + 1) % ranks) for z in range(ranks)])

    def down(block):
        return lax.ppermute(block, "mpo", [(z, (z - 1) % ranks) for z in range(ranks)])

    turn = [
        (
            place(y, x, c) * ranks + z,
            place(2 * (y // 2) + z // SIDE, z % SIDE, c) * ranks + x + SIDE * ((y + c) % 2),
        )
        for y, x, c in spots
        for z in range(ranks)
    ]
    own = lax.ppermute(right_env, ("blk", "mpo"), turn)
    up1, down1 = up(left_env), down(left_env)
    keep, give = cut(wavefunction, left_sizes, right_sizes)
    own, keep, give = together(own, keep, give)

    below, above, two = near_step(own, 1), near_step(own, -1), near_step(own, 2)
    below, above, two, up1, down1 = together(below, above, two, up1, down1)
    line_a, line_b = stack(own, below), stack(above, two)
    a_below, a_above = far_step(line_a, 1), far_step(line_a, -1)
    b_below, b_above = far_step(line_b, 1), far_step(line_b, -1)
    up2, down2 = up(up1), down(down1)
    up3, down3 = up(up2), down(down2)
    a_below, a_above, b_below, b_above, up3, down3 = together(
        a_below, a_above, b_below, b_above, up3, down3
    )
    a_two, b_two = far_step(a_below, 1), far_step(b_above, -1)
    up4 = up(up3)
    lefts = stack(left_env, down1, down2, down3, up4, up3, up2, up1, give)
    lefts, a_two, b_two = together(lefts, a_two, b_two)
    others = swap(lefts)

    pieces = ((0, 0), (SIDE - 1, 0), (1, 0), (0, 2), (SIDE - 1, 2), (1, 2), (2, 0), (2, 2))
    shards = (line_a, a_below, a_above, line_b, b_below, b_above, a_two, b_two)
    done = apply(pieces, shards, lefts, others, keep, left_sizes, right_sizes)

    by_plane = lax.all_to_all(done, "mpo", 0, 0)
    chips = SIDE * SIDE
    by_plane = by_plane.reshape(chips, 2, rows, right_dim)
    groups = [
        [place(2 * i + (g // SIDE + c) % 2, g % SIDE, c) for g in range(ranks) for i in range(2)]
        for c in range(2)
    ]
    out = order(lax.all_to_all(by_plane, "blk", 0, 0, axis_index_groups=groups))
    return out.reshape(sectors, rows, right_dim)


def solution(mesh):
    placed = (P("blk", None), P("mpo", "blk", None), P("mpo", "blk", None), P(), P())
    return jax.shard_map(
        local, mesh=mesh, in_specs=placed, out_specs=P(None, "mpo", "blk"), check_vma=False
    )
```

```python
import functools

import jax
import jax.numpy as jnp
from jax import lax
from jax.experimental import pallas as pl
from jax.experimental.pallas import tpu as pltpu
from jax.sharding import PartitionSpec as P

MIB = 1024 * 1024
SIDE = 4
OFFSETS = (0, SIDE - 1, 1, 2)
ANYWHERE = pl.BlockSpec(memory_space=pl.ANY)
SMEM = pl.BlockSpec(memory_space=pltpu.SMEM)
VMEM = pl.BlockSpec(memory_space=pltpu.VMEM)


def place(y, x, core):
    return ((y % SIDE) * SIDE + x % SIDE) * 2 + core


def stack_kernel(*refs):
    inputs, out, sems = refs[:-2], refs[-2], refs[-1]
    copies = [pltpu.make_async_copy(ref, out.at[i], sems.at[i]) for i, ref in enumerate(inputs)]
    for copy in copies:
        copy.start()
    for copy in copies:
        copy.wait()


def stack(*pieces):
    return pl.pallas_call(
        stack_kernel,
        out_shape=jax.ShapeDtypeStruct((len(pieces), *pieces[0].shape), pieces[0].dtype),
        in_specs=[ANYWHERE] * len(pieces),
        out_specs=ANYWHERE,
        scratch_shapes=[pltpu.SemaphoreType.DMA((len(pieces),))],
        compiler_params=pltpu.CompilerParams(vmem_limit_bytes=MIB),
    )(*pieces)


def coordinates():
    sector, rank = lax.axis_index("blk"), lax.axis_index("mpo")
    return sector, rank, sector % 2, sector // 2 % SIDE, sector // (2 * SIDE)


def right_sector(rank, core, which):
    y = ((rank // SIDE + core) & 1) + 2 * which
    return (y * SIDE + rank % SIDE) * 2 + core


def cut_kernel(left_sizes, right_sizes, psi_ref, keep_ref, give_ref, held, sems):
    sector, rank, core, _, _ = coordinates()
    _, left_dim, right_dim = keep_ref.shape
    wanted = [right_sector(rank, c, i) for c in (core, 1 - core) for i in range(2)]
    copies = []
    for i, b in enumerate(wanted):
        first = pl.multiple_of(b * right_dim, right_dim)
        copies.append(pltpu.make_async_copy(psi_ref.at[:, pl.ds(first, right_dim)], held.at[i], sems.at[i]))
    for copy in copies:
        copy.start()
    row = lax.broadcasted_iota(jnp.int32, (left_dim, right_dim), 0)
    col = lax.broadcasted_iota(jnp.int32, (left_dim, right_dim), 1)
    own_left = left_sizes[sector]
    for i, b in enumerate(wanted):
        copies[i].wait()
        inside = jnp.logical_and(row < own_left, col < right_sizes[b])
        block = jnp.where(inside, held[i].astype(jnp.float32), 0.0).astype(held.dtype)
        (keep_ref if i < 2 else give_ref)[i % 2] = block


def cut(wavefunction, left_sizes, right_sizes):
    left_dim, columns = wavefunction.shape
    block = (left_dim, columns // right_sizes.shape[0])
    shape = jax.ShapeDtypeStruct((2, *block), wavefunction.dtype)
    return pl.pallas_call(
        cut_kernel,
        out_shape=(shape, shape),
        in_specs=[SMEM, SMEM, ANYWHERE],
        out_specs=(VMEM, VMEM),
        scratch_shapes=[pltpu.VMEM((4, *block), wavefunction.dtype), pltpu.SemaphoreType.DMA((4,))],
        compiler_params=pltpu.CompilerParams(vmem_limit_bytes=60 * MIB),
    )(left_sizes, right_sizes, wavefunction)


def apply_kernel(pieces, left_sizes, right_sizes, *refs):
    ins, (out_ref, total, held, left_held, psi_held, middle, sems) = refs[:-7], refs[-7:]
    shards, (own, other, psi, other_psi) = ins[: len(pieces)], ins[len(pieces) :]
    sector, rank, core, x0, y0 = coordinates()
    ranks, _, _, rows, right_dim = out_ref.shape
    left_dim = ranks * rows
    first = [
        pltpu.make_async_copy(source, place_in, sems.at[i])
        for i, (source, place_in) in enumerate(
            (
                (psi, psi_held.at[0]),
                (other_psi, psi_held.at[1]),
                (own, left_held.at[0]),
                (other, left_held.at[1]),
            )
        )
    ]
    coming = [pltpu.make_async_copy(r, held.at[i], sems.at[4 + i]) for i, r in enumerate(shards)]
    for copy in first + coming:
        copy.start()
    total[...] = jnp.zeros_like(total)
    for copy in first:
        copy.wait()
    for i, (far, start) in enumerate(pieces):
        coming[i].wait()
        for k in range(held.shape[1]):
            near = OFFSETS[start + k]
            y = jnp.where(core == 0, y0 + far, y0 + near) & (SIDE - 1)
            x = jnp.where(core == 0, x0 + near, x0 + far) & (SIDE - 1)
            which, pair = y // 2, x + SIDE * (y & 1)
            for a in range(2):
                block = left_held[a, pair].reshape(2 * left_dim, left_dim)
                product = jnp.dot(block, psi_held[a, which], preferred_element_type=jnp.float32)
                product = product.astype(middle.dtype)
                for w in range(2):
                    middle[k % 2, a * left_dim : (a + 1) * left_dim, w * right_dim : (w + 1) * right_dim] = (
                        product[w * left_dim : (w + 1) * left_dim]
                    )
            shard = held[i, k].reshape(2 * right_dim, right_dim)
            total[which] += jnp.dot(middle[k % 2], shard, preferred_element_type=jnp.float32)
    row = lax.broadcasted_iota(jnp.int32, (left_dim, right_dim), 0)
    col = lax.broadcasted_iota(jnp.int32, (left_dim, right_dim), 1)
    for b in range(2):
        own_right = right_sizes[right_sector(rank, core, b)]
        for a, spot in enumerate((core, 1 - core)):
            inside = jnp.logical_and(row < left_sizes[sector - core + spot], col < own_right)
            block = jnp.where(inside, total[b, a * left_dim : (a + 1) * left_dim], 0.0)
            block = block.astype(out_ref.dtype).reshape(ranks, 1, rows, right_dim)
            out_ref[:, b, pl.ds(spot, 1)] = block


def apply(pieces, shards, own, other, psi, other_psi, left_sizes, right_sizes):
    dtype = psi.dtype
    ranks, pair, left_dim, _ = own.shape
    right_dim = psi.shape[2]
    others = (*shards, own, other, psi, other_psi)
    return pl.pallas_call(
        functools.partial(apply_kernel, pieces),
        out_shape=jax.ShapeDtypeStruct((ranks, 2, 2, left_dim // ranks, right_dim), dtype),
        in_specs=[SMEM, SMEM] + [ANYWHERE] * len(others),
        out_specs=VMEM,
        scratch_shapes=[
            pltpu.VMEM((2, 2 * left_dim, right_dim), jnp.float32),
            pltpu.VMEM((len(shards), *shards[0].shape), dtype),
            pltpu.VMEM((2, ranks, *own.shape[1:]), dtype),
            pltpu.VMEM((2, *psi.shape), dtype),
            pltpu.VMEM((2, 2 * left_dim, pair * right_dim), dtype),
            pltpu.SemaphoreType.DMA((len(shards) + 4,)),
        ],
        compiler_params=pltpu.CompilerParams(vmem_limit_bytes=60 * MIB),
    )(left_sizes, right_sizes, *others)


def order_kernel(in_ref, out_ref, sems):
    _, _, core, _, _ = coordinates()
    copies = []
    for i in range(SIDE * SIDE):
        half, x, which = i // (2 * SIDE), i // 2 % SIDE, i % 2
        chip = (2 * which + (half + core) % 2) * SIDE + x
        copies.append(pltpu.make_async_copy(in_ref.at[i], out_ref.at[chip], sems.at[i]))
    for copy in copies:
        copy.start()
    for copy in copies:
        copy.wait()


def order(blocks):
    return pl.pallas_call(
        order_kernel,
        out_shape=jax.ShapeDtypeStruct(blocks.shape, blocks.dtype),
        in_specs=[VMEM],
        out_specs=ANYWHERE,
        scratch_shapes=[pltpu.SemaphoreType.DMA((blocks.shape[0],))],
        compiler_params=pltpu.CompilerParams(vmem_limit_bytes=8 * MIB),
    )(blocks)


def together(*values):
    return lax.optimization_barrier(values)


def local(wavefunction, left_env, right_env, left_sizes, right_sizes):
    sectors, ranks = lax.axis_size("blk"), lax.axis_size("mpo")
    rows, right_dim = left_env.shape[1] // ranks, right_env.shape[2]
    spots = [(y, x, c) for y in range(SIDE) for x in range(SIDE) for c in range(2)]

    def step(second, by):
        pairs = []
        for y, x, c in spots:
            along_x = (c == 0) != second
            to = place(y, x + by, c) if along_x else place(y + by, x, c)
            pairs.append((place(y, x, c), to))
        return pairs

    def near_step(block, by):
        return lax.ppermute(block, "blk", step(False, by))

    def far_step(block, by):
        return lax.ppermute(block, "blk", step(True, by))

    def swap(block):
        return lax.ppermute(block, "blk", [(i, i ^ 1) for i in range(sectors)])

    turn = [
        (
            place(y, x, c) * ranks + z,
            place(2 * (y // 2) + z // SIDE, z % SIDE, c) * ranks + x + SIDE * ((y + c) % 2),
        )
        for y, x, c in spots
        for z in range(ranks)
    ]
    own = lax.ppermute(right_env, ("blk", "mpo"), turn)
    lefts = lax.all_gather(left_env, "mpo")
    keep, give = cut(wavefunction, left_sizes, right_sizes)
    own, keep, give = together(own, keep, give)

    below, above, two = near_step(own, 1), near_step(own, -1), near_step(own, 2)
    below, above, two = together(below, above, two)
    line_a, line_b = stack(own, below), stack(above, two)
    a_below, a_above = far_step(line_a, 1), far_step(line_a, -1)
    b_below, b_above = far_step(line_b, 1), far_step(line_b, -1)
    got = swap(give)
    a_below, a_above, b_below, b_above, got = together(a_below, a_above, b_below, b_above, got)
    a_two, b_two = far_step(a_below, 1), far_step(b_above, -1)
    lefts, a_two, b_two = together(lefts, a_two, b_two)
    others = swap(lefts)

    pieces = ((0, 0), (SIDE - 1, 0), (1, 0), (0, 2), (SIDE - 1, 2), (1, 2), (2, 0), (2, 2))
    shards = (line_a, a_below, a_above, line_b, b_below, b_above, a_two, b_two)
    done = apply(pieces, shards, lefts, others, keep, got, left_sizes, right_sizes)

    by_plane = lax.all_to_all(done, "mpo", 0, 0)
    chips = SIDE * SIDE
    by_plane = by_plane.reshape(chips, 2, rows, right_dim)
    groups = [
        [place(2 * i + (g // SIDE + c) % 2, g % SIDE, c) for g in range(ranks) for i in range(2)]
        for c in range(2)
    ]
    out = order(lax.all_to_all(by_plane, "blk", 0, 0, axis_index_groups=groups))
    return out.reshape(sectors, rows, right_dim)


def solution(mesh):
    placed = (P("blk", None), P("mpo", "blk", None), P("mpo", "blk", None), P(), P())
    return jax.shard_map(
        local, mesh=mesh, in_specs=placed, out_specs=P(None, "mpo", "blk"), check_vma=False
    )
```

```python
import functools

import jax
import jax.numpy as jnp
from jax import lax
from jax.experimental import pallas as pl
from jax.experimental.pallas import tpu as pltpu
from jax.sharding import PartitionSpec as P

MIB = 1024 * 1024
SIDE = 4
OFFSETS = (0, SIDE - 1, 1, 2)
ANYWHERE = pl.BlockSpec(memory_space=pl.ANY)
SMEM = pl.BlockSpec(memory_space=pltpu.SMEM)
VMEM = pl.BlockSpec(memory_space=pltpu.VMEM)


def place(y, x, core):
    return ((y % SIDE) * SIDE + x % SIDE) * 2 + core


def stack_kernel(*refs):
    inputs, out, sems = refs[:-2], refs[-2], refs[-1]
    copies = [pltpu.make_async_copy(ref, out.at[i], sems.at[i]) for i, ref in enumerate(inputs)]
    for copy in copies:
        copy.start()
    for copy in copies:
        copy.wait()


def stack(*pieces, limit=1):
    return pl.pallas_call(
        stack_kernel,
        out_shape=jax.ShapeDtypeStruct((len(pieces), *pieces[0].shape), pieces[0].dtype),
        in_specs=[ANYWHERE] * len(pieces),
        out_specs=ANYWHERE,
        scratch_shapes=[pltpu.SemaphoreType.DMA((len(pieces),))],
        compiler_params=pltpu.CompilerParams(vmem_limit_bytes=limit * MIB),
    )(*pieces)


def coordinates():
    sector, rank = lax.axis_index("blk"), lax.axis_index("mpo")
    return sector, rank, sector % 2, sector // 2 % SIDE, sector // (2 * SIDE)


def right_sector(rank, core, which):
    y = ((rank // SIDE + core) & 1) + 2 * which
    return (y * SIDE + rank % SIDE) * 2 + core


def cut_kernel(left_sizes, right_sizes, psi_ref, keep_ref, give_ref, held, sems):
    sector, rank, core, _, _ = coordinates()
    _, left_dim, right_dim = keep_ref.shape
    wanted = [right_sector(rank, c, i) for c in (core, 1 - core) for i in range(2)]
    copies = []
    for i, b in enumerate(wanted):
        first = pl.multiple_of(b * right_dim, right_dim)
        copies.append(pltpu.make_async_copy(psi_ref.at[:, pl.ds(first, right_dim)], held.at[i], sems.at[i]))
    for copy in copies:
        copy.start()
    row = lax.broadcasted_iota(jnp.int32, (left_dim, right_dim), 0)
    col = lax.broadcasted_iota(jnp.int32, (left_dim, right_dim), 1)
    own_left = left_sizes[sector]
    for i, b in enumerate(wanted):
        copies[i].wait()
        inside = jnp.logical_and(row < own_left, col < right_sizes[b])
        block = jnp.where(inside, held[i].astype(jnp.float32), 0.0).astype(held.dtype)
        (keep_ref if i < 2 else give_ref)[i % 2] = block


def cut(wavefunction, left_sizes, right_sizes):
    left_dim, columns = wavefunction.shape
    block = (left_dim, columns // right_sizes.shape[0])
    shape = jax.ShapeDtypeStruct((2, *block), wavefunction.dtype)
    return pl.pallas_call(
        cut_kernel,
        out_shape=(shape, shape),
        in_specs=[SMEM, SMEM, ANYWHERE],
        out_specs=(VMEM, VMEM),
        scratch_shapes=[pltpu.VMEM((4, *block), wavefunction.dtype), pltpu.SemaphoreType.DMA((4,))],
        compiler_params=pltpu.CompilerParams(vmem_limit_bytes=60 * MIB),
    )(left_sizes, right_sizes, wavefunction)


def apply_kernel(pieces, left_sizes, right_sizes, *refs):
    ins, (out_ref, total, held, left_held, psi_held, middle, sems) = refs[:-7], refs[-7:]
    shards, (own, other, psi) = ins[: len(pieces)], ins[len(pieces) :]
    sector, rank, core, x0, y0 = coordinates()
    ranks, _, _, rows, right_dim = out_ref.shape
    left_dim = ranks * rows
    first = [
        pltpu.make_async_copy(source, place_in, sems.at[i])
        for i, (source, place_in) in enumerate(
            (
                (psi, psi_held.at[0]),
                (other.at[ranks], psi_held.at[1]),
                (own.at[pl.ds(0, ranks)], left_held.at[0]),
                (other.at[pl.ds(0, ranks)], left_held.at[1]),
            )
        )
    ]
    coming = [pltpu.make_async_copy(r, held.at[i], sems.at[4 + i]) for i, r in enumerate(shards)]
    for copy in first + coming:
        copy.start()
    total[...] = jnp.zeros_like(total)
    some = ranks // 2
    for a in range(2):
        first[a].wait()
        first[2 + a].wait()
        for b in range(2):
            for part in range(0, ranks, some):
                block = left_held[a, part : part + some].reshape(some * 2 * left_dim, left_dim)
                product = jnp.dot(block, psi_held[a, b], preferred_element_type=jnp.float32)
                product = product.astype(middle.dtype).reshape(some, 2, left_dim, right_dim)
                for w in range(2):
                    columns = slice(w * right_dim, (w + 1) * right_dim)
                    middle[b, part : part + some, a * left_dim : (a + 1) * left_dim, columns] = product[:, w]
    for i, (far, start) in enumerate(pieces):
        coming[i].wait()
        for k in range(held.shape[1]):
            near = OFFSETS[start + k]
            y = jnp.where(core == 0, y0 + far, y0 + near) & (SIDE - 1)
            x = jnp.where(core == 0, x0 + near, x0 + far) & (SIDE - 1)
            which, pair = y // 2, (x + SIDE * (y & 1) - rank) & (ranks - 1)
            shard = held[i, k].reshape(2 * right_dim, right_dim)
            total[which] += jnp.dot(middle[which, pair], shard, preferred_element_type=jnp.float32)
    row = lax.broadcasted_iota(jnp.int32, (left_dim, right_dim), 0)
    col = lax.broadcasted_iota(jnp.int32, (left_dim, right_dim), 1)
    for b in range(2):
        own_right = right_sizes[right_sector(rank, core, b)]
        for a, spot in enumerate((core, 1 - core)):
            inside = jnp.logical_and(row < left_sizes[sector - core + spot], col < own_right)
            block = jnp.where(inside, total[b, a * left_dim : (a + 1) * left_dim], 0.0)
            block = block.astype(out_ref.dtype).reshape(ranks, 1, rows, right_dim)
            out_ref[:, b, pl.ds(spot, 1)] = block


def apply(pieces, shards, own, other, psi, left_sizes, right_sizes):
    dtype = psi.dtype
    slots, pair, left_dim, _ = own.shape
    ranks, right_dim = slots - 1, psi.shape[2]
    others = (*shards, own, other, psi)
    return pl.pallas_call(
        functools.partial(apply_kernel, pieces),
        out_shape=jax.ShapeDtypeStruct((ranks, 2, 2, left_dim // ranks, right_dim), dtype),
        in_specs=[SMEM, SMEM] + [ANYWHERE] * len(others),
        out_specs=VMEM,
        scratch_shapes=[
            pltpu.VMEM((2, 2 * left_dim, right_dim), jnp.float32),
            pltpu.VMEM((len(shards), *shards[0].shape), dtype),
            pltpu.VMEM((2, ranks, *own.shape[1:]), dtype),
            pltpu.VMEM((2, *psi.shape), dtype),
            pltpu.VMEM((2, ranks, 2 * left_dim, pair * right_dim), dtype),
            pltpu.SemaphoreType.DMA((len(shards) + 4,)),
        ],
        compiler_params=pltpu.CompilerParams(vmem_limit_bytes=60 * MIB),
    )(left_sizes, right_sizes, *others)


def order_kernel(in_ref, out_ref, sems):
    _, _, core, _, _ = coordinates()
    copies = []
    for i in range(SIDE * SIDE):
        half, x, which = i // (2 * SIDE), i // 2 % SIDE, i % 2
        chip = (2 * which + (half + core) % 2) * SIDE + x
        copies.append(pltpu.make_async_copy(in_ref.at[i], out_ref.at[chip], sems.at[i]))
    for copy in copies:
        copy.start()
    for copy in copies:
        copy.wait()


def order(blocks):
    return pl.pallas_call(
        order_kernel,
        out_shape=jax.ShapeDtypeStruct(blocks.shape, blocks.dtype),
        in_specs=[VMEM],
        out_specs=ANYWHERE,
        scratch_shapes=[pltpu.SemaphoreType.DMA((blocks.shape[0],))],
        compiler_params=pltpu.CompilerParams(vmem_limit_bytes=8 * MIB),
    )(blocks)


def together(*values):
    return lax.optimization_barrier(values)


def local(wavefunction, left_env, right_env, left_sizes, right_sizes):
    sectors, ranks = lax.axis_size("blk"), lax.axis_size("mpo")
    rows, right_dim = left_env.shape[1] // ranks, right_env.shape[2]
    spots = [(y, x, c) for y in range(SIDE) for x in range(SIDE) for c in range(2)]

    def step(second, by):
        pairs = []
        for y, x, c in spots:
            along_x = (c == 0) != second
            to = place(y, x + by, c) if along_x else place(y + by, x, c)
            pairs.append((place(y, x, c), to))
        return pairs

    def near_step(block, by):
        return lax.ppermute(block, "blk", step(False, by))

    def far_step(block, by):
        return lax.ppermute(block, "blk", step(True, by))

    def swap(block):
        return lax.ppermute(block, "blk", [(i, i ^ 1) for i in range(sectors)])

    def up(block):
        return lax.ppermute(block, "mpo", [(z, (z + 1) % ranks) for z in range(ranks)])

    def down(block):
        return lax.ppermute(block, "mpo", [(z, (z - 1) % ranks) for z in range(ranks)])

    turn = [
        (
            place(y, x, c) * ranks + z,
            place(2 * (y // 2) + z // SIDE, z % SIDE, c) * ranks + x + SIDE * ((y + c) % 2),
        )
        for y, x, c in spots
        for z in range(ranks)
    ]
    own = lax.ppermute(right_env, ("blk", "mpo"), turn)
    up1, down1 = up(left_env), down(left_env)
    keep, give = cut(wavefunction, left_sizes, right_sizes)
    up2, down2 = up(up1), down(down1)
    own, keep, give, up2, down2 = together(own, keep, give, up2, down2)

    below, above, two = near_step(own, 1), near_step(own, -1), near_step(own, 2)
    up3, down3 = up(up2), down(down2)
    below, above, two, up3, down3 = together(below, above, two, up3, down3)
    line_a, line_b = stack(own, below), stack(above, two)
    a_below, a_above = far_step(line_a, 1), far_step(line_a, -1)
    b_below, b_above = far_step(line_b, 1), far_step(line_b, -1)
    up4 = up(up3)
    a_below, a_above, b_below, b_above, up4 = together(a_below, a_above, b_below, b_above, up4)
    a_two, b_two = far_step(a_below, 1), far_step(b_above, -1)
    lefts = stack(left_env, down1, down2, down3, up4, up3, up2, up1, give, limit=60)
    others = swap(lefts)

    pieces = ((0, 0), (SIDE - 1, 0), (1, 0), (0, 2), (SIDE - 1, 2), (1, 2), (2, 0), (2, 2))
    shards = (line_a, a_below, a_above, line_b, b_below, b_above, a_two, b_two)
    done = apply(pieces, shards, lefts, others, keep, left_sizes, right_sizes)

    by_plane = lax.all_to_all(done, "mpo", 0, 0)
    chips = SIDE * SIDE
    by_plane = by_plane.reshape(chips, 2, rows, right_dim)
    groups = [
        [place(2 * i + (g // SIDE + c) % 2, g % SIDE, c) for g in range(ranks) for i in range(2)]
        for c in range(2)
    ]
    out = order(lax.all_to_all(by_plane, "blk", 0, 0, axis_index_groups=groups))
    return out.reshape(sectors, rows, right_dim)


def solution(mesh):
    placed = (P("blk", None), P("mpo", "blk", None), P("mpo", "blk", None), P(), P())
    return jax.shard_map(
        local, mesh=mesh, in_specs=placed, out_specs=P(None, "mpo", "blk"), check_vma=False
    )
```

```python
import functools

import jax
import jax.numpy as jnp
from jax import lax
from jax.experimental import pallas as pl
from jax.experimental.pallas import tpu as pltpu
from jax.sharding import PartitionSpec as P

MIB = 1024 * 1024
SIDE = 4
OFFSETS = (0, SIDE - 1, 1, 2)
ANYWHERE = pl.BlockSpec(memory_space=pl.ANY)
SMEM = pl.BlockSpec(memory_space=pltpu.SMEM)
VMEM = pl.BlockSpec(memory_space=pltpu.VMEM)


def place(y, x, core):
    return ((y % SIDE) * SIDE + x % SIDE) * 2 + core


def stack_kernel(*refs):
    inputs, out, sems = refs[:-2], refs[-2], refs[-1]
    copies = [pltpu.make_async_copy(ref, out.at[i], sems.at[i]) for i, ref in enumerate(inputs)]
    for copy in copies:
        copy.start()
    for copy in copies:
        copy.wait()


def stack(*pieces):
    return pl.pallas_call(
        stack_kernel,
        out_shape=jax.ShapeDtypeStruct((len(pieces), *pieces[0].shape), pieces[0].dtype),
        in_specs=[ANYWHERE] * len(pieces),
        out_specs=ANYWHERE,
        scratch_shapes=[pltpu.SemaphoreType.DMA((len(pieces),))],
        compiler_params=pltpu.CompilerParams(vmem_limit_bytes=MIB),
    )(*pieces)


def coordinates():
    sector, rank = lax.axis_index("blk"), lax.axis_index("mpo")
    return sector, rank, sector % 2, sector // 2 % SIDE, sector // (2 * SIDE)


def right_sector(rank, core, which):
    y = ((rank // SIDE + core) & 1) + 2 * which
    return (y * SIDE + rank % SIDE) * 2 + core


def cut_kernel(left_sizes, right_sizes, psi_ref, keep_ref, give_ref, held, sems):
    sector, rank, core, _, _ = coordinates()
    _, left_dim, right_dim = keep_ref.shape
    wanted = [right_sector(rank, c, i) for c in (core, 1 - core) for i in range(2)]
    copies = []
    for i, b in enumerate(wanted):
        first = pl.multiple_of(b * right_dim, right_dim)
        copies.append(pltpu.make_async_copy(psi_ref.at[:, pl.ds(first, right_dim)], held.at[i], sems.at[i]))
    for copy in copies:
        copy.start()
    row = lax.broadcasted_iota(jnp.int32, (left_dim, right_dim), 0)
    col = lax.broadcasted_iota(jnp.int32, (left_dim, right_dim), 1)
    own_left = left_sizes[sector]
    for i, b in enumerate(wanted):
        copies[i].wait()
        inside = jnp.logical_and(row < own_left, col < right_sizes[b])
        block = jnp.where(inside, held[i].astype(jnp.float32), 0.0).astype(held.dtype)
        (keep_ref if i < 2 else give_ref)[i % 2] = block


def cut(wavefunction, left_sizes, right_sizes):
    left_dim, columns = wavefunction.shape
    block = (left_dim, columns // right_sizes.shape[0])
    shape = jax.ShapeDtypeStruct((2, *block), wavefunction.dtype)
    return pl.pallas_call(
        cut_kernel,
        out_shape=(shape, shape),
        in_specs=[SMEM, SMEM, ANYWHERE],
        out_specs=(VMEM, VMEM),
        scratch_shapes=[pltpu.VMEM((4, *block), wavefunction.dtype), pltpu.SemaphoreType.DMA((4,))],
        compiler_params=pltpu.CompilerParams(vmem_limit_bytes=60 * MIB),
    )(left_sizes, right_sizes, wavefunction)


def apply_kernel(pieces, left_sizes, right_sizes, *refs):
    ins, (out_ref, total, held, left_held, psi_held, middle, sems) = refs[:-7], refs[-7:]
    shards, (own, other, psi, other_psi) = ins[: len(pieces)], ins[len(pieces) :]
    sector, rank, core, x0, y0 = coordinates()
    ranks, _, _, rows, right_dim = out_ref.shape
    left_dim = ranks * rows
    first = [
        pltpu.make_async_copy(source, place_in, sems.at[i])
        for i, (source, place_in) in enumerate(
            (
                (psi, psi_held.at[0]),
                (other_psi, psi_held.at[1]),
                (own, left_held.at[0]),
                (other, left_held.at[1]),
            )
        )
    ]
    coming = [pltpu.make_async_copy(r, held.at[i], sems.at[4 + i]) for i, r in enumerate(shards)]
    for copy in first + coming:
        copy.start()
    total[...] = jnp.zeros_like(total)
    some = ranks // 2
    for a in range(2):
        first[a].wait()
        first[2 + a].wait()
        for b in range(2):
            for part in range(0, ranks, some):
                block = left_held[a, part : part + some].reshape(some * 2 * left_dim, left_dim)
                product = jnp.dot(block, psi_held[a, b], preferred_element_type=jnp.float32)
                product = product.astype(middle.dtype).reshape(some, 2, left_dim, right_dim)
                for w in range(2):
                    columns = slice(w * right_dim, (w + 1) * right_dim)
                    middle[b, part : part + some, a * left_dim : (a + 1) * left_dim, columns] = product[:, w]
    for i, (far, start) in enumerate(pieces):
        coming[i].wait()
        for k in range(held.shape[1]):
            near = OFFSETS[start + k]
            y = jnp.where(core == 0, y0 + far, y0 + near) & (SIDE - 1)
            x = jnp.where(core == 0, x0 + near, x0 + far) & (SIDE - 1)
            which, pair = y // 2, x + SIDE * (y & 1)
            shard = held[i, k].reshape(2 * right_dim, right_dim)
            total[which] += jnp.dot(middle[which, pair], shard, preferred_element_type=jnp.float32)
    row = lax.broadcasted_iota(jnp.int32, (left_dim, right_dim), 0)
    col = lax.broadcasted_iota(jnp.int32, (left_dim, right_dim), 1)
    for b in range(2):
        own_right = right_sizes[right_sector(rank, core, b)]
        for a, spot in enumerate((core, 1 - core)):
            inside = jnp.logical_and(row < left_sizes[sector - core + spot], col < own_right)
            block = jnp.where(inside, total[b, a * left_dim : (a + 1) * left_dim], 0.0)
            block = block.astype(out_ref.dtype).reshape(ranks, 1, rows, right_dim)
            out_ref[:, b, pl.ds(spot, 1)] = block


def apply(pieces, shards, own, other, psi, other_psi, left_sizes, right_sizes):
    dtype = psi.dtype
    ranks, pair, left_dim, _ = own.shape
    right_dim = psi.shape[2]
    others = (*shards, own, other, psi, other_psi)
    return pl.pallas_call(
        functools.partial(apply_kernel, pieces),
        out_shape=jax.ShapeDtypeStruct((ranks, 2, 2, left_dim // ranks, right_dim), dtype),
        in_specs=[SMEM, SMEM] + [ANYWHERE] * len(others),
        out_specs=VMEM,
        scratch_shapes=[
            pltpu.VMEM((2, 2 * left_dim, right_dim), jnp.float32),
            pltpu.VMEM((len(shards), *shards[0].shape), dtype),
            pltpu.VMEM((2, ranks, *own.shape[1:]), dtype),
            pltpu.VMEM((2, *psi.shape), dtype),
            pltpu.VMEM((2, ranks, 2 * left_dim, pair * right_dim), dtype),
            pltpu.SemaphoreType.DMA((len(shards) + 4,)),
        ],
        compiler_params=pltpu.CompilerParams(vmem_limit_bytes=60 * MIB),
    )(left_sizes, right_sizes, *others)


def order_kernel(in_ref, out_ref, sems):
    _, _, core, _, _ = coordinates()
    copies = []
    for i in range(SIDE * SIDE):
        half, x, which = i // (2 * SIDE), i // 2 % SIDE, i % 2
        chip = (2 * which + (half + core) % 2) * SIDE + x
        copies.append(pltpu.make_async_copy(in_ref.at[i], out_ref.at[chip], sems.at[i]))
    for copy in copies:
        copy.start()
    for copy in copies:
        copy.wait()


def order(blocks):
    return pl.pallas_call(
        order_kernel,
        out_shape=jax.ShapeDtypeStruct(blocks.shape, blocks.dtype),
        in_specs=[VMEM],
        out_specs=ANYWHERE,
        scratch_shapes=[pltpu.SemaphoreType.DMA((blocks.shape[0],))],
        compiler_params=pltpu.CompilerParams(vmem_limit_bytes=8 * MIB),
    )(blocks)


def together(*values):
    return lax.optimization_barrier(values)


def local(wavefunction, left_env, right_env, left_sizes, right_sizes):
    sectors, ranks = lax.axis_size("blk"), lax.axis_size("mpo")
    rows, right_dim = left_env.shape[1] // ranks, right_env.shape[2]
    spots = [(y, x, c) for y in range(SIDE) for x in range(SIDE) for c in range(2)]

    def step(second, by):
        pairs = []
        for y, x, c in spots:
            along_x = (c == 0) != second
            to = place(y, x + by, c) if along_x else place(y + by, x, c)
            pairs.append((place(y, x, c), to))
        return pairs

    def near_step(block, by):
        return lax.ppermute(block, "blk", step(False, by))

    def far_step(block, by):
        return lax.ppermute(block, "blk", step(True, by))

    def swap(block):
        return lax.ppermute(block, "blk", [(i, i ^ 1) for i in range(sectors)])

    turn = [
        (
            place(y, x, c) * ranks + z,
            place(2 * (y // 2) + z // SIDE, z % SIDE, c) * ranks + x + SIDE * ((y + c) % 2),
        )
        for y, x, c in spots
        for z in range(ranks)
    ]
    own = lax.ppermute(right_env, ("blk", "mpo"), turn)
    lefts = lax.all_gather(left_env, "mpo")
    keep, give = cut(wavefunction, left_sizes, right_sizes)
    got = swap(give)
    own, keep, got = together(own, keep, got)

    below, above, two = near_step(own, 1), near_step(own, -1), near_step(own, 2)
    below, above, two = together(below, above, two)
    line_a, line_b = stack(own, below), stack(above, two)
    a_below, a_above = far_step(line_a, 1), far_step(line_a, -1)
    b_below, b_above = far_step(line_b, 1), far_step(line_b, -1)
    a_below, a_above, b_below, b_above, lefts = together(a_below, a_above, b_below, b_above, lefts)
    a_two, b_two = far_step(a_below, 1), far_step(b_above, -1)
    others = swap(lefts)

    pieces = ((0, 0), (SIDE - 1, 0), (1, 0), (0, 2), (SIDE - 1, 2), (1, 2), (2, 0), (2, 2))
    shards = (line_a, a_below, a_above, line_b, b_below, b_above, a_two, b_two)
    done = apply(pieces, shards, lefts, others, keep, got, left_sizes, right_sizes)

    by_plane = lax.all_to_all(done, "mpo", 0, 0)
    chips = SIDE * SIDE
    by_plane = by_plane.reshape(chips, 2, rows, right_dim)
    groups = [
        [place(2 * i + (g // SIDE + c) % 2, g % SIDE, c) for g in range(ranks) for i in range(2)]
        for c in range(2)
    ]
    out = order(lax.all_to_all(by_plane, "blk", 0, 0, axis_index_groups=groups))
    return out.reshape(sectors, rows, right_dim)


def solution(mesh):
    placed = (P("blk", None), P("mpo", "blk", None), P("mpo", "blk", None), P(), P())
    return jax.shard_map(
        local, mesh=mesh, in_specs=placed, out_specs=P(None, "mpo", "blk"), check_vma=False
    )
```

```python
import functools

import jax
import jax.numpy as jnp
from jax import lax
from jax.experimental import pallas as pl
from jax.experimental.pallas import tpu as pltpu
from jax.sharding import PartitionSpec as P

MIB = 1024 * 1024
SIDE = 4
OFFSETS = (0, SIDE - 1, 1, 2)
ANYWHERE = pl.BlockSpec(memory_space=pl.ANY)
SMEM = pl.BlockSpec(memory_space=pltpu.SMEM)
VMEM = pl.BlockSpec(memory_space=pltpu.VMEM)


def place(y, x, core):
    return ((y % SIDE) * SIDE + x % SIDE) * 2 + core


def stack_kernel(*refs):
    inputs, out, sems = refs[:-2], refs[-2], refs[-1]
    copies = [pltpu.make_async_copy(ref, out.at[i], sems.at[i]) for i, ref in enumerate(inputs)]
    for copy in copies:
        copy.start()
    for copy in copies:
        copy.wait()


def stack(*pieces):
    return pl.pallas_call(
        stack_kernel,
        out_shape=jax.ShapeDtypeStruct((len(pieces), *pieces[0].shape), pieces[0].dtype),
        in_specs=[ANYWHERE] * len(pieces),
        out_specs=ANYWHERE,
        scratch_shapes=[pltpu.SemaphoreType.DMA((len(pieces),))],
        compiler_params=pltpu.CompilerParams(vmem_limit_bytes=MIB),
    )(*pieces)


def coordinates():
    sector, rank = lax.axis_index("blk"), lax.axis_index("mpo")
    return sector, rank, sector % 2, sector // 2 % SIDE, sector // (2 * SIDE)


def right_sector(rank, core, which):
    y = ((rank // SIDE + core) & 1) + 2 * which
    return (y * SIDE + rank % SIDE) * 2 + core


def cut_kernel(left_sizes, right_sizes, psi_ref, keep_ref, give_ref, held, sems):
    sector, rank, core, _, _ = coordinates()
    _, left_dim, right_dim = keep_ref.shape
    wanted = [right_sector(rank, c, i) for c in (core, 1 - core) for i in range(2)]
    copies = []
    for i, b in enumerate(wanted):
        first = pl.multiple_of(b * right_dim, right_dim)
        copies.append(pltpu.make_async_copy(psi_ref.at[:, pl.ds(first, right_dim)], held.at[i], sems.at[i]))
    for copy in copies:
        copy.start()
    row = lax.broadcasted_iota(jnp.int32, (left_dim, right_dim), 0)
    col = lax.broadcasted_iota(jnp.int32, (left_dim, right_dim), 1)
    own_left = left_sizes[sector]
    for i, b in enumerate(wanted):
        copies[i].wait()
        inside = jnp.logical_and(row < own_left, col < right_sizes[b])
        block = jnp.where(inside, held[i].astype(jnp.float32), 0.0).astype(held.dtype)
        (keep_ref if i < 2 else give_ref)[i % 2] = block


def cut(wavefunction, left_sizes, right_sizes):
    left_dim, columns = wavefunction.shape
    block = (left_dim, columns // right_sizes.shape[0])
    shape = jax.ShapeDtypeStruct((2, *block), wavefunction.dtype)
    return pl.pallas_call(
        cut_kernel,
        out_shape=(shape, shape),
        in_specs=[SMEM, SMEM, ANYWHERE],
        out_specs=(VMEM, VMEM),
        scratch_shapes=[pltpu.VMEM((4, *block), wavefunction.dtype), pltpu.SemaphoreType.DMA((4,))],
        compiler_params=pltpu.CompilerParams(vmem_limit_bytes=60 * MIB),
    )(left_sizes, right_sizes, wavefunction)


def half_kernel(pieces, *refs):
    ins, (out_ref, held, left_held, psi_held, middle, sems) = refs[:-6], refs[-6:]
    shards, (lefts, psi) = ins[: len(pieces)], ins[len(pieces) :]
    _, rank, core, x0, y0 = coordinates()
    ranks, pair, left_dim, inner = left_held.shape
    right_dim = psi_held.shape[2]
    first = [
        pltpu.make_async_copy(psi, psi_held, sems.at[0]),
        pltpu.make_async_copy(lefts.at[pl.ds(0, ranks)], left_held, sems.at[1]),
    ]
    coming = [pltpu.make_async_copy(r, held.at[i], sems.at[2 + i]) for i, r in enumerate(shards)]
    for copy in first + coming:
        copy.start()
    out_ref[...] = jnp.zeros_like(out_ref)
    for copy in first:
        copy.wait()
    some = ranks // 2
    for b in range(2):
        for part in range(0, ranks, some):
            block = left_held[part : part + some].reshape(some * pair * left_dim, inner)
            product = jnp.dot(block, psi_held[b], preferred_element_type=jnp.float32)
            product = product.astype(middle.dtype).reshape(some, pair, left_dim, right_dim)
            for w in range(pair):
                columns = slice(w * right_dim, (w + 1) * right_dim)
                middle[b, part : part + some, :, columns] = product[:, w]
    for i, (far, start) in enumerate(pieces):
        coming[i].wait()
        for k in range(held.shape[1]):
            near = OFFSETS[start + k]
            y = jnp.where(core == 0, y0 + far, y0 + near) & (SIDE - 1)
            x = jnp.where(core == 0, x0 + near, x0 + far) & (SIDE - 1)
            which, at = y // 2, (x + SIDE * (y & 1) - rank) & (ranks - 1)
            shard = held[i, k].reshape(pair * right_dim, right_dim)
            out_ref[which] += jnp.dot(middle[which, at], shard, preferred_element_type=jnp.float32)


def half(pieces, shards, lefts, psi):
    dtype = psi.dtype
    slots, pair, left_dim, inner = lefts.shape
    ranks, right_dim = slots - 1, psi.shape[2]
    return pl.pallas_call(
        functools.partial(half_kernel, pieces),
        out_shape=jax.ShapeDtypeStruct((2, left_dim, right_dim), jnp.float32),
        in_specs=[ANYWHERE] * (len(shards) + 2),
        out_specs=VMEM,
        scratch_shapes=[
            pltpu.VMEM((len(shards), *shards[0].shape), dtype),
            pltpu.VMEM((ranks, pair, left_dim, inner), dtype),
            pltpu.VMEM(psi.shape, dtype),
            pltpu.VMEM((2, ranks, left_dim, pair * right_dim), dtype),
            pltpu.SemaphoreType.DMA((len(shards) + 2,)),
        ],
        compiler_params=pltpu.CompilerParams(vmem_limit_bytes=24 * MIB),
    )(*shards, lefts, psi)


def join_kernel(left_sizes, right_sizes, own_ref, other_ref, out_ref):
    sector, rank, core, _, _ = coordinates()
    ranks, _, _, rows, right_dim = out_ref.shape
    left_dim = ranks * rows
    row = lax.broadcasted_iota(jnp.int32, (left_dim, right_dim), 0)
    col = lax.broadcasted_iota(jnp.int32, (left_dim, right_dim), 1)
    for b in range(2):
        own_right = right_sizes[right_sector(rank, core, b)]
        for total, spot in ((own_ref, core), (other_ref, 1 - core)):
            inside = jnp.logical_and(row < left_sizes[sector - core + spot], col < own_right)
            block = jnp.where(inside, total[b], 0.0)
            block = block.astype(out_ref.dtype).reshape(ranks, 1, rows, right_dim)
            out_ref[:, b, pl.ds(spot, 1)] = block


def join(own, other, left_sizes, right_sizes, ranks, dtype):
    _, left_dim, right_dim = own.shape
    return pl.pallas_call(
        join_kernel,
        out_shape=jax.ShapeDtypeStruct((ranks, 2, 2, left_dim // ranks, right_dim), dtype),
        in_specs=[SMEM, SMEM, VMEM, VMEM],
        out_specs=VMEM,
        compiler_params=pltpu.CompilerParams(vmem_limit_bytes=8 * MIB),
    )(left_sizes, right_sizes, own, other)


def order_kernel(in_ref, out_ref, sems):
    _, _, core, _, _ = coordinates()
    copies = []
    for i in range(SIDE * SIDE):
        half, x, which = i // (2 * SIDE), i // 2 % SIDE, i % 2
        chip = (2 * which + (half + core) % 2) * SIDE + x
        copies.append(pltpu.make_async_copy(in_ref.at[i], out_ref.at[chip], sems.at[i]))
    for copy in copies:
        copy.start()
    for copy in copies:
        copy.wait()


def order(blocks):
    return pl.pallas_call(
        order_kernel,
        out_shape=jax.ShapeDtypeStruct(blocks.shape, blocks.dtype),
        in_specs=[VMEM],
        out_specs=ANYWHERE,
        scratch_shapes=[pltpu.SemaphoreType.DMA((blocks.shape[0],))],
        compiler_params=pltpu.CompilerParams(vmem_limit_bytes=8 * MIB),
    )(blocks)


def together(*values):
    return lax.optimization_barrier(values)


def local(wavefunction, left_env, right_env, left_sizes, right_sizes):
    sectors, ranks = lax.axis_size("blk"), lax.axis_size("mpo")
    rows, right_dim = left_env.shape[1] // ranks, right_env.shape[2]
    spots = [(y, x, c) for y in range(SIDE) for x in range(SIDE) for c in range(2)]

    def step(second, by):
        pairs = []
        for y, x, c in spots:
            along_x = (c == 0) != second
            to = place(y, x + by, c) if along_x else place(y + by, x, c)
            pairs.append((place(y, x, c), to))
        return pairs

    def near_step(block, by):
        return lax.ppermute(block, "blk", step(False, by))

    def far_step(block, by):
        return lax.ppermute(block, "blk", step(True, by))

    def swap(block):
        return lax.ppermute(block, "blk", [(i, i ^ 1) for i in range(sectors)])

    def up(block):
        return lax.ppermute(block, "mpo", [(z, (z + 1) % ranks) for z in range(ranks)])

    def down(block):
        return lax.ppermute(block, "mpo", [(z, (z - 1) % ranks) for z in range(ranks)])

    turn = [
        (
            place(y, x, c) * ranks + z,
            place(2 * (y // 2) + z // SIDE, z % SIDE, c) * ranks + x + SIDE * ((y + c) % 2),
        )
        for y, x, c in spots
        for z in range(ranks)
    ]
    own = lax.ppermute(right_env, ("blk", "mpo"), turn)
    up1, down1 = up(left_env), down(left_env)
    keep, give = cut(wavefunction, left_sizes, right_sizes)
    own, keep, give = together(own, keep, give)

    below, above, two = near_step(own, 1), near_step(own, -1), near_step(own, 2)
    below, above, two, up1, down1 = together(below, above, two, up1, down1)
    line_a, line_b = stack(own, below), stack(above, two)
    a_below, a_above = far_step(line_a, 1), far_step(line_a, -1)
    b_below, b_above = far_step(line_b, 1), far_step(line_b, -1)
    up2, down2 = up(up1), down(down1)
    up3, down3 = up(up2), down(down2)
    a_below, a_above, b_below, b_above, up3, down3 = together(
        a_below, a_above, b_below, b_above, up3, down3
    )
    a_two, b_two = far_step(a_below, 1), far_step(b_above, -1)
    up4 = up(up3)
    lefts = stack(left_env, down1, down2, down3, up4, up3, up2, up1, give)
    lefts, a_two, b_two = together(lefts, a_two, b_two)
    others = swap(lefts)

    pieces = ((0, 0), (SIDE - 1, 0), (1, 0), (0, 2), (SIDE - 1, 2), (1, 2), (2, 0), (2, 2))
    shards = (line_a, a_below, a_above, line_b, b_below, b_above, a_two, b_two)
    mine = half(pieces, shards, lefts, keep)
    theirs = half(pieces, shards, others, others[ranks])
    done = join(mine, theirs, left_sizes, right_sizes, ranks, wavefunction.dtype)

    by_plane = lax.all_to_all(done, "mpo", 0, 0)
    chips = SIDE * SIDE
    by_plane = by_plane.reshape(chips, 2, rows, right_dim)
    groups = [
        [place(2 * i + (g // SIDE + c) % 2, g % SIDE, c) for g in range(ranks) for i in range(2)]
        for c in range(2)
    ]
    out = order(lax.all_to_all(by_plane, "blk", 0, 0, axis_index_groups=groups))
    return out.reshape(sectors, rows, right_dim)


def solution(mesh):
    placed = (P("blk", None), P("mpo", "blk", None), P("mpo", "blk", None), P(), P())
    return jax.shard_map(
        local, mesh=mesh, in_specs=placed, out_specs=P(None, "mpo", "blk"), check_vma=False
    )
```

```python
import functools

import jax
import jax.numpy as jnp
from jax import lax
from jax.experimental import pallas as pl
from jax.experimental.pallas import tpu as pltpu
from jax.sharding import PartitionSpec as P

MIB = 1024 * 1024
SIDE = 4
OFFSETS = (0, SIDE - 1, 1, 2)
ANYWHERE = pl.BlockSpec(memory_space=pl.ANY)
SMEM = pl.BlockSpec(memory_space=pltpu.SMEM)
VMEM = pl.BlockSpec(memory_space=pltpu.VMEM)


def place(y, x, core):
    return ((y % SIDE) * SIDE + x % SIDE) * 2 + core


def stack_kernel(*refs):
    inputs, out, sems = refs[:-2], refs[-2], refs[-1]
    copies = [pltpu.make_async_copy(ref, out.at[i], sems.at[i]) for i, ref in enumerate(inputs)]
    for copy in copies:
        copy.start()
    for copy in copies:
        copy.wait()


def stack(*pieces):
    return pl.pallas_call(
        stack_kernel,
        out_shape=jax.ShapeDtypeStruct((len(pieces), *pieces[0].shape), pieces[0].dtype),
        in_specs=[ANYWHERE] * len(pieces),
        out_specs=ANYWHERE,
        scratch_shapes=[pltpu.SemaphoreType.DMA((len(pieces),))],
        compiler_params=pltpu.CompilerParams(vmem_limit_bytes=MIB),
    )(*pieces)


def coordinates():
    sector, rank = lax.axis_index("blk"), lax.axis_index("mpo")
    return sector, rank, sector % 2, sector // 2 % SIDE, sector // (2 * SIDE)


def right_sector(rank, core, which):
    y = ((rank // SIDE + core) & 1) + 2 * which
    return (y * SIDE + rank % SIDE) * 2 + core


def cut_kernel(left_sizes, right_sizes, psi_ref, keep_ref, give_ref, held, sems):
    sector, rank, core, _, _ = coordinates()
    _, left_dim, right_dim = keep_ref.shape
    wanted = [right_sector(rank, c, i) for c in (core, 1 - core) for i in range(2)]
    copies = []
    for i, b in enumerate(wanted):
        first = pl.multiple_of(b * right_dim, right_dim)
        copies.append(pltpu.make_async_copy(psi_ref.at[:, pl.ds(first, right_dim)], held.at[i], sems.at[i]))
    for copy in copies:
        copy.start()
    row = lax.broadcasted_iota(jnp.int32, (left_dim, right_dim), 0)
    col = lax.broadcasted_iota(jnp.int32, (left_dim, right_dim), 1)
    own_left = left_sizes[sector]
    for i, b in enumerate(wanted):
        copies[i].wait()
        inside = jnp.logical_and(row < own_left, col < right_sizes[b])
        block = jnp.where(inside, held[i].astype(jnp.float32), 0.0).astype(held.dtype)
        (keep_ref if i < 2 else give_ref)[i % 2] = block


def cut(wavefunction, left_sizes, right_sizes):
    left_dim, columns = wavefunction.shape
    block = (left_dim, columns // right_sizes.shape[0])
    shape = jax.ShapeDtypeStruct((2, *block), wavefunction.dtype)
    return pl.pallas_call(
        cut_kernel,
        out_shape=(shape, shape),
        in_specs=[SMEM, SMEM, ANYWHERE],
        out_specs=(VMEM, VMEM),
        scratch_shapes=[pltpu.VMEM((4, *block), wavefunction.dtype), pltpu.SemaphoreType.DMA((4,))],
        compiler_params=pltpu.CompilerParams(vmem_limit_bytes=60 * MIB),
    )(left_sizes, right_sizes, wavefunction)


def half_kernel(pieces, *refs):
    ins, (out_ref, held, left_held, psi_held, middle, sems) = refs[:-6], refs[-6:]
    shards, lefts, psi = ins[: len(pieces)], ins[len(pieces)], ins[len(pieces) + 1 :]
    _, rank, core, x0, y0 = coordinates()
    ranks, pair, left_dim, inner = left_held.shape
    right_dim = psi_held.shape[2]
    first = [
        pltpu.make_async_copy(psi[0] if psi else lefts.at[ranks], psi_held, sems.at[0]),
        pltpu.make_async_copy(lefts.at[pl.ds(0, ranks)], left_held, sems.at[1]),
    ]
    coming = [pltpu.make_async_copy(r, held.at[i], sems.at[2 + i]) for i, r in enumerate(shards)]
    for copy in first + coming:
        copy.start()
    out_ref[...] = jnp.zeros_like(out_ref)
    for copy in first:
        copy.wait()
    some = ranks // 2
    for b in range(2):
        for part in range(0, ranks, some):
            block = left_held[part : part + some].reshape(some * pair * left_dim, inner)
            product = jnp.dot(block, psi_held[b], preferred_element_type=jnp.float32)
            product = product.astype(middle.dtype).reshape(some, pair, left_dim, right_dim)
            for w in range(pair):
                columns = slice(w * right_dim, (w + 1) * right_dim)
                middle[b, part : part + some, :, columns] = product[:, w]
    for i, (far, start) in enumerate(pieces):
        coming[i].wait()
        for k in range(held.shape[1]):
            near = OFFSETS[start + k]
            y = jnp.where(core == 0, y0 + far, y0 + near) & (SIDE - 1)
            x = jnp.where(core == 0, x0 + near, x0 + far) & (SIDE - 1)
            which, at = y // 2, (x + SIDE * (y & 1) - rank) & (ranks - 1)
            shard = held[i, k].reshape(pair * right_dim, right_dim)
            out_ref[which] += jnp.dot(middle[which, at], shard, preferred_element_type=jnp.float32)


def half(pieces, shards, lefts, *psi):
    dtype = lefts.dtype
    slots, pair, left_dim, inner = lefts.shape
    ranks, right_dim = slots - 1, shards[0].shape[-1]
    return pl.pallas_call(
        functools.partial(half_kernel, pieces),
        out_shape=jax.ShapeDtypeStruct((2, left_dim, right_dim), jnp.float32),
        in_specs=[ANYWHERE] * (len(shards) + 1 + len(psi)),
        out_specs=VMEM,
        scratch_shapes=[
            pltpu.VMEM((len(shards), *shards[0].shape), dtype),
            pltpu.VMEM((ranks, pair, left_dim, inner), dtype),
            pltpu.VMEM((2, inner, right_dim), dtype),
            pltpu.VMEM((2, ranks, left_dim, pair * right_dim), dtype),
            pltpu.SemaphoreType.DMA((len(shards) + 2,)),
        ],
        compiler_params=pltpu.CompilerParams(vmem_limit_bytes=24 * MIB),
    )(*shards, lefts, *psi)


def last_kernel(pieces, left_sizes, right_sizes, mine, theirs, *refs):
    ins, (out_ref, held, left_held, psi_held, total, sems) = refs[:-6], refs[-6:]
    shards, (lefts, others, psi) = ins[: len(pieces)], ins[len(pieces) :]
    sector, rank, core, x0, y0 = coordinates()
    ranks, _, _, rows, right_dim = out_ref.shape
    left_dim = ranks * rows
    copies = [
        pltpu.make_async_copy(psi, psi_held.at[0], sems.at[0]),
        pltpu.make_async_copy(others.at[ranks], psi_held.at[1], sems.at[1]),
    ]
    sectors_of = []
    for i, (far, start) in enumerate(pieces):
        copies.append(pltpu.make_async_copy(shards[i], held.at[i], sems.at[len(copies)]))
        for k in range(held.shape[1]):
            near = OFFSETS[start + k]
            y = jnp.where(core == 0, y0 + far, y0 + near) & (SIDE - 1)
            x = jnp.where(core == 0, x0 + near, x0 + far) & (SIDE - 1)
            at = (x + SIDE * (y & 1) - rank) & (ranks - 1)
            for a, source in enumerate((lefts, others)):
                place_in = left_held.at[len(sectors_of), a]
                copies.append(pltpu.make_async_copy(source.at[at], place_in, sems.at[len(copies)]))
            sectors_of.append(y // 2)
    for copy in copies:
        copy.start()
    total[0] = mine[...]
    total[1] = theirs[...]
    for copy in copies:
        copy.wait()
    for i, which in enumerate(sectors_of):
        shard = held[i // held.shape[1], i % held.shape[1]]
        for a in range(2):
            block = left_held[i, a].reshape(2 * left_dim, left_dim)
            product = jnp.dot(block, psi_held[a, which], preferred_element_type=jnp.float32)
            product = product.astype(held.dtype)
            term = jnp.dot(product[:left_dim], shard[0], preferred_element_type=jnp.float32)
            term += jnp.dot(product[left_dim:], shard[1], preferred_element_type=jnp.float32)
            total[a, which] += term
    row = lax.broadcasted_iota(jnp.int32, (left_dim, right_dim), 0)
    col = lax.broadcasted_iota(jnp.int32, (left_dim, right_dim), 1)
    for b in range(2):
        own_right = right_sizes[right_sector(rank, core, b)]
        for a, spot in enumerate((core, 1 - core)):
            inside = jnp.logical_and(row < left_sizes[sector - core + spot], col < own_right)
            block = jnp.where(inside, total[a, b], 0.0)
            block = block.astype(out_ref.dtype).reshape(ranks, 1, rows, right_dim)
            out_ref[:, b, pl.ds(spot, 1)] = block


def last(pieces, shards, mine, theirs, lefts, others, psi, left_sizes, right_sizes):
    dtype = psi.dtype
    slots, pair, left_dim, inner = lefts.shape
    ranks, right_dim = slots - 1, psi.shape[2]
    count = len(shards) * shards[0].shape[0]
    return pl.pallas_call(
        functools.partial(last_kernel, pieces),
        out_shape=jax.ShapeDtypeStruct((ranks, 2, 2, left_dim // ranks, right_dim), dtype),
        in_specs=[SMEM, SMEM, VMEM, VMEM] + [ANYWHERE] * (len(shards) + 3),
        out_specs=VMEM,
        scratch_shapes=[
            pltpu.VMEM((len(shards), *shards[0].shape), dtype),
            pltpu.VMEM((count, 2, pair, left_dim, inner), dtype),
            pltpu.VMEM((2, *psi.shape), dtype),
            pltpu.VMEM((2, *mine.shape), jnp.float32),
            pltpu.SemaphoreType.DMA((2 + len(shards) + 2 * count,)),
        ],
        compiler_params=pltpu.CompilerParams(vmem_limit_bytes=24 * MIB),
    )(left_sizes, right_sizes, mine, theirs, *shards, lefts, others, psi)


def order_kernel(in_ref, out_ref, sems):
    _, _, core, _, _ = coordinates()
    copies = []
    for i in range(SIDE * SIDE):
        half, x, which = i // (2 * SIDE), i // 2 % SIDE, i % 2
        chip = (2 * which + (half + core) % 2) * SIDE + x
        copies.append(pltpu.make_async_copy(in_ref.at[i], out_ref.at[chip], sems.at[i]))
    for copy in copies:
        copy.start()
    for copy in copies:
        copy.wait()


def order(blocks):
    return pl.pallas_call(
        order_kernel,
        out_shape=jax.ShapeDtypeStruct(blocks.shape, blocks.dtype),
        in_specs=[VMEM],
        out_specs=ANYWHERE,
        scratch_shapes=[pltpu.SemaphoreType.DMA((blocks.shape[0],))],
        compiler_params=pltpu.CompilerParams(vmem_limit_bytes=8 * MIB),
    )(blocks)


def together(*values):
    return lax.optimization_barrier(values)


def local(wavefunction, left_env, right_env, left_sizes, right_sizes):
    sectors, ranks = lax.axis_size("blk"), lax.axis_size("mpo")
    rows, right_dim = left_env.shape[1] // ranks, right_env.shape[2]
    spots = [(y, x, c) for y in range(SIDE) for x in range(SIDE) for c in range(2)]

    def step(second, by):
        pairs = []
        for y, x, c in spots:
            along_x = (c == 0) != second
            to = place(y, x + by, c) if along_x else place(y + by, x, c)
            pairs.append((place(y, x, c), to))
        return pairs

    def near_step(block, by):
        return lax.ppermute(block, "blk", step(False, by))

    def far_step(block, by):
        return lax.ppermute(block, "blk", step(True, by))

    def swap(block):
        return lax.ppermute(block, "blk", [(i, i ^ 1) for i in range(sectors)])

    def up(block):
        return lax.ppermute(block, "mpo", [(z, (z + 1) % ranks) for z in range(ranks)])

    def down(block):
        return lax.ppermute(block, "mpo", [(z, (z - 1) % ranks) for z in range(ranks)])

    turn = [
        (
            place(y, x, c) * ranks + z,
            place(2 * (y // 2) + z // SIDE, z % SIDE, c) * ranks + x + SIDE * ((y + c) % 2),
        )
        for y, x, c in spots
        for z in range(ranks)
    ]
    own = lax.ppermute(right_env, ("blk", "mpo"), turn)
    up1, down1 = up(left_env), down(left_env)
    keep, give = cut(wavefunction, left_sizes, right_sizes)
    up2, down2 = up(up1), down(down1)
    own, keep, give, up2, down2 = together(own, keep, give, up2, down2)

    below, above, two = near_step(own, 1), near_step(own, -1), near_step(own, 2)
    up3, down3 = up(up2), down(down2)
    below, above, two, up3, down3 = together(below, above, two, up3, down3)
    line_a, line_b = stack(own, below), stack(above, two)
    a_below, a_above = far_step(line_a, 1), far_step(line_a, -1)
    b_below, b_above = far_step(line_b, 1), far_step(line_b, -1)
    up4 = up(up3)
    lefts = stack(left_env, down1, down2, down3, up4, up3, up2, up1, give)
    a_below, a_above, b_below, b_above, lefts = together(a_below, a_above, b_below, b_above, lefts)
    a_two, b_two = far_step(a_below, 1), far_step(b_above, -1)
    others = swap(lefts)

    early = ((0, 0), (SIDE - 1, 0), (1, 0), (0, 2), (SIDE - 1, 2), (1, 2))
    shards = (line_a, a_below, a_above, line_b, b_below, b_above)
    mine = half(early, shards, lefts, keep)
    theirs = half(early, shards, others)
    late = ((2, 0), (2, 2))
    done = last(late, (a_two, b_two), mine, theirs, lefts, others, keep, left_sizes, right_sizes)

    by_plane = lax.all_to_all(done, "mpo", 0, 0)
    chips = SIDE * SIDE
    by_plane = by_plane.reshape(chips, 2, rows, right_dim)
    groups = [
        [place(2 * i + (g // SIDE + c) % 2, g % SIDE, c) for g in range(ranks) for i in range(2)]
        for c in range(2)
    ]
    out = order(lax.all_to_all(by_plane, "blk", 0, 0, axis_index_groups=groups))
    return out.reshape(sectors, rows, right_dim)


def solution(mesh):
    placed = (P("blk", None), P("mpo", "blk", None), P("mpo", "blk", None), P(), P())
    return jax.shard_map(
        local, mesh=mesh, in_specs=placed, out_specs=P(None, "mpo", "blk"), check_vma=False
    )
```

```python
import functools

import jax
import jax.numpy as jnp
from jax import lax
from jax.experimental import pallas as pl
from jax.experimental.pallas import tpu as pltpu
from jax.sharding import PartitionSpec as P

MIB = 1024 * 1024
SIDE = 4
OFFSETS = (0, SIDE - 1, 1, 2)
ANYWHERE = pl.BlockSpec(memory_space=pl.ANY)
SMEM = pl.BlockSpec(memory_space=pltpu.SMEM)
VMEM = pl.BlockSpec(memory_space=pltpu.VMEM)


def place(y, x, core):
    return ((y % SIDE) * SIDE + x % SIDE) * 2 + core


def stack_kernel(*refs):
    inputs, out, sems = refs[:-2], refs[-2], refs[-1]
    copies = [pltpu.make_async_copy(ref, out.at[i], sems.at[i]) for i, ref in enumerate(inputs)]
    for copy in copies:
        copy.start()
    for copy in copies:
        copy.wait()


def stack(*pieces):
    return pl.pallas_call(
        stack_kernel,
        out_shape=jax.ShapeDtypeStruct((len(pieces), *pieces[0].shape), pieces[0].dtype),
        in_specs=[ANYWHERE] * len(pieces),
        out_specs=ANYWHERE,
        scratch_shapes=[pltpu.SemaphoreType.DMA((len(pieces),))],
        compiler_params=pltpu.CompilerParams(vmem_limit_bytes=MIB),
    )(*pieces)


def coordinates():
    sector, rank = lax.axis_index("blk"), lax.axis_index("mpo")
    return sector, rank, sector % 2, sector // 2 % SIDE, sector // (2 * SIDE)


def right_sector(rank, core, which):
    y = ((rank // SIDE + core) & 1) + 2 * which
    return (y * SIDE + rank % SIDE) * 2 + core


def cut_kernel(left_sizes, right_sizes, psi_ref, keep_ref, give_ref, held, sems):
    sector, rank, core, _, _ = coordinates()
    _, left_dim, right_dim = keep_ref.shape
    wanted = [right_sector(rank, c, i) for c in (core, 1 - core) for i in range(2)]
    copies = []
    for i, b in enumerate(wanted):
        first = pl.multiple_of(b * right_dim, right_dim)
        copies.append(pltpu.make_async_copy(psi_ref.at[:, pl.ds(first, right_dim)], held.at[i], sems.at[i]))
    for copy in copies:
        copy.start()
    row = lax.broadcasted_iota(jnp.int32, (left_dim, right_dim), 0)
    col = lax.broadcasted_iota(jnp.int32, (left_dim, right_dim), 1)
    own_left = left_sizes[sector]
    for i, b in enumerate(wanted):
        copies[i].wait()
        inside = jnp.logical_and(row < own_left, col < right_sizes[b])
        block = jnp.where(inside, held[i].astype(jnp.float32), 0.0).astype(held.dtype)
        (keep_ref if i < 2 else give_ref)[i % 2] = block


def cut(wavefunction, left_sizes, right_sizes):
    left_dim, columns = wavefunction.shape
    block = (left_dim, columns // right_sizes.shape[0])
    shape = jax.ShapeDtypeStruct((2, *block), wavefunction.dtype)
    return pl.pallas_call(
        cut_kernel,
        out_shape=(shape, shape),
        in_specs=[SMEM, SMEM, ANYWHERE],
        out_specs=(VMEM, VMEM),
        scratch_shapes=[pltpu.VMEM((4, *block), wavefunction.dtype), pltpu.SemaphoreType.DMA((4,))],
        compiler_params=pltpu.CompilerParams(vmem_limit_bytes=60 * MIB),
    )(left_sizes, right_sizes, wavefunction)


def half_kernel(pieces, *refs):
    ins, (out_ref, held, left_held, psi_held, middle, sems) = refs[:-6], refs[-6:]
    shards, lefts, psi = ins[: len(pieces)], ins[len(pieces)], ins[len(pieces) + 1 :]
    _, rank, core, x0, y0 = coordinates()
    ranks, pair, left_dim, inner = left_held.shape
    right_dim = psi_held.shape[2]
    first = [
        pltpu.make_async_copy(psi[0] if psi else lefts.at[ranks], psi_held, sems.at[0]),
        pltpu.make_async_copy(lefts.at[pl.ds(0, ranks)], left_held, sems.at[1]),
    ]
    coming = [pltpu.make_async_copy(r, held.at[i], sems.at[2 + i]) for i, r in enumerate(shards)]
    for copy in first + coming:
        copy.start()
    out_ref[...] = jnp.zeros_like(out_ref)
    for copy in first:
        copy.wait()
    some = ranks // 2
    for b in range(2):
        for part in range(0, ranks, some):
            block = left_held[part : part + some].reshape(some * pair * left_dim, inner)
            product = jnp.dot(block, psi_held[b], preferred_element_type=jnp.float32)
            product = product.astype(middle.dtype).reshape(some, pair, left_dim, right_dim)
            for w in range(pair):
                columns = slice(w * right_dim, (w + 1) * right_dim)
                middle[b, part : part + some, :, columns] = product[:, w]
    for i, (far, start) in enumerate(pieces):
        coming[i].wait()
        for k in range(held.shape[1]):
            near = OFFSETS[start + k]
            y = jnp.where(core == 0, y0 + far, y0 + near) & (SIDE - 1)
            x = jnp.where(core == 0, x0 + near, x0 + far) & (SIDE - 1)
            which, at = y // 2, (x + SIDE * (y & 1) - rank) & (ranks - 1)
            shard = held[i, k].reshape(pair * right_dim, right_dim)
            out_ref[which] += jnp.dot(middle[which, at], shard, preferred_element_type=jnp.float32)


def half(pieces, shards, lefts, *psi):
    dtype = lefts.dtype
    slots, pair, left_dim, inner = lefts.shape
    ranks, right_dim = slots - 1, shards[0].shape[-1]
    return pl.pallas_call(
        functools.partial(half_kernel, pieces),
        out_shape=jax.ShapeDtypeStruct((2, left_dim, right_dim), jnp.float32),
        in_specs=[ANYWHERE] * (len(shards) + 1 + len(psi)),
        out_specs=VMEM,
        scratch_shapes=[
            pltpu.VMEM((len(shards), *shards[0].shape), dtype),
            pltpu.VMEM((ranks, pair, left_dim, inner), dtype),
            pltpu.VMEM((2, inner, right_dim), dtype),
            pltpu.VMEM((2, ranks, left_dim, pair * right_dim), dtype),
            pltpu.SemaphoreType.DMA((len(shards) + 2,)),
        ],
        compiler_params=pltpu.CompilerParams(vmem_limit_bytes=24 * MIB),
    )(*shards, lefts, *psi)


def last_kernel(pieces, left_sizes, right_sizes, mine, theirs, *refs):
    ins, (out_ref, held, left_held, psi_held, total, sems) = refs[:-6], refs[-6:]
    shards, (lefts, others, psi) = ins[: len(pieces)], ins[len(pieces) :]
    sector, rank, core, x0, y0 = coordinates()
    ranks, _, _, rows, right_dim = out_ref.shape
    left_dim = ranks * rows
    copies = [
        pltpu.make_async_copy(psi, psi_held.at[0], sems.at[0]),
        pltpu.make_async_copy(others.at[ranks], psi_held.at[1], sems.at[1]),
    ]
    sectors_of = []
    for i, (far, start) in enumerate(pieces):
        copies.append(pltpu.make_async_copy(shards[i], held.at[i], sems.at[len(copies)]))
        for k in range(held.shape[1]):
            near = OFFSETS[start + k]
            y = jnp.where(core == 0, y0 + far, y0 + near) & (SIDE - 1)
            x = jnp.where(core == 0, x0 + near, x0 + far) & (SIDE - 1)
            at = (x + SIDE * (y & 1) - rank) & (ranks - 1)
            for a, source in enumerate((lefts, others)):
                place_in = left_held.at[len(sectors_of), a]
                copies.append(pltpu.make_async_copy(source.at[at], place_in, sems.at[len(copies)]))
            sectors_of.append(y // 2)
    for copy in copies:
        copy.start()
    total[0] = mine[...]
    total[1] = theirs[...]
    for copy in copies:
        copy.wait()
    for i, which in enumerate(sectors_of):
        shard = held[i // held.shape[1], i % held.shape[1]]
        for a in range(2):
            block = left_held[i, a].reshape(2 * left_dim, left_dim)
            product = jnp.dot(block, psi_held[a, which], preferred_element_type=jnp.float32)
            product = product.astype(held.dtype)
            term = jnp.dot(product[:left_dim], shard[0], preferred_element_type=jnp.float32)
            term += jnp.dot(product[left_dim:], shard[1], preferred_element_type=jnp.float32)
            total[a, which] += term
    row = lax.broadcasted_iota(jnp.int32, (left_dim, right_dim), 0)
    col = lax.broadcasted_iota(jnp.int32, (left_dim, right_dim), 1)
    for b in range(2):
        own_right = right_sizes[right_sector(rank, core, b)]
        for a, spot in enumerate((core, 1 - core)):
            inside = jnp.logical_and(row < left_sizes[sector - core + spot], col < own_right)
            block = jnp.where(inside, total[a, b], 0.0)
            block = block.astype(out_ref.dtype).reshape(ranks, 1, rows, right_dim)
            out_ref[:, b, pl.ds(spot, 1)] = block


def last(pieces, shards, mine, theirs, lefts, others, psi, left_sizes, right_sizes):
    dtype = psi.dtype
    slots, pair, left_dim, inner = lefts.shape
    ranks, right_dim = slots - 1, psi.shape[2]
    count = len(shards) * shards[0].shape[0]
    return pl.pallas_call(
        functools.partial(last_kernel, pieces),
        out_shape=jax.ShapeDtypeStruct((ranks, 2, 2, left_dim // ranks, right_dim), dtype),
        in_specs=[SMEM, SMEM, VMEM, VMEM] + [ANYWHERE] * (len(shards) + 3),
        out_specs=VMEM,
        scratch_shapes=[
            pltpu.VMEM((len(shards), *shards[0].shape), dtype),
            pltpu.VMEM((count, 2, pair, left_dim, inner), dtype),
            pltpu.VMEM((2, *psi.shape), dtype),
            pltpu.VMEM((2, *mine.shape), jnp.float32),
            pltpu.SemaphoreType.DMA((2 + len(shards) + 2 * count,)),
        ],
        compiler_params=pltpu.CompilerParams(vmem_limit_bytes=24 * MIB),
    )(left_sizes, right_sizes, mine, theirs, *shards, lefts, others, psi)


def order_kernel(in_ref, out_ref, sems):
    _, _, core, _, _ = coordinates()
    copies = []
    for i in range(SIDE * SIDE):
        half, x, which = i // (2 * SIDE), i // 2 % SIDE, i % 2
        chip = (2 * which + (half + core) % 2) * SIDE + x
        copies.append(pltpu.make_async_copy(in_ref.at[i], out_ref.at[chip], sems.at[i]))
    for copy in copies:
        copy.start()
    for copy in copies:
        copy.wait()


def order(blocks):
    return pl.pallas_call(
        order_kernel,
        out_shape=jax.ShapeDtypeStruct(blocks.shape, blocks.dtype),
        in_specs=[VMEM],
        out_specs=ANYWHERE,
        scratch_shapes=[pltpu.SemaphoreType.DMA((blocks.shape[0],))],
        compiler_params=pltpu.CompilerParams(vmem_limit_bytes=8 * MIB),
    )(blocks)


def together(*values):
    return lax.optimization_barrier(values)


def local(wavefunction, left_env, right_env, left_sizes, right_sizes):
    sectors, ranks = lax.axis_size("blk"), lax.axis_size("mpo")
    rows, right_dim = left_env.shape[1] // ranks, right_env.shape[2]
    spots = [(y, x, c) for y in range(SIDE) for x in range(SIDE) for c in range(2)]

    def step(second, by):
        pairs = []
        for y, x, c in spots:
            along_x = (c == 0) != second
            to = place(y, x + by, c) if along_x else place(y + by, x, c)
            pairs.append((place(y, x, c), to))
        return pairs

    def near_step(block, by):
        return lax.ppermute(block, "blk", step(False, by))

    def far_step(block, by):
        return lax.ppermute(block, "blk", step(True, by))

    def swap(block):
        return lax.ppermute(block, "blk", [(i, i ^ 1) for i in range(sectors)])

    def up(block):
        return lax.ppermute(block, "mpo", [(z, (z + 1) % ranks) for z in range(ranks)])

    def down(block):
        return lax.ppermute(block, "mpo", [(z, (z - 1) % ranks) for z in range(ranks)])

    turn = [
        (
            place(y, x, c) * ranks + z,
            place(2 * (y // 2) + z // SIDE, z % SIDE, c) * ranks + x + SIDE * ((y + c) % 2),
        )
        for y, x, c in spots
        for z in range(ranks)
    ]
    own = lax.ppermute(right_env, ("blk", "mpo"), turn)
    up1, down1 = up(left_env), down(left_env)
    keep, give = cut(wavefunction, left_sizes, right_sizes)
    up2, down2 = up(up1), down(down1)
    own, keep, give = together(own, keep, give)

    below, above, two = near_step(own, 1), near_step(own, -1), near_step(own, 2)
    below, above, two, up2, down2 = together(below, above, two, up2, down2)
    line_a, line_b = stack(own, below), stack(above, two)
    a_below, a_above = far_step(line_a, 1), far_step(line_a, -1)
    b_below, b_above = far_step(line_b, 1), far_step(line_b, -1)
    up3, down3 = up(up2), down(down2)
    up4 = up(up3)
    lefts = stack(left_env, down1, down2, down3, up4, up3, up2, up1, give)
    a_below, a_above, b_below, b_above, lefts = together(a_below, a_above, b_below, b_above, lefts)
    a_two, b_two = far_step(a_below, 1), far_step(b_above, -1)
    others = swap(lefts)

    early = ((0, 0), (SIDE - 1, 0), (1, 0), (0, 2), (SIDE - 1, 2), (1, 2))
    shards = (line_a, a_below, a_above, line_b, b_below, b_above)
    mine = half(early, shards, lefts, keep)
    theirs = half(early, shards, others)
    late = ((2, 0), (2, 2))
    done = last(late, (a_two, b_two), mine, theirs, lefts, others, keep, left_sizes, right_sizes)

    by_plane = lax.all_to_all(done, "mpo", 0, 0)
    chips = SIDE * SIDE
    by_plane = by_plane.reshape(chips, 2, rows, right_dim)
    groups = [
        [place(2 * i + (g // SIDE + c) % 2, g % SIDE, c) for g in range(ranks) for i in range(2)]
        for c in range(2)
    ]
    out = order(lax.all_to_all(by_plane, "blk", 0, 0, axis_index_groups=groups))
    return out.reshape(sectors, rows, right_dim)


def solution(mesh):
    placed = (P("blk", None), P("mpo", "blk", None), P("mpo", "blk", None), P(), P())
    return jax.shard_map(
        local, mesh=mesh, in_specs=placed, out_specs=P(None, "mpo", "blk"), check_vma=False
    )
```

```python
import functools

import jax
import jax.numpy as jnp
from jax import lax
from jax.experimental import pallas as pl
from jax.experimental.pallas import tpu as pltpu
from jax.sharding import PartitionSpec as P

MIB = 1024 * 1024
SIDE = 4
OFFSETS = (0, SIDE - 1, 1, 2)
ANYWHERE = pl.BlockSpec(memory_space=pl.ANY)
SMEM = pl.BlockSpec(memory_space=pltpu.SMEM)
VMEM = pl.BlockSpec(memory_space=pltpu.VMEM)


def place(y, x, core):
    return ((y % SIDE) * SIDE + x % SIDE) * 2 + core


def stack_kernel(*refs):
    inputs, out, sems = refs[:-2], refs[-2], refs[-1]
    copies = [pltpu.make_async_copy(ref, out.at[i], sems.at[i]) for i, ref in enumerate(inputs)]
    for copy in copies:
        copy.start()
    for copy in copies:
        copy.wait()


def stack(*pieces):
    return pl.pallas_call(
        stack_kernel,
        out_shape=jax.ShapeDtypeStruct((len(pieces), *pieces[0].shape), pieces[0].dtype),
        in_specs=[ANYWHERE] * len(pieces),
        out_specs=ANYWHERE,
        scratch_shapes=[pltpu.SemaphoreType.DMA((len(pieces),))],
        compiler_params=pltpu.CompilerParams(vmem_limit_bytes=MIB),
    )(*pieces)


def coordinates():
    sector, rank = lax.axis_index("blk"), lax.axis_index("mpo")
    return sector, rank, sector % 2, sector // 2 % SIDE, sector // (2 * SIDE)


def right_sector(rank, core, which):
    y = ((rank // SIDE + core) & 1) + 2 * which
    return (y * SIDE + rank % SIDE) * 2 + core


def cut_kernel(left_sizes, right_sizes, psi_ref, keep_ref, give_ref, held, sems):
    sector, rank, core, _, _ = coordinates()
    _, left_dim, right_dim = keep_ref.shape
    wanted = [right_sector(rank, c, i) for c in (core, 1 - core) for i in range(2)]
    copies = []
    for i, b in enumerate(wanted):
        first = pl.multiple_of(b * right_dim, right_dim)
        copies.append(pltpu.make_async_copy(psi_ref.at[:, pl.ds(first, right_dim)], held.at[i], sems.at[i]))
    for copy in copies:
        copy.start()
    row = lax.broadcasted_iota(jnp.int32, (left_dim, right_dim), 0)
    col = lax.broadcasted_iota(jnp.int32, (left_dim, right_dim), 1)
    own_left = left_sizes[sector]
    for i, b in enumerate(wanted):
        copies[i].wait()
        inside = jnp.logical_and(row < own_left, col < right_sizes[b])
        block = jnp.where(inside, held[i].astype(jnp.float32), 0.0).astype(held.dtype)
        (keep_ref if i < 2 else give_ref)[i % 2] = block


def cut(wavefunction, left_sizes, right_sizes):
    left_dim, columns = wavefunction.shape
    block = (left_dim, columns // right_sizes.shape[0])
    shape = jax.ShapeDtypeStruct((2, *block), wavefunction.dtype)
    return pl.pallas_call(
        cut_kernel,
        out_shape=(shape, shape),
        in_specs=[SMEM, SMEM, ANYWHERE],
        out_specs=(VMEM, VMEM),
        scratch_shapes=[pltpu.VMEM((4, *block), wavefunction.dtype), pltpu.SemaphoreType.DMA((4,))],
        compiler_params=pltpu.CompilerParams(vmem_limit_bytes=60 * MIB),
    )(left_sizes, right_sizes, wavefunction)


def half_kernel(pieces, *refs):
    ins, (out_ref, held, left_held, psi_held, middle, sems) = refs[:-6], refs[-6:]
    shards, lefts, psi = ins[: len(pieces)], ins[len(pieces)], ins[len(pieces) + 1 :]
    _, rank, core, x0, y0 = coordinates()
    ranks, pair, left_dim, inner = left_held.shape
    right_dim = psi_held.shape[2]
    first = [
        pltpu.make_async_copy(psi[0] if psi else lefts.at[ranks], psi_held, sems.at[0]),
        pltpu.make_async_copy(lefts.at[pl.ds(0, ranks)], left_held, sems.at[1]),
    ]
    coming = [pltpu.make_async_copy(r, held.at[i], sems.at[2 + i]) for i, r in enumerate(shards)]
    for copy in first + coming:
        copy.start()
    out_ref[...] = jnp.zeros_like(out_ref)
    for copy in first:
        copy.wait()
    some = ranks // 2
    for b in range(2):
        for part in range(0, ranks, some):
            block = left_held[part : part + some].reshape(some * pair * left_dim, inner)
            product = jnp.dot(block, psi_held[b], preferred_element_type=jnp.float32)
            product = product.astype(middle.dtype).reshape(some, pair, left_dim, right_dim)
            for w in range(pair):
                columns = slice(w * right_dim, (w + 1) * right_dim)
                middle[b, part : part + some, :, columns] = product[:, w]
    for i, (far, start) in enumerate(pieces):
        coming[i].wait()
        for k in range(held.shape[1]):
            near = OFFSETS[start + k]
            y = jnp.where(core == 0, y0 + far, y0 + near) & (SIDE - 1)
            x = jnp.where(core == 0, x0 + near, x0 + far) & (SIDE - 1)
            which, at = y // 2, (x + SIDE * (y & 1) - rank) & (ranks - 1)
            shard = held[i, k].reshape(pair * right_dim, right_dim)
            out_ref[which] += jnp.dot(middle[which, at], shard, preferred_element_type=jnp.float32)


def half(pieces, shards, lefts, *psi):
    dtype = lefts.dtype
    slots, pair, left_dim, inner = lefts.shape
    ranks, right_dim = slots - 1, shards[0].shape[-1]
    return pl.pallas_call(
        functools.partial(half_kernel, pieces),
        out_shape=jax.ShapeDtypeStruct((2, left_dim, right_dim), jnp.float32),
        in_specs=[ANYWHERE] * (len(shards) + 1 + len(psi)),
        out_specs=VMEM,
        scratch_shapes=[
            pltpu.VMEM((len(shards), *shards[0].shape), dtype),
            pltpu.VMEM((ranks, pair, left_dim, inner), dtype),
            pltpu.VMEM((2, inner, right_dim), dtype),
            pltpu.VMEM((2, ranks, left_dim, pair * right_dim), dtype),
            pltpu.SemaphoreType.DMA((len(shards) + 2,)),
        ],
        compiler_params=pltpu.CompilerParams(vmem_limit_bytes=24 * MIB),
    )(*shards, lefts, *psi)


def last_kernel(pieces, left_sizes, right_sizes, mine, theirs, *refs):
    ins, (out_ref, held, left_held, psi_held, total, sems) = refs[:-6], refs[-6:]
    shards, (lefts, others, psi) = ins[: len(pieces)], ins[len(pieces) :]
    sector, rank, core, x0, y0 = coordinates()
    ranks, _, _, rows, right_dim = out_ref.shape
    left_dim = ranks * rows
    copies = [
        pltpu.make_async_copy(psi, psi_held.at[0], sems.at[0]),
        pltpu.make_async_copy(others.at[ranks], psi_held.at[1], sems.at[1]),
    ]
    sectors_of = []
    for i, (far, start) in enumerate(pieces):
        copies.append(pltpu.make_async_copy(shards[i], held.at[i], sems.at[len(copies)]))
        for k in range(held.shape[1]):
            near = OFFSETS[start + k]
            y = jnp.where(core == 0, y0 + far, y0 + near) & (SIDE - 1)
            x = jnp.where(core == 0, x0 + near, x0 + far) & (SIDE - 1)
            at = (x + SIDE * (y & 1) - rank) & (ranks - 1)
            for a, source in enumerate((lefts, others)):
                place_in = left_held.at[len(sectors_of), a]
                copies.append(pltpu.make_async_copy(source.at[at], place_in, sems.at[len(copies)]))
            sectors_of.append(y // 2)
    for copy in copies:
        copy.start()
    total[0] = mine[...]
    total[1] = theirs[...]
    for copy in copies:
        copy.wait()
    for i, which in enumerate(sectors_of):
        shard = held[i // held.shape[1], i % held.shape[1]]
        for a in range(2):
            block = left_held[i, a].reshape(2 * left_dim, left_dim)
            product = jnp.dot(block, psi_held[a, which], preferred_element_type=jnp.float32)
            product = product.astype(held.dtype)
            term = jnp.dot(product[:left_dim], shard[0], preferred_element_type=jnp.float32)
            term += jnp.dot(product[left_dim:], shard[1], preferred_element_type=jnp.float32)
            total[a, which] += term
    row = lax.broadcasted_iota(jnp.int32, (left_dim, right_dim), 0)
    col = lax.broadcasted_iota(jnp.int32, (left_dim, right_dim), 1)
    for b in range(2):
        own_right = right_sizes[right_sector(rank, core, b)]
        for a, spot in enumerate((core, 1 - core)):
            inside = jnp.logical_and(row < left_sizes[sector - core + spot], col < own_right)
            block = jnp.where(inside, total[a, b], 0.0)
            block = block.astype(out_ref.dtype).reshape(ranks, 1, rows, right_dim)
            out_ref[:, b, pl.ds(spot, 1)] = block


def last(pieces, shards, mine, theirs, lefts, others, psi, left_sizes, right_sizes):
    dtype = psi.dtype
    slots, pair, left_dim, inner = lefts.shape
    ranks, right_dim = slots - 1, psi.shape[2]
    count = len(shards) * shards[0].shape[0]
    return pl.pallas_call(
        functools.partial(last_kernel, pieces),
        out_shape=jax.ShapeDtypeStruct((ranks, 2, 2, left_dim // ranks, right_dim), dtype),
        in_specs=[SMEM, SMEM, VMEM, VMEM] + [ANYWHERE] * (len(shards) + 3),
        out_specs=VMEM,
        scratch_shapes=[
            pltpu.VMEM((len(shards), *shards[0].shape), dtype),
            pltpu.VMEM((count, 2, pair, left_dim, inner), dtype),
            pltpu.VMEM((2, *psi.shape), dtype),
            pltpu.VMEM((2, *mine.shape), jnp.float32),
            pltpu.SemaphoreType.DMA((2 + len(shards) + 2 * count,)),
        ],
        compiler_params=pltpu.CompilerParams(vmem_limit_bytes=24 * MIB),
    )(left_sizes, right_sizes, mine, theirs, *shards, lefts, others, psi)


def order_kernel(in_ref, out_ref, sems):
    _, _, core, _, _ = coordinates()
    copies = []
    for i in range(SIDE * SIDE):
        half, x, which = i // (2 * SIDE), i // 2 % SIDE, i % 2
        chip = (2 * which + (half + core) % 2) * SIDE + x
        copies.append(pltpu.make_async_copy(in_ref.at[i], out_ref.at[chip], sems.at[i]))
    for copy in copies:
        copy.start()
    for copy in copies:
        copy.wait()


def order(blocks):
    return pl.pallas_call(
        order_kernel,
        out_shape=jax.ShapeDtypeStruct(blocks.shape, blocks.dtype),
        in_specs=[VMEM],
        out_specs=ANYWHERE,
        scratch_shapes=[pltpu.SemaphoreType.DMA((blocks.shape[0],))],
        compiler_params=pltpu.CompilerParams(vmem_limit_bytes=8 * MIB),
    )(blocks)


def together(*values):
    return lax.optimization_barrier(values)


def local(wavefunction, left_env, right_env, left_sizes, right_sizes):
    sectors, ranks = lax.axis_size("blk"), lax.axis_size("mpo")
    rows, right_dim = left_env.shape[1] // ranks, right_env.shape[2]
    spots = [(y, x, c) for y in range(SIDE) for x in range(SIDE) for c in range(2)]

    def step(second, by):
        pairs = []
        for y, x, c in spots:
            along_x = (c == 0) != second
            to = place(y, x + by, c) if along_x else place(y + by, x, c)
            pairs.append((place(y, x, c), to))
        return pairs

    def near_step(block, by):
        return lax.ppermute(block, "blk", step(False, by))

    def far_step(block, by):
        return lax.ppermute(block, "blk", step(True, by))

    def swap(block):
        return lax.ppermute(block, "blk", [(i, i ^ 1) for i in range(sectors)])

    def up(block):
        return lax.ppermute(block, "mpo", [(z, (z + 1) % ranks) for z in range(ranks)])

    def down(block):
        return lax.ppermute(block, "mpo", [(z, (z - 1) % ranks) for z in range(ranks)])

    turn = [
        (
            place(y, x, c) * ranks + z,
            place(2 * (y // 2) + z // SIDE, z % SIDE, c) * ranks + x + SIDE * ((y + c) % 2),
        )
        for y, x, c in spots
        for z in range(ranks)
    ]
    keep, give = cut(wavefunction, left_sizes, right_sizes)
    up1, down1 = up(left_env), down(left_env)
    right_env, keep, give = together(right_env, keep, give)
    own = lax.ppermute(right_env, ("blk", "mpo"), turn)
    up2, down2 = up(up1), down(down1)

    below, above, two = near_step(own, 1), near_step(own, -1), near_step(own, 2)
    up3, down3 = up(up2), down(down2)
    below, above, two, up3, down3 = together(below, above, two, up3, down3)
    line_a, line_b = stack(own, below), stack(above, two)
    a_below, a_above = far_step(line_a, 1), far_step(line_a, -1)
    b_below, b_above = far_step(line_b, 1), far_step(line_b, -1)
    up4 = up(up3)
    lefts = stack(left_env, down1, down2, down3, up4, up3, up2, up1, give)
    a_below, a_above, b_below, b_above, lefts = together(a_below, a_above, b_below, b_above, lefts)
    a_two, b_two = far_step(a_below, 1), far_step(b_above, -1)
    others = swap(lefts)

    early = ((0, 0), (SIDE - 1, 0), (1, 0), (0, 2), (SIDE - 1, 2), (1, 2))
    shards = (line_a, a_below, a_above, line_b, b_below, b_above)
    mine = half(early, shards, lefts, keep)
    theirs = half(early, shards, others)
    late = ((2, 0), (2, 2))
    done = last(late, (a_two, b_two), mine, theirs, lefts, others, keep, left_sizes, right_sizes)

    by_plane = lax.all_to_all(done, "mpo", 0, 0)
    chips = SIDE * SIDE
    by_plane = by_plane.reshape(chips, 2, rows, right_dim)
    groups = [
        [place(2 * i + (g // SIDE + c) % 2, g % SIDE, c) for g in range(ranks) for i in range(2)]
        for c in range(2)
    ]
    out = order(lax.all_to_all(by_plane, "blk", 0, 0, axis_index_groups=groups))
    return out.reshape(sectors, rows, right_dim)


def solution(mesh):
    placed = (P("blk", None), P("mpo", "blk", None), P("mpo", "blk", None), P(), P())
    return jax.shard_map(
        local, mesh=mesh, in_specs=placed, out_specs=P(None, "mpo", "blk"), check_vma=False
    )
```

```python
import functools

import jax
import jax.numpy as jnp
from jax import lax
from jax.experimental import pallas as pl
from jax.experimental.pallas import tpu as pltpu
from jax.sharding import PartitionSpec as P

MIB = 1024 * 1024
SIDE = 4
OFFSETS = (0, SIDE - 1, 1, 2)
ANYWHERE = pl.BlockSpec(memory_space=pl.ANY)
SMEM = pl.BlockSpec(memory_space=pltpu.SMEM)
VMEM = pl.BlockSpec(memory_space=pltpu.VMEM)


def place(y, x, core):
    return ((y % SIDE) * SIDE + x % SIDE) * 2 + core


def stack_kernel(*refs):
    inputs, out, sems = refs[:-2], refs[-2], refs[-1]
    copies = [pltpu.make_async_copy(ref, out.at[i], sems.at[i]) for i, ref in enumerate(inputs)]
    for copy in copies:
        copy.start()
    for copy in copies:
        copy.wait()


def stack(*pieces):
    return pl.pallas_call(
        stack_kernel,
        out_shape=jax.ShapeDtypeStruct((len(pieces), *pieces[0].shape), pieces[0].dtype),
        in_specs=[ANYWHERE] * len(pieces),
        out_specs=ANYWHERE,
        scratch_shapes=[pltpu.SemaphoreType.DMA((len(pieces),))],
        compiler_params=pltpu.CompilerParams(vmem_limit_bytes=MIB),
    )(*pieces)


def coordinates():
    sector, rank = lax.axis_index("blk"), lax.axis_index("mpo")
    return sector, rank, sector % 2, sector // 2 % SIDE, sector // (2 * SIDE)


def right_sector(rank, core, which):
    y = ((rank // SIDE + core) & 1) + 2 * which
    return (y * SIDE + rank % SIDE) * 2 + core


def cut_kernel(left_sizes, right_sizes, psi_ref, keep_ref, give_ref, held, sems):
    sector, rank, core, _, _ = coordinates()
    _, left_dim, right_dim = keep_ref.shape
    wanted = [right_sector(rank, c, i) for c in (core, 1 - core) for i in range(2)]
    copies = []
    for i, b in enumerate(wanted):
        first = pl.multiple_of(b * right_dim, right_dim)
        copies.append(pltpu.make_async_copy(psi_ref.at[:, pl.ds(first, right_dim)], held.at[i], sems.at[i]))
    for copy in copies:
        copy.start()
    row = lax.broadcasted_iota(jnp.int32, (left_dim, right_dim), 0)
    col = lax.broadcasted_iota(jnp.int32, (left_dim, right_dim), 1)
    own_left = left_sizes[sector]
    for i, b in enumerate(wanted):
        copies[i].wait()
        inside = jnp.logical_and(row < own_left, col < right_sizes[b])
        block = jnp.where(inside, held[i].astype(jnp.float32), 0.0).astype(held.dtype)
        (keep_ref if i < 2 else give_ref)[i % 2] = block


def cut(wavefunction, left_sizes, right_sizes):
    left_dim, columns = wavefunction.shape
    block = (left_dim, columns // right_sizes.shape[0])
    shape = jax.ShapeDtypeStruct((2, *block), wavefunction.dtype)
    return pl.pallas_call(
        cut_kernel,
        out_shape=(shape, shape),
        in_specs=[SMEM, SMEM, ANYWHERE],
        out_specs=(VMEM, VMEM),
        scratch_shapes=[pltpu.VMEM((4, *block), wavefunction.dtype), pltpu.SemaphoreType.DMA((4,))],
        compiler_params=pltpu.CompilerParams(vmem_limit_bytes=60 * MIB),
    )(left_sizes, right_sizes, wavefunction)


def half_kernel(pieces, *refs):
    ins, (out_ref, held, left_held, psi_held, middle, sems) = refs[:-6], refs[-6:]
    shards, lefts, psi = ins[: len(pieces)], ins[len(pieces)], ins[len(pieces) + 1 :]
    _, rank, core, x0, y0 = coordinates()
    ranks, pair, left_dim, inner = left_held.shape
    right_dim = psi_held.shape[2]
    first = [
        pltpu.make_async_copy(psi[0] if psi else lefts.at[ranks], psi_held, sems.at[0]),
        pltpu.make_async_copy(lefts.at[pl.ds(0, ranks)], left_held, sems.at[1]),
    ]
    coming = [pltpu.make_async_copy(r, held.at[i], sems.at[2 + i]) for i, r in enumerate(shards)]
    for copy in first + coming:
        copy.start()
    out_ref[...] = jnp.zeros_like(out_ref)
    for copy in first:
        copy.wait()
    some = ranks // 2
    for b in range(2):
        for part in range(0, ranks, some):
            block = left_held[part : part + some].reshape(some * pair * left_dim, inner)
            product = jnp.dot(block, psi_held[b], preferred_element_type=jnp.float32)
            product = product.astype(middle.dtype).reshape(some, pair, left_dim, right_dim)
            for w in range(pair):
                columns = slice(w * right_dim, (w + 1) * right_dim)
                middle[b, part : part + some, :, columns] = product[:, w]
    for i, (far, start) in enumerate(pieces):
        coming[i].wait()
        for k in range(held.shape[1]):
            near = OFFSETS[start + k]
            y = jnp.where(core == 0, y0 + far, y0 + near) & (SIDE - 1)
            x = jnp.where(core == 0, x0 + near, x0 + far) & (SIDE - 1)
            which, at = y // 2, (x + SIDE * (y & 1) - rank) & (ranks - 1)
            shard = held[i, k].reshape(pair * right_dim, right_dim)
            out_ref[which] += jnp.dot(middle[which, at], shard, preferred_element_type=jnp.float32)


def half(pieces, shards, lefts, *psi):
    dtype = lefts.dtype
    slots, pair, left_dim, inner = lefts.shape
    ranks, right_dim = slots - 1, shards[0].shape[-1]
    return pl.pallas_call(
        functools.partial(half_kernel, pieces),
        out_shape=jax.ShapeDtypeStruct((2, left_dim, right_dim), jnp.float32),
        in_specs=[ANYWHERE] * (len(shards) + 1 + len(psi)),
        out_specs=VMEM,
        scratch_shapes=[
            pltpu.VMEM((len(shards), *shards[0].shape), dtype),
            pltpu.VMEM((ranks, pair, left_dim, inner), dtype),
            pltpu.VMEM((2, inner, right_dim), dtype),
            pltpu.VMEM((2, ranks, left_dim, pair * right_dim), dtype),
            pltpu.SemaphoreType.DMA((len(shards) + 2,)),
        ],
        compiler_params=pltpu.CompilerParams(vmem_limit_bytes=24 * MIB),
    )(*shards, lefts, *psi)


def last_kernel(pieces, left_sizes, right_sizes, mine, theirs, *refs):
    ins, (out_ref, held, left_held, psi_held, total, sems) = refs[:-6], refs[-6:]
    shards, (lefts, others, psi) = ins[: len(pieces)], ins[len(pieces) :]
    sector, rank, core, x0, y0 = coordinates()
    ranks, _, _, rows, right_dim = out_ref.shape
    left_dim = ranks * rows
    copies = [
        pltpu.make_async_copy(psi, psi_held.at[0], sems.at[0]),
        pltpu.make_async_copy(others.at[ranks], psi_held.at[1], sems.at[1]),
    ]
    sectors_of = []
    for i, (far, start) in enumerate(pieces):
        copies.append(pltpu.make_async_copy(shards[i], held.at[i], sems.at[len(copies)]))
        for k in range(held.shape[1]):
            near = OFFSETS[start + k]
            y = jnp.where(core == 0, y0 + far, y0 + near) & (SIDE - 1)
            x = jnp.where(core == 0, x0 + near, x0 + far) & (SIDE - 1)
            at = (x + SIDE * (y & 1) - rank) & (ranks - 1)
            for a, source in enumerate((lefts, others)):
                place_in = left_held.at[len(sectors_of), a]
                copies.append(pltpu.make_async_copy(source.at[at], place_in, sems.at[len(copies)]))
            sectors_of.append(y // 2)
    for copy in copies:
        copy.start()
    total[0] = mine[...]
    total[1] = theirs[...]
    for copy in copies:
        copy.wait()
    for i, which in enumerate(sectors_of):
        shard = held[i // held.shape[1], i % held.shape[1]]
        for a in range(2):
            block = left_held[i, a].reshape(2 * left_dim, left_dim)
            product = jnp.dot(block, psi_held[a, which], preferred_element_type=jnp.float32)
            product = product.astype(held.dtype)
            term = jnp.dot(product[:left_dim], shard[0], preferred_element_type=jnp.float32)
            term += jnp.dot(product[left_dim:], shard[1], preferred_element_type=jnp.float32)
            total[a, which] += term
    row = lax.broadcasted_iota(jnp.int32, (left_dim, right_dim), 0)
    col = lax.broadcasted_iota(jnp.int32, (left_dim, right_dim), 1)
    for b in range(2):
        own_right = right_sizes[right_sector(rank, core, b)]
        for a, spot in enumerate((core, 1 - core)):
            inside = jnp.logical_and(row < left_sizes[sector - core + spot], col < own_right)
            block = jnp.where(inside, total[a, b], 0.0)
            block = block.astype(out_ref.dtype).reshape(ranks, 1, rows, right_dim)
            out_ref[:, b, pl.ds(spot, 1)] = block


def last(pieces, shards, mine, theirs, lefts, others, psi, left_sizes, right_sizes):
    dtype = psi.dtype
    slots, pair, left_dim, inner = lefts.shape
    ranks, right_dim = slots - 1, psi.shape[2]
    count = len(shards) * shards[0].shape[0]
    return pl.pallas_call(
        functools.partial(last_kernel, pieces),
        out_shape=jax.ShapeDtypeStruct((ranks, 2, 2, left_dim // ranks, right_dim), dtype),
        in_specs=[SMEM, SMEM, VMEM, VMEM] + [ANYWHERE] * (len(shards) + 3),
        out_specs=VMEM,
        scratch_shapes=[
            pltpu.VMEM((len(shards), *shards[0].shape), dtype),
            pltpu.VMEM((count, 2, pair, left_dim, inner), dtype),
            pltpu.VMEM((2, *psi.shape), dtype),
            pltpu.VMEM((2, *mine.shape), jnp.float32),
            pltpu.SemaphoreType.DMA((2 + len(shards) + 2 * count,)),
        ],
        compiler_params=pltpu.CompilerParams(vmem_limit_bytes=24 * MIB),
    )(left_sizes, right_sizes, mine, theirs, *shards, lefts, others, psi)


def order_kernel(in_ref, out_ref, sems):
    _, _, core, _, _ = coordinates()
    copies = []
    for i in range(SIDE * SIDE):
        half, x, which = i // (2 * SIDE), i // 2 % SIDE, i % 2
        chip = (2 * which + (half + core) % 2) * SIDE + x
        copies.append(pltpu.make_async_copy(in_ref.at[i], out_ref.at[chip], sems.at[i]))
    for copy in copies:
        copy.start()
    for copy in copies:
        copy.wait()


def order(blocks):
    return pl.pallas_call(
        order_kernel,
        out_shape=jax.ShapeDtypeStruct(blocks.shape, blocks.dtype),
        in_specs=[VMEM],
        out_specs=ANYWHERE,
        scratch_shapes=[pltpu.SemaphoreType.DMA((blocks.shape[0],))],
        compiler_params=pltpu.CompilerParams(vmem_limit_bytes=8 * MIB),
    )(blocks)


def together(*values):
    return lax.optimization_barrier(values)


def local(wavefunction, left_env, right_env, left_sizes, right_sizes):
    sectors, ranks = lax.axis_size("blk"), lax.axis_size("mpo")
    rows, right_dim = left_env.shape[1] // ranks, right_env.shape[2]
    spots = [(y, x, c) for y in range(SIDE) for x in range(SIDE) for c in range(2)]

    def step(second, by):
        pairs = []
        for y, x, c in spots:
            along_x = (c == 0) != second
            to = place(y, x + by, c) if along_x else place(y + by, x, c)
            pairs.append((place(y, x, c), to))
        return pairs

    def near_step(block, by):
        return lax.ppermute(block, "blk", step(False, by))

    def far_step(block, by):
        return lax.ppermute(block, "blk", step(True, by))

    def swap(block):
        return lax.ppermute(block, "blk", [(i, i ^ 1) for i in range(sectors)])

    def up(block):
        return lax.ppermute(block, "mpo", [(z, (z + 1) % ranks) for z in range(ranks)])

    def down(block):
        return lax.ppermute(block, "mpo", [(z, (z - 1) % ranks) for z in range(ranks)])

    turn = [
        (
            place(y, x, c) * ranks + z,
            place(2 * (y // 2) + z // SIDE, z % SIDE, c) * ranks + x + SIDE * ((y + c) % 2),
        )
        for y, x, c in spots
        for z in range(ranks)
    ]
    keep, give = cut(wavefunction, left_sizes, right_sizes)
    up1, down1 = up(left_env), down(left_env)
    right_env, keep, give = together(right_env, keep, give)
    own = lax.ppermute(right_env, ("blk", "mpo"), turn)
    up2, down2 = up(up1), down(down1)

    below, above, two = near_step(own, 1), near_step(own, -1), near_step(own, 2)
    below, above, two, up2, down2 = together(below, above, two, up2, down2)
    line_a, line_b = stack(own, below), stack(above, two)
    a_below, a_above = far_step(line_a, 1), far_step(line_a, -1)
    b_below, b_above = far_step(line_b, 1), far_step(line_b, -1)
    up3, down3 = up(up2), down(down2)
    up4 = up(up3)
    lefts = stack(left_env, down1, down2, down3, up4, up3, up2, up1, give)
    a_below, a_above, b_below, b_above, lefts = together(a_below, a_above, b_below, b_above, lefts)
    a_two, b_two = far_step(a_below, 1), far_step(b_above, -1)
    others = swap(lefts)

    early = ((0, 0), (SIDE - 1, 0), (1, 0), (0, 2), (SIDE - 1, 2), (1, 2))
    shards = (line_a, a_below, a_above, line_b, b_below, b_above)
    mine = half(early, shards, lefts, keep)
    theirs = half(early, shards, others)
    late = ((2, 0), (2, 2))
    done = last(late, (a_two, b_two), mine, theirs, lefts, others, keep, left_sizes, right_sizes)

    by_plane = lax.all_to_all(done, "mpo", 0, 0)
    chips = SIDE * SIDE
    by_plane = by_plane.reshape(chips, 2, rows, right_dim)
    groups = [
        [place(2 * i + (g // SIDE + c) % 2, g % SIDE, c) for g in range(ranks) for i in range(2)]
        for c in range(2)
    ]
    out = order(lax.all_to_all(by_plane, "blk", 0, 0, axis_index_groups=groups))
    return out.reshape(sectors, rows, right_dim)


def solution(mesh):
    placed = (P("blk", None), P("mpo", "blk", None), P("mpo", "blk", None), P(), P())
    return jax.shard_map(
        local, mesh=mesh, in_specs=placed, out_specs=P(None, "mpo", "blk"), check_vma=False
    )
```

```python
import functools

import jax
import jax.numpy as jnp
from jax import lax
from jax.experimental import pallas as pl
from jax.experimental.pallas import tpu as pltpu
from jax.sharding import PartitionSpec as P

MIB = 1024 * 1024
SIDE = 4
OFFSETS = (0, SIDE - 1, 1, 2)
ANYWHERE = pl.BlockSpec(memory_space=pl.ANY)
SMEM = pl.BlockSpec(memory_space=pltpu.SMEM)
VMEM = pl.BlockSpec(memory_space=pltpu.VMEM)


def place(y, x, core):
    return ((y % SIDE) * SIDE + x % SIDE) * 2 + core


def stack_kernel(*refs):
    inputs, out, sems = refs[:-2], refs[-2], refs[-1]
    copies = [pltpu.make_async_copy(ref, out.at[i], sems.at[i]) for i, ref in enumerate(inputs)]
    for copy in copies:
        copy.start()
    for copy in copies:
        copy.wait()


def stack(*pieces):
    return pl.pallas_call(
        stack_kernel,
        out_shape=jax.ShapeDtypeStruct((len(pieces), *pieces[0].shape), pieces[0].dtype),
        in_specs=[ANYWHERE] * len(pieces),
        out_specs=ANYWHERE,
        scratch_shapes=[pltpu.SemaphoreType.DMA((len(pieces),))],
        compiler_params=pltpu.CompilerParams(vmem_limit_bytes=MIB),
    )(*pieces)


def coordinates():
    sector, rank = lax.axis_index("blk"), lax.axis_index("mpo")
    return sector, rank, sector % 2, sector // 2 % SIDE, sector // (2 * SIDE)


def right_sector(rank, core, which):
    y = ((rank // SIDE + core) & 1) + 2 * which
    return (y * SIDE + rank % SIDE) * 2 + core


def cut_kernel(left_sizes, right_sizes, psi_ref, keep_ref, give_ref, held, sems):
    sector, rank, core, _, _ = coordinates()
    _, left_dim, right_dim = keep_ref.shape
    wanted = [right_sector(rank, c, i) for c in (core, 1 - core) for i in range(2)]
    copies = []
    for i, b in enumerate(wanted):
        first = pl.multiple_of(b * right_dim, right_dim)
        copies.append(pltpu.make_async_copy(psi_ref.at[:, pl.ds(first, right_dim)], held.at[i], sems.at[i]))
    for copy in copies:
        copy.start()
    row = lax.broadcasted_iota(jnp.int32, (left_dim, right_dim), 0)
    col = lax.broadcasted_iota(jnp.int32, (left_dim, right_dim), 1)
    own_left = left_sizes[sector]
    for i, b in enumerate(wanted):
        copies[i].wait()
        inside = jnp.logical_and(row < own_left, col < right_sizes[b])
        block = jnp.where(inside, held[i].astype(jnp.float32), 0.0).astype(held.dtype)
        (keep_ref if i < 2 else give_ref)[i % 2] = block


def cut(wavefunction, left_sizes, right_sizes):
    left_dim, columns = wavefunction.shape
    block = (left_dim, columns // right_sizes.shape[0])
    shape = jax.ShapeDtypeStruct((2, *block), wavefunction.dtype)
    return pl.pallas_call(
        cut_kernel,
        out_shape=(shape, shape),
        in_specs=[SMEM, SMEM, ANYWHERE],
        out_specs=(VMEM, VMEM),
        scratch_shapes=[pltpu.VMEM((4, *block), wavefunction.dtype), pltpu.SemaphoreType.DMA((4,))],
        compiler_params=pltpu.CompilerParams(vmem_limit_bytes=60 * MIB),
    )(left_sizes, right_sizes, wavefunction)


def half_kernel(pieces, *refs):
    ins, (out_ref, held, left_held, psi_held, middle, sems) = refs[:-6], refs[-6:]
    shards, lefts, psi = ins[: len(pieces)], ins[len(pieces)], ins[len(pieces) + 1 :]
    _, rank, core, x0, y0 = coordinates()
    ranks, pair, left_dim, inner = left_held.shape
    right_dim = psi_held.shape[2]
    first = [
        pltpu.make_async_copy(psi[0] if psi else lefts.at[ranks], psi_held, sems.at[0]),
        pltpu.make_async_copy(lefts.at[pl.ds(0, ranks)], left_held, sems.at[1]),
    ]
    coming = [pltpu.make_async_copy(r, held.at[i], sems.at[2 + i]) for i, r in enumerate(shards)]
    for copy in first + coming:
        copy.start()
    out_ref[...] = jnp.zeros_like(out_ref)
    for copy in first:
        copy.wait()
    some = ranks // 2
    for b in range(2):
        for part in range(0, ranks, some):
            block = left_held[part : part + some].reshape(some * pair * left_dim, inner)
            product = jnp.dot(block, psi_held[b], preferred_element_type=jnp.float32)
            product = product.astype(middle.dtype).reshape(some, pair, left_dim, right_dim)
            for w in range(pair):
                columns = slice(w * right_dim, (w + 1) * right_dim)
                middle[b, part : part + some, :, columns] = product[:, w]
    for i, (far, start) in enumerate(pieces):
        coming[i].wait()
        for k in range(held.shape[1]):
            near = OFFSETS[start + k]
            y = jnp.where(core == 0, y0 + far, y0 + near) & (SIDE - 1)
            x = jnp.where(core == 0, x0 + near, x0 + far) & (SIDE - 1)
            which, at = y // 2, (x + SIDE * (y & 1) - rank) & (ranks - 1)
            shard = held[i, k].reshape(pair * right_dim, right_dim)
            out_ref[which] += jnp.dot(middle[which, at], shard, preferred_element_type=jnp.float32)


def half(pieces, shards, lefts, *psi):
    dtype = lefts.dtype
    slots, pair, left_dim, inner = lefts.shape
    ranks, right_dim = slots - 1, shards[0].shape[-1]
    return pl.pallas_call(
        functools.partial(half_kernel, pieces),
        out_shape=jax.ShapeDtypeStruct((2, left_dim, right_dim), jnp.float32),
        in_specs=[ANYWHERE] * (len(shards) + 1 + len(psi)),
        out_specs=VMEM,
        scratch_shapes=[
            pltpu.VMEM((len(shards), *shards[0].shape), dtype),
            pltpu.VMEM((ranks, pair, left_dim, inner), dtype),
            pltpu.VMEM((2, inner, right_dim), dtype),
            pltpu.VMEM((2, ranks, left_dim, pair * right_dim), dtype),
            pltpu.SemaphoreType.DMA((len(shards) + 2,)),
        ],
        compiler_params=pltpu.CompilerParams(vmem_limit_bytes=24 * MIB),
    )(*shards, lefts, *psi)


def last_kernel(pieces, left_sizes, right_sizes, mine, theirs, *refs):
    ins, (out_ref, held, left_held, psi_held, total, sems) = refs[:-6], refs[-6:]
    shards, (lefts, others, psi) = ins[: len(pieces)], ins[len(pieces) :]
    sector, rank, core, x0, y0 = coordinates()
    ranks, _, _, rows, right_dim = out_ref.shape
    left_dim = ranks * rows
    copies = [
        pltpu.make_async_copy(psi, psi_held.at[0], sems.at[0]),
        pltpu.make_async_copy(others.at[ranks], psi_held.at[1], sems.at[1]),
    ]
    sectors_of = []
    for i, (far, start) in enumerate(pieces):
        copies.append(pltpu.make_async_copy(shards[i], held.at[i], sems.at[len(copies)]))
        for k in range(held.shape[1]):
            near = OFFSETS[start + k]
            y = jnp.where(core == 0, y0 + far, y0 + near) & (SIDE - 1)
            x = jnp.where(core == 0, x0 + near, x0 + far) & (SIDE - 1)
            at = (x + SIDE * (y & 1) - rank) & (ranks - 1)
            for a, source in enumerate((lefts, others)):
                place_in = left_held.at[len(sectors_of), a]
                copies.append(pltpu.make_async_copy(source.at[at], place_in, sems.at[len(copies)]))
            sectors_of.append(y // 2)
    for copy in copies:
        copy.start()
    total[0] = mine[...]
    total[1] = theirs[...]
    for copy in copies:
        copy.wait()
    for i, which in enumerate(sectors_of):
        shard = held[i // held.shape[1], i % held.shape[1]]
        for a in range(2):
            block = left_held[i, a].reshape(2 * left_dim, left_dim)
            product = jnp.dot(block, psi_held[a, which], preferred_element_type=jnp.float32)
            product = product.astype(held.dtype)
            term = jnp.dot(product[:left_dim], shard[0], preferred_element_type=jnp.float32)
            term += jnp.dot(product[left_dim:], shard[1], preferred_element_type=jnp.float32)
            total[a, which] += term
    row = lax.broadcasted_iota(jnp.int32, (left_dim, right_dim), 0)
    col = lax.broadcasted_iota(jnp.int32, (left_dim, right_dim), 1)
    for b in range(2):
        own_right = right_sizes[right_sector(rank, core, b)]
        for a, spot in enumerate((core, 1 - core)):
            inside = jnp.logical_and(row < left_sizes[sector - core + spot], col < own_right)
            block = jnp.where(inside, total[a, b], 0.0)
            block = block.astype(out_ref.dtype).reshape(ranks, 1, rows, right_dim)
            out_ref[:, b, pl.ds(spot, 1)] = block


def last(pieces, shards, mine, theirs, lefts, others, psi, left_sizes, right_sizes):
    dtype = psi.dtype
    slots, pair, left_dim, inner = lefts.shape
    ranks, right_dim = slots - 1, psi.shape[2]
    count = len(shards) * shards[0].shape[0]
    return pl.pallas_call(
        functools.partial(last_kernel, pieces),
        out_shape=jax.ShapeDtypeStruct((ranks, 2, 2, left_dim // ranks, right_dim), dtype),
        in_specs=[SMEM, SMEM, VMEM, VMEM] + [ANYWHERE] * (len(shards) + 3),
        out_specs=VMEM,
        scratch_shapes=[
            pltpu.VMEM((len(shards), *shards[0].shape), dtype),
            pltpu.VMEM((count, 2, pair, left_dim, inner), dtype),
            pltpu.VMEM((2, *psi.shape), dtype),
            pltpu.VMEM((2, *mine.shape), jnp.float32),
            pltpu.SemaphoreType.DMA((2 + len(shards) + 2 * count,)),
        ],
        compiler_params=pltpu.CompilerParams(vmem_limit_bytes=24 * MIB),
    )(left_sizes, right_sizes, mine, theirs, *shards, lefts, others, psi)


def order_kernel(in_ref, out_ref, sems):
    _, _, core, _, _ = coordinates()
    copies = []
    for i in range(SIDE * SIDE):
        half, x, which = i // (2 * SIDE), i // 2 % SIDE, i % 2
        chip = (2 * which + (half + core) % 2) * SIDE + x
        copies.append(pltpu.make_async_copy(in_ref.at[i], out_ref.at[chip], sems.at[i]))
    for copy in copies:
        copy.start()
    for copy in copies:
        copy.wait()


def order(blocks):
    return pl.pallas_call(
        order_kernel,
        out_shape=jax.ShapeDtypeStruct(blocks.shape, blocks.dtype),
        in_specs=[VMEM],
        out_specs=ANYWHERE,
        scratch_shapes=[pltpu.SemaphoreType.DMA((blocks.shape[0],))],
        compiler_params=pltpu.CompilerParams(vmem_limit_bytes=8 * MIB),
    )(blocks)


def together(*values):
    return lax.optimization_barrier(values)


def local(wavefunction, left_env, right_env, left_sizes, right_sizes):
    sectors, ranks = lax.axis_size("blk"), lax.axis_size("mpo")
    rows, right_dim = left_env.shape[1] // ranks, right_env.shape[2]
    spots = [(y, x, c) for y in range(SIDE) for x in range(SIDE) for c in range(2)]

    def step(second, by):
        pairs = []
        for y, x, c in spots:
            along_x = (c == 0) != second
            to = place(y, x + by, c) if along_x else place(y + by, x, c)
            pairs.append((place(y, x, c), to))
        return pairs

    def near_step(block, by):
        return lax.ppermute(block, "blk", step(False, by))

    def far_step(block, by):
        return lax.ppermute(block, "blk", step(True, by))

    def swap(block):
        return lax.ppermute(block, "blk", [(i, i ^ 1) for i in range(sectors)])

    def up(block):
        return lax.ppermute(block, "mpo", [(z, (z + 1) % ranks) for z in range(ranks)])

    def down(block):
        return lax.ppermute(block, "mpo", [(z, (z - 1) % ranks) for z in range(ranks)])

    turn = [
        (
            place(y, x, c) * ranks + z,
            place(2 * (y // 2) + z // SIDE, z % SIDE, c) * ranks + x + SIDE * ((y + c) % 2),
        )
        for y, x, c in spots
        for z in range(ranks)
    ]
    keep, give = cut(wavefunction, left_sizes, right_sizes)
    up1, down1 = up(left_env), down(left_env)
    right_env, keep, give = together(right_env, keep, give)
    own = lax.ppermute(right_env, ("blk", "mpo"), turn)
    up2, down2 = up(up1), down(down1)

    below, above, two = near_step(own, 1), near_step(own, -1), near_step(own, 2)
    up3 = up(up2)
    below, above, two, up3, down2 = together(below, above, two, up3, down2)
    line_a, line_b = stack(own, below), stack(above, two)
    a_below, a_above = far_step(line_a, 1), far_step(line_a, -1)
    b_below, b_above = far_step(line_b, 1), far_step(line_b, -1)
    up4, down3 = up(up3), down(down2)
    lefts = stack(left_env, down1, down2, down3, up4, up3, up2, up1, give)
    a_below, a_above, b_below, b_above, lefts = together(a_below, a_above, b_below, b_above, lefts)
    a_two, b_two = far_step(a_below, 1), far_step(b_above, -1)
    others = swap(lefts)

    early = ((0, 0), (SIDE - 1, 0), (1, 0), (0, 2), (SIDE - 1, 2), (1, 2))
    shards = (line_a, a_below, a_above, line_b, b_below, b_above)
    mine = half(early, shards, lefts, keep)
    theirs = half(early, shards, others)
    late = ((2, 0), (2, 2))
    done = last(late, (a_two, b_two), mine, theirs, lefts, others, keep, left_sizes, right_sizes)

    by_plane = lax.all_to_all(done, "mpo", 0, 0)
    chips = SIDE * SIDE
    by_plane = by_plane.reshape(chips, 2, rows, right_dim)
    groups = [
        [place(2 * i + (g // SIDE + c) % 2, g % SIDE, c) for g in range(ranks) for i in range(2)]
        for c in range(2)
    ]
    out = order(lax.all_to_all(by_plane, "blk", 0, 0, axis_index_groups=groups))
    return out.reshape(sectors, rows, right_dim)


def solution(mesh):
    placed = (P("blk", None), P("mpo", "blk", None), P("mpo", "blk", None), P(), P())
    return jax.shard_map(
        local, mesh=mesh, in_specs=placed, out_specs=P(None, "mpo", "blk"), check_vma=False
    )
```

```python
import functools

import jax
import jax.numpy as jnp
from jax import lax
from jax.experimental import pallas as pl
from jax.experimental.pallas import tpu as pltpu
from jax.sharding import PartitionSpec as P

MIB = 1024 * 1024
SIDE = 4
OFFSETS = (0, SIDE - 1, 1, 2)
ANYWHERE = pl.BlockSpec(memory_space=pl.ANY)
SMEM = pl.BlockSpec(memory_space=pltpu.SMEM)
VMEM = pl.BlockSpec(memory_space=pltpu.VMEM)


def place(y, x, core):
    return ((y % SIDE) * SIDE + x % SIDE) * 2 + core


def stack_kernel(*refs):
    inputs, out, sems = refs[:-2], refs[-2], refs[-1]
    copies = [pltpu.make_async_copy(ref, out.at[i], sems.at[i]) for i, ref in enumerate(inputs)]
    for copy in copies:
        copy.start()
    for copy in copies:
        copy.wait()


def stack(*pieces):
    return pl.pallas_call(
        stack_kernel,
        out_shape=jax.ShapeDtypeStruct((len(pieces), *pieces[0].shape), pieces[0].dtype),
        in_specs=[ANYWHERE] * len(pieces),
        out_specs=ANYWHERE,
        scratch_shapes=[pltpu.SemaphoreType.DMA((len(pieces),))],
        compiler_params=pltpu.CompilerParams(vmem_limit_bytes=MIB),
    )(*pieces)


def coordinates():
    sector, rank = lax.axis_index("blk"), lax.axis_index("mpo")
    return sector, rank, sector % 2, sector // 2 % SIDE, sector // (2 * SIDE)


def right_sector(rank, core, which):
    y = ((rank // SIDE + core) & 1) + 2 * which
    return (y * SIDE + rank % SIDE) * 2 + core


def cut_kernel(left_sizes, right_sizes, psi_ref, keep_ref, give_ref, held, sems):
    sector, rank, core, _, _ = coordinates()
    _, left_dim, right_dim = keep_ref.shape
    wanted = [right_sector(rank, c, i) for c in (core, 1 - core) for i in range(2)]
    copies = []
    for i, b in enumerate(wanted):
        first = pl.multiple_of(b * right_dim, right_dim)
        copies.append(pltpu.make_async_copy(psi_ref.at[:, pl.ds(first, right_dim)], held.at[i], sems.at[i]))
    for copy in copies:
        copy.start()
    row = lax.broadcasted_iota(jnp.int32, (left_dim, right_dim), 0)
    col = lax.broadcasted_iota(jnp.int32, (left_dim, right_dim), 1)
    own_left = left_sizes[sector]
    for i, b in enumerate(wanted):
        copies[i].wait()
        inside = jnp.logical_and(row < own_left, col < right_sizes[b])
        block = jnp.where(inside, held[i].astype(jnp.float32), 0.0).astype(held.dtype)
        (keep_ref if i < 2 else give_ref)[i % 2] = block


def cut(wavefunction, left_sizes, right_sizes):
    left_dim, columns = wavefunction.shape
    block = (left_dim, columns // right_sizes.shape[0])
    shape = jax.ShapeDtypeStruct((2, *block), wavefunction.dtype)
    return pl.pallas_call(
        cut_kernel,
        out_shape=(shape, shape),
        in_specs=[SMEM, SMEM, ANYWHERE],
        out_specs=(VMEM, VMEM),
        scratch_shapes=[pltpu.VMEM((4, *block), wavefunction.dtype), pltpu.SemaphoreType.DMA((4,))],
        compiler_params=pltpu.CompilerParams(vmem_limit_bytes=60 * MIB),
    )(left_sizes, right_sizes, wavefunction)


def half_kernel(pieces, *refs):
    ins, (out_ref, held, left_held, psi_held, middle, sems) = refs[:-6], refs[-6:]
    shards, lefts, psi = ins[: len(pieces)], ins[len(pieces)], ins[len(pieces) + 1 :]
    _, rank, core, x0, y0 = coordinates()
    ranks, pair, left_dim, inner = left_held.shape
    right_dim = psi_held.shape[2]
    first = [
        pltpu.make_async_copy(psi[0] if psi else lefts.at[ranks], psi_held, sems.at[0]),
        pltpu.make_async_copy(lefts.at[pl.ds(0, ranks)], left_held, sems.at[1]),
    ]
    coming = [pltpu.make_async_copy(r, held.at[i], sems.at[2 + i]) for i, r in enumerate(shards)]
    for copy in first + coming:
        copy.start()
    out_ref[...] = jnp.zeros_like(out_ref)
    for copy in first:
        copy.wait()
    some = ranks // 2
    for b in range(2):
        for part in range(0, ranks, some):
            block = left_held[part : part + some].reshape(some * pair * left_dim, inner)
            product = jnp.dot(block, psi_held[b], preferred_element_type=jnp.float32)
            product = product.astype(middle.dtype).reshape(some, pair, left_dim, right_dim)
            for w in range(pair):
                columns = slice(w * right_dim, (w + 1) * right_dim)
                middle[b, part : part + some, :, columns] = product[:, w]
    for i, (far, start) in enumerate(pieces):
        coming[i].wait()
        for k in range(held.shape[1]):
            near = OFFSETS[start + k]
            y = jnp.where(core == 0, y0 + far, y0 + near) & (SIDE - 1)
            x = jnp.where(core == 0, x0 + near, x0 + far) & (SIDE - 1)
            which, at = y // 2, (x + SIDE * (y & 1) - rank) & (ranks - 1)
            shard = held[i, k].reshape(pair * right_dim, right_dim)
            out_ref[which] += jnp.dot(middle[which, at], shard, preferred_element_type=jnp.float32)


def half(pieces, shards, lefts, *psi):
    dtype = lefts.dtype
    slots, pair, left_dim, inner = lefts.shape
    ranks, right_dim = slots - 1, shards[0].shape[-1]
    return pl.pallas_call(
        functools.partial(half_kernel, pieces),
        out_shape=jax.ShapeDtypeStruct((2, left_dim, right_dim), jnp.float32),
        in_specs=[ANYWHERE] * (len(shards) + 1 + len(psi)),
        out_specs=VMEM,
        scratch_shapes=[
            pltpu.VMEM((len(shards), *shards[0].shape), dtype),
            pltpu.VMEM((ranks, pair, left_dim, inner), dtype),
            pltpu.VMEM((2, inner, right_dim), dtype),
            pltpu.VMEM((2, ranks, left_dim, pair * right_dim), dtype),
            pltpu.SemaphoreType.DMA((len(shards) + 2,)),
        ],
        compiler_params=pltpu.CompilerParams(vmem_limit_bytes=24 * MIB),
    )(*shards, lefts, *psi)


def last_kernel(pieces, left_sizes, right_sizes, mine, theirs, *refs):
    ins, (out_ref, held, left_held, psi_held, total, sems) = refs[:-6], refs[-6:]
    shards, (lefts, others, psi) = ins[: len(pieces)], ins[len(pieces) :]
    sector, rank, core, x0, y0 = coordinates()
    ranks, _, _, rows, right_dim = out_ref.shape
    left_dim = ranks * rows
    copies = [
        pltpu.make_async_copy(psi, psi_held.at[0], sems.at[0]),
        pltpu.make_async_copy(others.at[ranks], psi_held.at[1], sems.at[1]),
    ]
    sectors_of = []
    for i, (far, start) in enumerate(pieces):
        copies.append(pltpu.make_async_copy(shards[i], held.at[i], sems.at[len(copies)]))
        for k in range(held.shape[1]):
            near = OFFSETS[start + k]
            y = jnp.where(core == 0, y0 + far, y0 + near) & (SIDE - 1)
            x = jnp.where(core == 0, x0 + near, x0 + far) & (SIDE - 1)
            at = (x + SIDE * (y & 1) - rank) & (ranks - 1)
            for a, source in enumerate((lefts, others)):
                place_in = left_held.at[len(sectors_of), a]
                copies.append(pltpu.make_async_copy(source.at[at], place_in, sems.at[len(copies)]))
            sectors_of.append(y // 2)
    for copy in copies:
        copy.start()
    total[0] = mine[...]
    total[1] = theirs[...]
    for copy in copies:
        copy.wait()
    for i, which in enumerate(sectors_of):
        shard = held[i // held.shape[1], i % held.shape[1]]
        for a in range(2):
            block = left_held[i, a].reshape(2 * left_dim, left_dim)
            product = jnp.dot(block, psi_held[a, which], preferred_element_type=jnp.float32)
            product = product.astype(held.dtype)
            term = jnp.dot(product[:left_dim], shard[0], preferred_element_type=jnp.float32)
            term += jnp.dot(product[left_dim:], shard[1], preferred_element_type=jnp.float32)
            total[a, which] += term
    row = lax.broadcasted_iota(jnp.int32, (left_dim, right_dim), 0)
    col = lax.broadcasted_iota(jnp.int32, (left_dim, right_dim), 1)
    for b in range(2):
        own_right = right_sizes[right_sector(rank, core, b)]
        for a, spot in enumerate((core, 1 - core)):
            inside = jnp.logical_and(row < left_sizes[sector - core + spot], col < own_right)
            block = jnp.where(inside, total[a, b], 0.0)
            block = block.astype(out_ref.dtype).reshape(ranks, 1, rows, right_dim)
            out_ref[:, b, pl.ds(spot, 1)] = block


def last(pieces, shards, mine, theirs, lefts, others, psi, left_sizes, right_sizes):
    dtype = psi.dtype
    slots, pair, left_dim, inner = lefts.shape
    ranks, right_dim = slots - 1, psi.shape[2]
    count = len(shards) * shards[0].shape[0]
    return pl.pallas_call(
        functools.partial(last_kernel, pieces),
        out_shape=jax.ShapeDtypeStruct((ranks, 2, 2, left_dim // ranks, right_dim), dtype),
        in_specs=[SMEM, SMEM, VMEM, VMEM] + [ANYWHERE] * (len(shards) + 3),
        out_specs=VMEM,
        scratch_shapes=[
            pltpu.VMEM((len(shards), *shards[0].shape), dtype),
            pltpu.VMEM((count, 2, pair, left_dim, inner), dtype),
            pltpu.VMEM((2, *psi.shape), dtype),
            pltpu.VMEM((2, *mine.shape), jnp.float32),
            pltpu.SemaphoreType.DMA((2 + len(shards) + 2 * count,)),
        ],
        compiler_params=pltpu.CompilerParams(vmem_limit_bytes=24 * MIB),
    )(left_sizes, right_sizes, mine, theirs, *shards, lefts, others, psi)


def order_kernel(in_ref, out_ref, sems):
    _, _, core, _, _ = coordinates()
    copies = []
    for i in range(SIDE * SIDE):
        half, x, which = i // (2 * SIDE), i // 2 % SIDE, i % 2
        chip = (2 * which + (half + core) % 2) * SIDE + x
        copies.append(pltpu.make_async_copy(in_ref.at[i], out_ref.at[chip], sems.at[i]))
    for copy in copies:
        copy.start()
    for copy in copies:
        copy.wait()


def order(blocks):
    return pl.pallas_call(
        order_kernel,
        out_shape=jax.ShapeDtypeStruct(blocks.shape, blocks.dtype),
        in_specs=[VMEM],
        out_specs=ANYWHERE,
        scratch_shapes=[pltpu.SemaphoreType.DMA((blocks.shape[0],))],
        compiler_params=pltpu.CompilerParams(vmem_limit_bytes=8 * MIB),
    )(blocks)


def together(*values):
    return lax.optimization_barrier(values)


def local(wavefunction, left_env, right_env, left_sizes, right_sizes):
    sectors, ranks = lax.axis_size("blk"), lax.axis_size("mpo")
    rows, right_dim = left_env.shape[1] // ranks, right_env.shape[2]
    spots = [(y, x, c) for y in range(SIDE) for x in range(SIDE) for c in range(2)]

    def step(second, by):
        pairs = []
        for y, x, c in spots:
            along_x = (c == 0) != second
            to = place(y, x + by, c) if along_x else place(y + by, x, c)
            pairs.append((place(y, x, c), to))
        return pairs

    def near_step(block, by):
        return lax.ppermute(block, "blk", step(False, by))

    def far_step(block, by):
        return lax.ppermute(block, "blk", step(True, by))

    def swap(block):
        return lax.ppermute(block, "blk", [(i, i ^ 1) for i in range(sectors)])

    def up(block):
        return lax.ppermute(block, "mpo", [(z, (z + 1) % ranks) for z in range(ranks)])

    def down(block):
        return lax.ppermute(block, "mpo", [(z, (z - 1) % ranks) for z in range(ranks)])

    turn = [
        (
            place(y, x, c) * ranks + z,
            place(2 * (y // 2) + z // SIDE, z % SIDE, c) * ranks + x + SIDE * ((y + c) % 2),
        )
        for y, x, c in spots
        for z in range(ranks)
    ]
    own = lax.ppermute(right_env, ("blk", "mpo"), turn)
    up1, down1 = up(left_env), down(left_env)
    keep, give = cut(wavefunction, left_sizes, right_sizes)
    up2, down2 = up(up1), down(down1)
    own, keep, give = together(own, keep, give)

    below, above, two = near_step(own, 1), near_step(own, -1), near_step(own, 2)
    below, above, two, up2, down2 = together(below, above, two, up2, down2)
    line_a, line_b = stack(own, below), stack(above, two)
    a_below, a_above = far_step(line_a, 1), far_step(line_a, -1)
    b_below, b_above = far_step(line_b, 1), far_step(line_b, -1)
    up3, down3 = up(up2), down(down2)
    up4 = up(up3)
    lefts = stack(left_env, down1, down2, down3, up4, up3, up2, up1, give)
    a_two = far_step(a_below, 1)
    a_above, b_below, b_above, a_two, lefts = together(a_above, b_below, b_above, a_two, lefts)
    b_two = far_step(b_above, -1)
    others = swap(lefts)

    early = ((0, 0), (SIDE - 1, 0), (1, 0), (0, 2), (SIDE - 1, 2), (1, 2))
    shards = (line_a, a_below, a_above, line_b, b_below, b_above)
    mine = half(early, shards, lefts, keep)
    theirs = half(early, shards, others)
    late = ((2, 0), (2, 2))
    done = last(late, (a_two, b_two), mine, theirs, lefts, others, keep, left_sizes, right_sizes)

    by_plane = lax.all_to_all(done, "mpo", 0, 0)
    chips = SIDE * SIDE
    by_plane = by_plane.reshape(chips, 2, rows, right_dim)
    groups = [
        [place(2 * i + (g // SIDE + c) % 2, g % SIDE, c) for g in range(ranks) for i in range(2)]
        for c in range(2)
    ]
    out = order(lax.all_to_all(by_plane, "blk", 0, 0, axis_index_groups=groups))
    return out.reshape(sectors, rows, right_dim)


def solution(mesh):
    placed = (P("blk", None), P("mpo", "blk", None), P("mpo", "blk", None), P(), P())
    return jax.shard_map(
        local, mesh=mesh, in_specs=placed, out_specs=P(None, "mpo", "blk"), check_vma=False
    )
```
